128 devices in a mesh: region: 4 (over z), member: 32 (over x, y, core).
Axes of the slice: x: 4, y: 4, z: 4, core: 2. Of those that a mesh axis runs over, the one named last changes fastest.
Arguments:
- source: float32 [128, 1024, 128], P('region', 'member'), may hold values from -6 to 6
- inverse_density: float32 [3, 128, 1024, 128], P(None, 'region', 'member'), may hold values from 0.1 to 10
- block_level: int32 [512], P(('region', 'member')), may hold values from 0 to 2, as said below
- level_sweeps: int32 [3], replicated, may hold values from 1 to 6, as said below
- new_owner: int32 [512], replicated, may hold values from 0 to 127, as said below
Outputs:
- moved_pressure: float32 [768, 32768], P(('region', 'member'))
- moved_residual: float32 [768, 32768], P(('region', 'member'))
The draws below stay inside these ranges and needn't reach their ends.
Inputs may be any that keep to these rules, and one draw needn't show every extreme that they name: `block_level`: the blocks of one run of 64 consecutive blocks all have level 2. `level_sweeps`: Nondecreasing; level 0 takes one sweep and level 2 takes 6. `new_owner`: nondecreasing in b; block b goes to device b // 4 - 1, b // 4 or b // 4 + 1; block 3 goes to device 1; every device receives at most 6 blocks and some device exactly 6.
All inputs are finite; a program needn't handle non-finite values.
Results may differ from the reference program's by a relative error of at most 0.00018.
Values sent between devices are 32-bit elements; how exact they have to be, the bound alone decides.
No kernel may reach another device: no remote copies, remote signals or barrier semaphores. Data moves between devices by JAX's collectives and lax.ppermute only.
A program may use at most 128 MiB of HBM per device.

```python
import math
import jax
import jax.numpy as jnp
from jax import lax

BS = 32
BLK = 4
LEVELS = 3
SWEEP_MAX = 6
CSWEEPS = 8
CYCLES = 2
CAP = 6
BLOCKS = 512
NX = 128
NY = 1024
NZ = 128
N_REGION = 4
N_MEMBER = 32


def draw_block_level(key, part):
    first_key, second_key = jax.random.split(jax.random.fold_in(key, 3))
    levels_base = jax.random.randint(first_key, (BLOCKS,), 0, LEVELS - 1)
    band_length = BLOCKS // 8
    band_start = jax.random.randint(second_key, (), 0, BLOCKS - band_length + 1)
    position = jnp.arange(BLOCKS)
    inside = (position >= band_start) & (position < band_start + band_length)
    return jnp.where(inside, LEVELS - 1, levels_base).astype(jnp.int32)


def draw_level_sweeps(key, part):
    middle = jax.random.randint(jax.random.fold_in(key, 5), (LEVELS - 2,), 2, SWEEP_MAX)
    middle = jnp.sort(middle)
    return jnp.concatenate([jnp.ones((1,), jnp.int32), middle.astype(jnp.int32), jnp.full((1,), SWEEP_MAX, jnp.int32)]).astype(jnp.int32)


def draw_new_owner(key, part):
    device_total = BLOCKS // BLK
    first_key, second_key = jax.random.split(jax.random.fold_in(key, 11))
    shifts = jax.random.randint(first_key, (device_total + 1,), -1, 2)
    chosen = jax.random.randint(second_key, (), 2, device_total - 1)
    boundary = jnp.arange(device_total + 1)
    shifts = jnp.where(boundary == 1, -1, shifts)
    shifts = jnp.where(boundary == chosen, -1, shifts)
    shifts = jnp.where(boundary == chosen + 1, 1, shifts)
    shifts = jnp.where((boundary == 0) | (boundary == device_total), 0, shifts)
    starts = boundary * BLK + shifts
    position = jnp.arange(BLOCKS)
    return jnp.sum((position[:, None] >= starts[None, 1:device_total]).astype(jnp.int32), axis=1).astype(jnp.int32)


def shard_levels(rng, shape, shards, smallest, top_value):
    level, own = 1.0, jax.random.fold_in(rng, 6)
    for dim, shards_of in shards:
        draws = jnp.exp(jax.random.uniform(jax.random.fold_in(own, dim), (shards_of,), jnp.float32, smallest / len(shards), top_value / len(shards)))
        level = level * jnp.repeat(draws, shape[dim] // shards_of).reshape([-1 if axis == dim else 1 for axis in range(len(shape))])
    return level


def normal_values(key, extent, width, reach, cuts=(), held_as=jnp.bfloat16):
    values = width * jax.random.normal(key, extent, jnp.float32)
    if cuts:
        values = values * shard_levels(key, extent, cuts, -0.22, 0.18)
    return jnp.clip(values, -reach, reach).astype(held_as)


def setup_inputs(seed: int = 0) -> dict:
    streams_of = jax.random.split(jax.random.key(seed), 6)
    return {
        "source": normal_values(streams_of[0], (NX, NY, NZ), 1.0, 6.0, ((0, 4), (1, 32)), jnp.float32),
        "inverse_density": jnp.clip(jnp.exp(math.log(10.0) - 4.6051702 * jax.random.uniform(streams_of[1], (3, NX, NY, NZ), jnp.float32) ** shard_levels(streams_of[1], (3, NX, NY, NZ), ((1, 4), (2, 32)), -0.2, 0.2)), 0.1, 10.0),
        "block_level": draw_block_level(jax.random.fold_in(streams_of[5], 71), 0),
        "level_sweeps": draw_level_sweeps(jax.random.fold_in(streams_of[5], 71), 0),
        "new_owner": draw_new_owner(jax.random.fold_in(streams_of[5], 71), 0),
    }


RELAX = 0.8


def shifted(field, direction):
    length = field.shape[direction]
    widths = [(1, 1) if axis_id == direction else (0, 0) for axis_id in range(field.ndim)]
    padded = jnp.pad(field, widths)
    return lax.slice_in_dim(padded, 2, length + 2, axis=direction), lax.slice_in_dim(padded, 0, length, axis=direction)


def neighbours(field, direction, period):
    forward, backward = shifted(field, direction)
    if period > 0:
        place = lax.broadcasted_iota(jnp.int32, field.shape, direction) % period
        forward = jnp.where(place == period - 1, 0.0, forward)
        backward = jnp.where(place == 0, 0.0, backward)
    return forward, backward


def combine(field, pairs, upward, downward):
    result = jnp.zeros_like(field)
    for direction in range(3):
        forward, backward = pairs[direction]
        result = result + upward[direction] * (field - forward) + downward[direction] * (field - backward)
    return result


def operate(field, upward, downward, periods):
    pairs = [neighbours(field, direction, periods[direction]) for direction in range(3)]
    return combine(field, pairs, upward, downward)


def face_weights(inverse_density):
    upward, downward = [], []
    for direction in range(3):
        component = inverse_density[direction]
        forward, backward = shifted(component, direction)
        upward.append(0.5 * (component + forward))
        downward.append(0.5 * (component + backward))
    return jnp.stack(upward), jnp.stack(downward)


def centre_of(upward, downward):
    return upward[0] + upward[1] + upward[2] + downward[0] + downward[1] + downward[2]


def coarse_weights(upward, downward):
    size_x, size_y, size_z = upward.shape[1] // 4, upward.shape[2] // 4, upward.shape[3] // 4
    coarse_up, coarse_down = [], []
    for direction in range(3):
        upper_face = upward[direction].reshape(size_x, 4, size_y, 4, size_z, 4)
        lower_face = downward[direction].reshape(size_x, 4, size_y, 4, size_z, 4)
        upper_face = lax.slice_in_dim(upper_face, 3, 4, axis=2 * direction + 1)
        lower_face = lax.slice_in_dim(lower_face, 0, 1, axis=2 * direction + 1)
        coarse_up.append(jnp.sum(upper_face, axis=(1, 3, 5)) / 64.0)
        coarse_down.append(jnp.sum(lower_face, axis=(1, 3, 5)) / 64.0)
    return jnp.stack(coarse_up), jnp.stack(coarse_down)


def restrict(field):
    size_x, size_y, size_z = field.shape[0] // 4, field.shape[1] // 4, field.shape[2] // 4
    return jnp.sum(field.reshape(size_x, 4, size_y, 4, size_z, 4), axis=(1, 3, 5)) / 64.0


def prolong(field):
    size_x, size_y, size_z = field.shape
    spread_out = jnp.broadcast_to(field[:, None, :, None, :, None], (size_x, 4, size_y, 4, size_z, 4))
    return spread_out.reshape(4 * size_x, 4 * size_y, 4 * size_z)


def smooth(residual, upward, downward, centre, counts, most_sweeps, block_edge):
    periods = (block_edge, block_edge, block_edge)

    def sweep(sweep_number, correction):
        updated = correction + RELAX * (residual - operate(correction, upward, downward, periods)) / centre
        return jnp.where(sweep_number < counts, updated, correction)

    return lax.fori_loop(0, most_sweeps, sweep, jnp.zeros_like(residual))


def relocate(field, new_owner):
    blocks = field.reshape(N_REGION, BS, N_MEMBER, BS, BLK, BS).transpose(0, 2, 4, 1, 3, 5).reshape(BLOCKS, BS * BS * BS)
    owners = jnp.arange(N_REGION * N_MEMBER, dtype=jnp.int32)
    starts = jnp.sum((new_owner[None, :] < owners[:, None]).astype(jnp.int32), axis=1)
    holding = jnp.sum((new_owner[None, :] == owners[:, None]).astype(jnp.int32), axis=1)
    slot_index = jnp.arange(CAP, dtype=jnp.int32)
    source_row = jnp.clip(starts[:, None] + slot_index[None, :], 0, BLOCKS - 1).astype(jnp.int32)
    is_valid = (slot_index[None, :] < holding[:, None]).reshape(-1, 1)
    picked = jnp.take(blocks, source_row.reshape(-1), axis=0)
    return jnp.where(is_valid, picked, 0.0)


def reference(source, inverse_density, block_level, level_sweeps, new_owner):
    upward, downward = face_weights(inverse_density)
    centre = centre_of(upward, downward)
    coarse_up, coarse_down = coarse_weights(upward, downward)
    coarse_centre = centre_of(coarse_up, coarse_down)
    sweeps = level_sweeps[block_level].reshape(N_REGION, N_MEMBER, BLK)
    counts = jnp.broadcast_to(sweeps[:, None, :, None, :, None], (N_REGION, BS, N_MEMBER, BS, BLK, BS)).reshape(NX, NY, NZ)

    def apply_fine(field):
        return operate(field, upward, downward, (0, 0, 0))

    def solve_coarse(coarse_rhs):
        correction = jnp.zeros_like(coarse_rhs)
        for sweep_number in range(CSWEEPS):
            correction = correction + RELAX * (coarse_rhs - operate(correction, coarse_up, coarse_down, (BS // 4, 0, 0))) / coarse_centre
        return correction

    pressure = jnp.zeros_like(source)
    for cycle_number in range(CYCLES):
        residual = source - apply_fine(pressure)
        pressure = pressure + smooth(residual, upward, downward, centre, counts, SWEEP_MAX, BS)
        residual = source - apply_fine(pressure)
        pressure = pressure + prolong(solve_coarse(restrict(residual)))
        residual = source - apply_fine(pressure)
        pressure = pressure + smooth(residual, upward, downward, centre, counts, SWEEP_MAX, BS)
    residual = source - apply_fine(pressure)
    return relocate(pressure, new_owner), relocate(residual, new_owner)
```

```python
import functools

import jax
import jax.numpy as jnp
from jax import lax
from jax.experimental import pallas as pl
from jax.experimental.pallas import tpu as pltpu
from jax.sharding import PartitionSpec as P


BS = 32
BLK = 4
CSWEEPS = 8
CYCLES = 2
CAP = 6
RELAX = 0.8
KEEP = 0.2
LANES = 128
ROWS = BS * BS
XC = BS // 4
CROWS = XC * XC
UNROLL = 2
F32 = jnp.float32

MEVEN, REVEN, MLO, MHI, RLO, RHI, SWEEPS, START, COUNT, FIRST = range(10)


def call(body, out_rows, args, scalars, scratch=(), flops=2e6, mib=48):
    outs = [jax.ShapeDtypeStruct(s, F32) for s in out_rows]
    moved = sum(a.size * 4 for a in args) + sum(o.size * 4 for o in outs)
    return pl.pallas_call(
        body,
        out_shape=outs,
        in_specs=[pl.BlockSpec(memory_space=pltpu.SMEM)]
        + [pl.BlockSpec(memory_space=pltpu.VMEM)] * len(args),
        out_specs=[pl.BlockSpec(memory_space=pltpu.VMEM)] * len(outs),
        scratch_shapes=list(scratch),
        compiler_params=pltpu.CompilerParams(vmem_limit_bytes=mib << 20),
        cost_estimate=pl.CostEstimate(flops=int(flops), bytes_accessed=int(moved), transcendentals=0),
    )(scalars, *args)


def lane_ids(rows):
    return lax.broadcasted_iota(jnp.int32, (rows, LANES), 1)


def row_ids(rows):
    return lax.broadcasted_iota(jnp.int32, (rows, LANES), 0)


def next_y(v):
    return jnp.concatenate([v[8:32], pltpu.roll(v[0:8], 7, 0)], axis=0)


def prev_y(v):
    return jnp.concatenate([pltpu.roll(v[24:32], 1, 0), v[0:24]], axis=0)


def next_z(v):
    return pltpu.roll(v, LANES - 1, 1)


def prev_z(v):
    return pltpu.roll(v, 1, 1)


def fold(v):
    return v[0:8] + v[8:16] + v[16:24] + v[24:32]


def tiled(v):
    return jnp.concatenate([v, v, v, v], axis=0)


def plane(x):
    return pl.ds(pl.multiple_of(x * BS, BS), BS)


def pick(flag, yes, no):
    return jnp.where(jnp.full(yes.shape, flag, jnp.int32) == 1, yes, no)


def low_high(even, ok_low, ok_high, first, second):
    low = pick(even, second, first) * ok_low.astype(F32)
    high = pick(even, first, second) * ok_high.astype(F32)
    return low, high


def group_matrix():
    return jnp.where(
        row_ids(LANES) // 4 == lane_ids(LANES) // 4, jnp.float32(1.0), jnp.float32(0.0)
    )


def group_sum(v, ones):
    return lax.dot_general(
        v, ones, (((1,), (0,)), ((), ())), precision=lax.Precision.HIGHEST, preferred_element_type=F32
    )


def by_fours(ref, base):
    total = ref[pl.ds(base, 8, stride=4), :]
    for j in range(1, 4):
        total = total + ref[pl.ds(base + j, 8, stride=4), :]
    return total


def weights_kernel(prm, src, inv, src_t, f0, fy, fz, fzs, c0, fx, fyf, czu, czd):
    row, lane = row_ids(BS), lane_ids(BS)

    def load(ref, x, offset):
        return jnp.concatenate(
            [ref[pl.ds(offset + x * BS + k, 8, stride=4), :] for k in range(4)], axis=0
        )

    def body(xc, carry):
        before, here = carry
        total_up = jnp.zeros((8, LANES), F32)
        total_down = jnp.zeros((8, LANES), F32)
        for j in range(4):
            x = xc * 4 + j
            src_t[plane(x), :] = load(src, x, 0)
            inside = (x < BS - 1).astype(F32)
            after = load(inv, jnp.minimum(x + 1, BS - 1), 0) * inside
            one = load(inv, x, ROWS)
            two = load(inv, x, 2 * ROWS)
            one_n = jnp.where(row == BS - 1, 0.0, next_y(one))
            one_p = jnp.where(row == 0, 0.0, prev_y(one))
            two_n = jnp.where(lane == LANES - 1, 0.0, next_z(two))
            two_p = jnp.where(lane == 0, 0.0, prev_z(two))
            up0 = 0.5 * (here + after)
            upy = 0.5 * (one + one_n)
            upz = 0.5 * (two + two_n)
            downz = 0.5 * (two + two_p)
            f0[plane(x), :] = up0 * inside
            fy[plane(x), :] = jnp.where(row == BS - 1, 0.0, upy)
            masked = jnp.where(lane == LANES - 1, 0.0, upz)
            fz[plane(x), :] = masked
            fzs[plane(x), :] = jnp.where(lane % BS == BS - 1, 0.0, upz)
            c0[plane(x), :] = up0 + upy + upz + 0.5 * (here + before) + 0.5 * (one + one_p) + downz
            total_up = total_up + fold(upz)
            total_down = total_down + fold(downz)
            before, here = here, after
        at = pl.ds(pl.multiple_of(xc * 8, 8), 8)
        czu[at, :] = total_up
        czd[at, :] = total_down
        return before, here

    lax.fori_loop(0, XC, body, (jnp.zeros((BS, LANES), F32), load(inv, 0, 0)))
    fx[0:BS, :] = load(inv, 0, 0)
    fx[BS : 2 * BS, :] = load(inv, BS - 1, 0)
    for g in range(4):
        fyf[8 * g : 8 * g + 8, :] = inv[pl.ds(ROWS + 256 * g, 8, stride=BS), :]
        fyf[BS + 8 * g : BS + 8 * g + 8, :] = inv[pl.ds(ROWS + 256 * g + 31, 8, stride=BS), :]


def add_faces_y(ref, low, high):
    for g in range(4):
        at = pl.ds(256 * g, 8, stride=BS)
        ref[at, :] = ref[at, :] + low[8 * g : 8 * g + 8]
        at = pl.ds(256 * g + 31, 8, stride=BS)
        ref[at, :] = ref[at, :] + high[8 * g : 8 * g + 8]


def add_faces_x(ref, low, high):
    ref[0:BS, :] = ref[0:BS, :] + low
    ref[ROWS - BS : ROWS, :] = ref[ROWS - BS : ROWS, :] + high


def send_faces(prm, p, sa, sb, sc, sd):
    for g in range(4):
        low = p[pl.ds(256 * g, 8, stride=BS), :]
        high = p[pl.ds(256 * g + 31, 8, stride=BS), :]
        sa[8 * g : 8 * g + 8, :] = pick(prm[MEVEN], high, low)
        sb[8 * g : 8 * g + 8, :] = pick(prm[MEVEN], low, high)
    low = p[0:BS, :]
    high = p[ROWS - BS : ROWS, :]
    sc[...] = pick(prm[REVEN], high, low)
    sd[...] = pick(prm[REVEN], low, high)


def relax(prm, counts, r, e, f0, fy, fzs, d):
    limit = counts[...]

    def sweep(i, _):
        active = jnp.broadcast_to(limit, (BS, LANES)) > i

        def body(x, carry):
            t0, here = carry
            at = plane(x)
            after = e[plane(jnp.minimum(x + 1, BS - 1)), :]
            w0, wy, wz = f0[at, :], fy[at, :], fzs[at, :]
            t1 = w0 * here
            total = r[at, :] + t0 + w0 * after
            total = total + wy * next_y(here) + prev_y(wy * here)
            total = total + wz * next_z(here) + prev_z(wz * here)
            e[at, :] = jnp.where(active, KEEP * here + d[at, :] * total, here)
            return t1, after

        lax.fori_loop(
            0, BS, body, (jnp.zeros((BS, LANES), F32), e[0:BS, :]), unroll=UNROLL
        )
        return 0

    lax.fori_loop(1, prm[SWEEPS], sweep, 0)


def first_kernel(
    prm, counts, src, f0, fy, fzs, c0, fx, fyf, ra, rb, rc, rd,
    c, d, gx, gy, p, sa, sb, sc, sd,
):
    def natural(ref):
        return jnp.concatenate([ref[pl.ds(k, 8, stride=4), :] for k in range(4)], axis=0)

    xlo, xhi = low_high(prm[REVEN], prm[RLO], prm[RHI], natural(rc), natural(rd))
    ylo, yhi = low_high(prm[MEVEN], prm[MLO], prm[MHI], ra[...], rb[...])
    gx[0:BS, :] = 0.5 * (fx[0:BS, :] + xlo)
    gx[BS : 2 * BS, :] = 0.5 * (fx[BS : 2 * BS, :] + xhi)
    gy[0:BS, :] = 0.5 * (fyf[0:BS, :] + ylo)
    gy[BS : 2 * BS, :] = 0.5 * (fyf[BS : 2 * BS, :] + yhi)

    def copy(x, _):
        c[plane(x), :] = c0[plane(x), :]
        return 0

    lax.fori_loop(0, BS, copy, 0)
    add_faces_x(c, 0.5 * xlo, 0.5 * xhi)
    add_faces_y(c, 0.5 * ylo, 0.5 * yhi)

    def begin(x, _):
        at = plane(x)
        scale = RELAX / c[at, :]
        d[at, :] = scale
        p[at, :] = scale * src[at, :]
        return 0

    lax.fori_loop(0, BS, begin, 0)
    relax(prm, counts, src, p, f0, fy, fzs, d)
    send_faces(prm, p, sa, sb, sc, sd)


def residual_plane(src, c, f0, fy, fz, at, t0, here, after):
    w0, wy, wz = f0[at, :], fy[at, :], fz[at, :]
    total = src[at, :] - c[at, :] * here + t0 + w0 * after
    total = total + wy * next_y(here) + prev_y(wy * here)
    total = total + wz * next_z(here) + prev_z(wz * here)
    return total, w0 * here


def coarse_rhs_kernel(prm, src, c, f0, fy, fz, p, q, scr):
    def body(xc, carry):
        t0, here = carry
        total = jnp.zeros((8, LANES), F32)
        for j in range(4):
            x = xc * 4 + j
            after = p[plane(jnp.minimum(x + 1, BS - 1)), :]
            r, t0 = residual_plane(src, c, f0, fy, fz, plane(x), t0, here, after)
            total = total + fold(r)
            here = after
        scr[pl.ds(pl.multiple_of(xc * 8, 8), 8), :] = total
        return t0, here

    lax.fori_loop(0, XC, body, (jnp.zeros((BS, LANES), F32), p[0:BS, :]))
    q[...] = group_sum(scr[...], group_matrix()) * (1.0 / 64.0)


def coarse_weights_kernel(prm, f0, fy, gx, gy, czu, czd, packed, scr, cy):
    ones = group_matrix()
    part = 1.0 / 64.0
    lane = lane_ids(CROWS)
    row = row_ids(CROWS)
    for xc in range(XC):
        scr[8 * xc : 8 * xc + 8, :] = fold(f0[(4 * xc + 3) * BS : (4 * xc + 4) * BS, :])
        total = fy[4 * xc * BS + 24 : 4 * xc * BS + 32, :]
        for j in range(1, 4):
            at = (4 * xc + j) * BS
            total = total + fy[at + 24 : at + 32, :]
        cy[8 * xc : 8 * xc + 8, :] = total
    c0 = group_sum(scr[...], ones) * part
    cy[pl.ds(7, 8, stride=8), :] = by_fours(gy, BS)
    scr[...] = group_sum(cy[...], ones) * part
    up_y = scr[...]
    gxlo = group_sum(fold(gx[0:BS, :]), ones) * part
    gxhi = group_sum(fold(gx[BS : 2 * BS, :]), ones) * part
    up_z = group_sum(jnp.where(lane % 4 == 3, czu[...], 0.0), ones) * part
    down_z = group_sum(jnp.where(lane % 4 == 0, czd[...], 0.0), ones) * part
    up_0 = jnp.concatenate([c0[0 : CROWS - 8], gxhi], axis=0)
    down_0 = jnp.concatenate([gxlo, c0[0 : CROWS - 8]], axis=0)
    shifted = jnp.concatenate(
        [pltpu.roll(up_y[8 * xc : 8 * xc + 8], 1, 0) for xc in range(XC)], axis=0
    )
    cy[...] = shifted
    cy[pl.ds(0, 8, stride=8), :] = group_sum(by_fours(gy, 0), ones) * part
    scale = RELAX / (up_0 + up_y + up_z + down_0 + cy[...] + down_z)
    couple_y = jnp.where(row % 8 == 7, up_y * prm[MHI].astype(F32), up_y)
    couple_z = jnp.where(lane >= LANES - 4, 0.0, up_z)
    place = lane % 4
    packed[...] = jnp.where(
        place == 0, c0, jnp.where(place == 1, couple_y, jnp.where(place == 2, couple_z, scale))
    )


def coarse_faces_kernel(prm, qi, gx, gy, ra, rb, rc, rd, q, scr):
    ones = group_matrix()
    part = 1.0 / 64.0
    xlo, xhi = low_high(prm[REVEN], prm[RLO], prm[RHI], rc[...], rd[...])
    ylo, yhi = low_high(prm[MEVEN], prm[MLO], prm[MHI], ra[...], rb[...])
    scr[0:BS, :] = gy[0:BS, :] * ylo
    scr[BS : 2 * BS, :] = gy[BS : 2 * BS, :] * yhi
    faces = jnp.concatenate(
        [
            fold(gx[0:BS, :] * xlo),
            fold(gx[BS : 2 * BS, :] * xhi),
            by_fours(scr, 0),
            by_fours(scr, BS),
        ],
        axis=0,
    )
    faces = group_sum(faces, ones) * part
    q[...] = qi[...]
    q[0:8, :] = q[0:8, :] + faces[0:8]
    q[CROWS - 8 : CROWS, :] = q[CROWS - 8 : CROWS, :] + faces[8:16]
    q[pl.ds(0, 8, stride=8), :] = q[pl.ds(0, 8, stride=8), :] + faces[16:24]
    q[pl.ds(7, 8, stride=8), :] = q[pl.ds(7, 8, stride=8), :] + faces[24:32]


def coarse_solve_kernel(prm, q, qa, qb, w, wa, wb, c, cyf, sc, sd, scr):
    ones = group_matrix()
    even = prm[MEVEN]

    def joined(own, first, second):
        low, high = pick(even, second, first), pick(even, first, second)
        parts = []
        for xc in range(XC):
            at = slice(8 * xc, 8 * xc + 8)
            parts += [low[at], own[at], high[at]]
        return jnp.concatenate(parts, axis=0)

    packed = joined(w[...], wa[...], wb[...])
    rhs = joined(q[...], qa[...], qb[...])
    place = lane_ids(3 * CROWS) % 4
    weights = [group_sum(jnp.where(place == j, packed, 0.0), ones) for j in range(4)]
    w0, wy, wz, scale = weights

    def up_x(v):
        return jnp.concatenate([v[24:], v[:24]], axis=0)

    def down_x(v):
        return jnp.concatenate([v[-24:], v[:-24]], axis=0)

    def by_plane(v, shift):
        return jnp.concatenate(
            [pltpu.roll(v[24 * xc : 24 * xc + 24], shift, 0) for xc in range(XC)], axis=0
        )

    field = scale * rhs
    for _ in range(CSWEEPS - 1):
        total = rhs + w0 * up_x(field) + down_x(w0 * field)
        total = total + wy * by_plane(field, 23) + by_plane(wy * field, 1)
        total = total + wz * pltpu.roll(field, LANES - 4, 1) + pltpu.roll(wz * field, 4, 1)
        field = KEEP * field + scale * total
    scr[...] = field
    for xc in range(XC):
        c[8 * xc : 8 * xc + 8, :] = field[24 * xc + 8 : 24 * xc + 16]
    cyf[0:8, :] = scr[pl.ds(7, 8, stride=24), :]
    cyf[8:16, :] = scr[pl.ds(16, 8, stride=24), :]
    low, high = field[8:16], field[24 * 7 + 8 : 24 * 7 + 16]
    sc[...] = pick(prm[REVEN], high, low)
    sd[...] = pick(prm[REVEN], low, high)


def correct_kernel(prm, src, c, f0, fy, fz, p, gy, ra, rb, cc, cyf, p2, r, scr):
    def body(xc, carry):
        t0, here = carry
        add = tiled(cc[pl.ds(pl.multiple_of(xc * 8, 8), 8), :])
        later = pl.ds(pl.multiple_of(jnp.minimum(xc + 1, XC - 1) * 8, 8), 8)
        add_next = tiled(cc[later, :])
        for j in range(4):
            x = xc * 4 + j
            at = plane(x)
            after = p[plane(jnp.minimum(x + 1, BS - 1)), :] + (add if j < 3 else add_next)
            p2[at, :] = here
            r[at, :], t0 = residual_plane(src, c, f0, fy, fz, at, t0, here, after)
            here = after
        return t0, here

    lax.fori_loop(0, XC, body, (jnp.zeros((BS, LANES), F32), p[0:BS, :] + tiled(cc[0:8, :])))
    ylo, yhi = pick(prm[MEVEN], rb[...], ra[...]), pick(prm[MEVEN], ra[...], rb[...])
    for j in range(4):
        scr[pl.ds(j, 8, stride=4), :] = cyf[0:8, :]
        scr[pl.ds(BS + j, 8, stride=4), :] = cyf[8:16, :]
    ylo = (ylo + scr[0:BS, :]) * prm[MLO].astype(F32)
    yhi = (yhi + scr[BS : 2 * BS, :]) * prm[MHI].astype(F32)
    add_faces_y(r, gy[0:BS, :] * ylo, gy[BS : 2 * BS, :] * yhi)


def residual_kernel(prm, src, c, f0, fy, fz, p, r):
    def body(x, carry):
        t0, here = carry
        at = plane(x)
        after = p[plane(jnp.minimum(x + 1, BS - 1)), :]
        r[at, :], t1 = residual_plane(src, c, f0, fy, fz, at, t0, here, after)
        return t1, after

    lax.fori_loop(0, BS, body, (jnp.zeros((BS, LANES), F32), p[0:BS, :]), unroll=UNROLL)


def finish_smooth(prm, counts, ri, f0, fy, fzs, d, p, p_out, sa, sb, sc, sd, rs, e, add):
    def copy(x, _):
        rs[plane(x), :] = ri[plane(x), :]
        return 0

    lax.fori_loop(0, BS, copy, 0)
    add(rs)

    def begin(x, _):
        e[plane(x), :] = d[plane(x), :] * rs[plane(x), :]
        return 0

    lax.fori_loop(0, BS, begin, 0)
    relax(prm, counts, rs, e, f0, fy, fzs, d)

    def end(x, _):
        p_out[plane(x), :] = p[plane(x), :] + e[plane(x), :]
        return 0

    lax.fori_loop(0, BS, end, 0)
    send_faces(prm, p_out, sa, sb, sc, sd)


def smooth_x_kernel(
    prm, counts, ri, f0, fy, fzs, d, p, gx, rc, rd, kc, kd, p_out, sa, sb, sc, sd, rs, e
):
    def add(ref):
        first = rc[...] + tiled(kc[...])
        second = rd[...] + tiled(kd[...])
        xlo, xhi = low_high(prm[REVEN], prm[RLO], prm[RHI], first, second)
        add_faces_x(ref, gx[0:BS, :] * xlo, gx[BS : 2 * BS, :] * xhi)

    finish_smooth(prm, counts, ri, f0, fy, fzs, d, p, p_out, sa, sb, sc, sd, rs, e, add)


def add_all(prm, gx, gy, ra, rb, rc, rd, ref):
    xlo, xhi = low_high(prm[REVEN], prm[RLO], prm[RHI], rc[...], rd[...])
    add_faces_x(ref, gx[0:BS, :] * xlo, gx[BS : 2 * BS, :] * xhi)
    ylo, yhi = low_high(prm[MEVEN], prm[MLO], prm[MHI], ra[...], rb[...])
    add_faces_y(ref, gy[0:BS, :] * ylo, gy[BS : 2 * BS, :] * yhi)


def smooth_kernel(
    prm, counts, ri, f0, fy, fzs, d, p, gx, gy, ra, rb, rc, rd, p_out, sa, sb, sc, sd, rs, e
):
    add = functools.partial(add_all, prm, gx, gy, ra, rb, rc, rd)
    finish_smooth(prm, counts, ri, f0, fy, fzs, d, p, p_out, sa, sb, sc, sd, rs, e, add)


def to_blocks(ref, out):
    lane = lane_ids(8)
    half = lane < 64
    even = (lane // BS) % 2 == 0

    def body(x, _):
        v = ref[plane(x), :]
        v = [v[8 * k : 8 * k + 8] for k in range(4)]
        u = [None] * 4
        for k in range(2):
            low, high = v[k], v[k + 2]
            u[k] = jnp.where(half, low, pltpu.roll(high, 64, 1))
            u[k + 2] = jnp.where(half, pltpu.roll(low, 64, 1), high)
        for b in (0, 2):
            low, high = u[b], u[b + 1]
            first = jnp.where(even, low, pltpu.roll(high, BS, 1))
            second = jnp.where(even, pltpu.roll(low, LANES - BS, 1), high)
            out[pl.ds(pl.multiple_of(b * 256 + x * 8, 8), 8), :] = first
            out[pl.ds(pl.multiple_of((b + 1) * 256 + x * 8, 8), 8), :] = second
        return 0

    lax.fori_loop(0, BS, body, 0, unroll=UNROLL)


def send_blocks(prm, blocks, sa, sb, count):
    size = count * 256
    last = (BLK - count) * 256

    def body(t, _):
        at = pl.ds(pl.multiple_of(t * 32, 32), 32)
        low = blocks[at, :]
        high = blocks[pl.ds(pl.multiple_of(last + t * 32, 32), 32), :]
        sa[at, :] = pick(prm[MEVEN], high, low)
        sb[at, :] = pick(prm[MEVEN], low, high)
        return 0

    lax.fori_loop(0, size // 32, body, 0)


def pressure_blocks_kernel(prm, p, blocks, sa, sb, *, count):
    to_blocks(p, blocks)
    send_blocks(prm, blocks, sa, sb, count)


def final_kernel(prm, ri, gx, gy, ra, rb, rc, rd, blocks, sa, sb, rs, *, count):
    def copy(x, _):
        rs[plane(x), :] = ri[plane(x), :]
        return 0

    lax.fori_loop(0, BS, copy, 0)
    add_all(prm, gx, gy, ra, rb, rc, rd, rs)
    to_blocks(rs, blocks)
    send_blocks(prm, blocks, sa, sb, count)


def place_kernel(prm, own, ra, rb, out, *, count):
    even = prm[MEVEN]

    def fill(ref, base, j):
        def body(t, _):
            out[pl.ds(t * 8, 8), j, :] = ref[pl.ds(pl.multiple_of(base + t * 8, 8), 8), :]
            return 0

        lax.fori_loop(0, 32, body, 0, unroll=4)

    for j in range(CAP):
        where = prm[START] + j - prm[FIRST]
        used = j < prm[COUNT]
        mine = used & (where >= 0) & (where < BLK)
        low = used & (where < 0)
        high = used & (where >= BLK)
        low_base = jnp.clip(where + count, 0, count - 1) * 256
        high_base = jnp.clip(where - BLK, 0, count - 1) * 256

        @pl.when(mine)
        def _():
            fill(own, jnp.clip(where, 0, BLK - 1) * 256, j)

        @pl.when((low & (even == 0)) | (high & (even == 1)))
        def _():
            fill(ra, jnp.where(low, low_base, high_base), j)

        @pl.when((low & (even == 1)) | (high & (even == 0)))
        def _():
            fill(rb, jnp.where(low, low_base, high_base), j)

        @pl.when(jnp.logical_not(used))
        def _():
            def body(t, _):
                out[pl.ds(t * 8, 8), j, :] = jnp.zeros((8, LANES), F32)
                return 0

            lax.fori_loop(0, 32, body, 0, unroll=4)


def swap_pairs(count):
    inner = [(i, i ^ 1) for i in range(count)]
    outer = [(i, (i + 1) % count if i % 2 else (i - 1) % count) for i in range(count)]
    return inner, outer


def swap(first, second, axis):
    inner, outer = swap_pairs(lax.axis_size(axis))
    return lax.ppermute(first, axis, inner), lax.ppermute(second, axis, outer)


def swap_faces(sa, sb, sc, sd):
    return (*swap(sa, sb, "member"), *swap(sc, sd, "region"))


def on_device(source, inverse_density, block_level, level_sweeps, new_owner):
    regions, members = lax.axis_size("region"), lax.axis_size("member")
    region, member = lax.axis_index("region"), lax.axis_index("member")
    device = region * members + member
    level_ids = jnp.arange(level_sweeps.shape[0], dtype=jnp.int32)
    sweeps = jnp.sum(
        jnp.where(block_level[:, None] == level_ids[None, :], level_sweeps[None, :], 0), axis=1
    )
    counts = jnp.repeat(sweeps, BS)[None, :]
    start = jnp.sum((new_owner < device).astype(jnp.int32))
    held = jnp.sum((new_owner == device).astype(jnp.int32))
    prm = jnp.stack(
        [
            1 - member % 2,
            1 - region % 2,
            (member > 0).astype(jnp.int32),
            (member < members - 1).astype(jnp.int32),
            (region > 0).astype(jnp.int32),
            (region < regions - 1).astype(jnp.int32),
            jnp.max(sweeps),
            start,
            held,
            device * BLK,
        ]
    ).astype(jnp.int32)

    src = source.reshape(ROWS, LANES)
    inv = inverse_density.reshape(3 * ROWS, LANES)
    edge = jnp.where(member % 2 == 0, BS - 1, 0)
    ia = lax.dynamic_slice_in_dim(inverse_density[1], edge, 1, axis=1)[:, 0]
    ib = lax.dynamic_slice_in_dim(inverse_density[1], BS - 1 - edge, 1, axis=1)[:, 0]
    edge = jnp.where(region % 2 == 0, BS - 1, 0)
    ic = lax.dynamic_slice_in_dim(inverse_density[0], edge, 1, axis=0)[0]
    id_ = lax.dynamic_slice_in_dim(inverse_density[0], BS - 1 - edge, 1, axis=0)[0]
    halos = swap_faces(ia, ib, ic, id_)

    full, two, cfield = (ROWS, LANES), (2 * BS, LANES), (CROWS, LANES)
    face, cface = (BS, LANES), (8, LANES)
    src, f0, fy, fz, fzs, c0, fx, fyf, czu, czd = call(
        weights_kernel, [full] * 6 + [two] * 2 + [cfield] * 2, [src, inv], prm
    )
    c, d, gx, gy, p, *sends = call(
        first_kernel,
        [full, full, two, two, full] + [face] * 4,
        [counts, src, f0, fy, fzs, c0, fx, fyf, *halos],
        prm,
    )
    fine = [src, c, f0, fy, fz]
    full_scratch = [pltpu.VMEM(full, F32)]
    packed = None
    for cycle in range(CYCLES):
        ra, rb, rc, rd = swap_faces(*sends)
        if cycle > 0:
            (ri,) = call(residual_kernel, [full], [*fine, p], prm)
            p, *sends = call(
                smooth_kernel,
                [full] + [face] * 4,
                [counts, ri, f0, fy, fzs, d, p, gx, gy, ra, rb, rc, rd],
                prm,
                full_scratch * 2,
            )
            ra, rb, rc, rd = swap_faces(*sends)
        (qi,) = call(coarse_rhs_kernel, [cfield], [*fine, p], prm, [pltpu.VMEM(cfield, F32)])
        if packed is None:
            (packed,) = call(
                coarse_weights_kernel,
                [cfield],
                [f0, fy, gx, gy, czu, czd],
                prm,
                [pltpu.VMEM(cfield, F32)] * 2,
            )
            wa, wb = swap(packed, packed, "member")
        (q,) = call(
            coarse_faces_kernel,
            [cfield],
            [qi, gx, gy, ra, rb, rc, rd],
            prm,
            [pltpu.VMEM(two, F32)],
        )
        qa, qb = swap(q, q, "member")
        cc, cyf, sc, sd = call(
            coarse_solve_kernel,
            [cfield, (16, LANES), cface, cface],
            [q, qa, qb, packed, wa, wb],
            prm,
            [pltpu.VMEM((3 * CROWS, LANES), F32)],
        )
        kc, kd = swap(sc, sd, "region")
        p, ri = call(
            correct_kernel,
            [full, full],
            [*fine, p, gy, ra, rb, cc, cyf],
            prm,
            [pltpu.VMEM(two, F32)],
        )
        p, *sends = call(
            smooth_x_kernel,
            [full] + [face] * 4,
            [counts, ri, f0, fy, fzs, d, p, gx, rc, rd, kc, kd],
            prm,
            full_scratch * 2,
        )

    def tail(count, p, sends, fine, gx, gy, prm):
        halos = swap_faces(*sends)
        part = (count * 256, LANES)
        pairs = ("region", "member")
        (ri,) = call(residual_kernel, [full], [*fine, p], prm)
        blocks_p, sa, sb = call(
            functools.partial(pressure_blocks_kernel, count=count), [full, part, part], [p], prm
        )
        pa, pb = swap(sa, sb, pairs)
        blocks_r, sa, sb = call(
            functools.partial(final_kernel, count=count),
            [full, part, part],
            [ri, gx, gy, *halos],
            prm,
            full_scratch,
        )
        ra, rb = swap(sa, sb, pairs)
        place = functools.partial(place_kernel, count=count)
        slots = [(256, CAP, LANES)]
        (out_p,) = call(place, slots, [blocks_p, pa, pb], prm)
        (out_r,) = call(place, slots, [blocks_r, ra, rb], prm)
        return tuple(
            o.transpose(1, 0, 2).reshape(CAP, 256 * LANES) for o in (out_p, out_r)
        )

    block = jnp.arange(new_owner.shape[0], dtype=jnp.int32)
    home = block // BLK
    up = jnp.where(new_owner > home, BLK - block % BLK, 0)
    down = jnp.where(new_owner < home, block % BLK + 1, 0)
    most = jnp.max(jnp.maximum(up, down))
    operands = (p, sends, fine, gx, gy, prm)
    return lax.cond(
        most <= 1,
        lambda *a: tail(1, *a),
        lambda *a: tail(BLK, *a),
        *operands,
    )


def solution(mesh):
    placed = (
        P("region", "member", None),
        P(None, "region", "member", None),
        P(("region", "member")),
        P(),
        P(),
    )
    return jax.shard_map(
        on_device,
        mesh=mesh,
        in_specs=placed,
        out_specs=(P(("region", "member"), None), P(("region", "member"), None)),
        check_vma=False,
    )
```

```python
import functools

import jax
import jax.numpy as jnp
from jax import lax
from jax.experimental import pallas as pl
from jax.experimental.pallas import tpu as pltpu
from jax.sharding import PartitionSpec as P


BS = 32
BLK = 4
CSWEEPS = 8
CYCLES = 2
CAP = 6
SWEEP_MAX = 6
RELAX = 0.8
KEEP = 0.2
PART = 1.0 / 64.0
LANES = 128
ROWS = BS * BS
XC = BS // 4
CROWS = XC * XC
UNROLL = 2
ZERO = functools.partial(jnp.zeros, (BS, LANES), jnp.float32)
F32 = jnp.float32


def vmem(*shape):
    return pltpu.VMEM(shape, F32)


def call(body, out_rows, args, scalars=(), scratch=(), aliases=None, flops=2e6, mib=48):
    outs = [jax.ShapeDtypeStruct(s, F32) for s in out_rows]
    moved = sum(a.size * 4 for a in args) + sum(o.size * 4 for o in outs)
    return pl.pallas_call(
        body,
        out_shape=outs,
        in_specs=[pl.BlockSpec(memory_space=pltpu.SMEM)] * len(scalars)
        + [pl.BlockSpec(memory_space=pltpu.VMEM)] * len(args),
        out_specs=[pl.BlockSpec(memory_space=pltpu.VMEM)] * len(outs),
        scratch_shapes=list(scratch),
        input_output_aliases={len(scalars) + k: v for k, v in (aliases or {}).items()},
        compiler_params=pltpu.CompilerParams(vmem_limit_bytes=mib << 20),
        cost_estimate=pl.CostEstimate(flops=int(flops), bytes_accessed=int(moved), transcendentals=0),
    )(*scalars, *args)


class Place:
    def __init__(self):
        region, member = lax.axis_index("region"), lax.axis_index("member")
        self.device = region * lax.axis_size("member") + member
        self.even = (member % 2 == 0, region % 2 == 0)
        self.low = (member > 0, region > 0)
        self.high = (member < lax.axis_size("member") - 1, region < lax.axis_size("region") - 1)


def lane_ids(rows):
    return lax.broadcasted_iota(jnp.int32, (rows, LANES), 1)


def row_ids(rows):
    return lax.broadcasted_iota(jnp.int32, (rows, LANES), 0)


def next_y(v):
    return jnp.concatenate([v[8:32], pltpu.roll(v[0:8], 7, 0)], axis=0)


def prev_y(v):
    return jnp.concatenate([pltpu.roll(v[24:32], 1, 0), v[0:24]], axis=0)


def next_z(v):
    return pltpu.roll(v, LANES - 1, 1)


def prev_z(v):
    return pltpu.roll(v, 1, 1)


def fold(v):
    return v[0:8] + v[8:16] + v[16:24] + v[24:32]


def tiled(v):
    return jnp.concatenate([v, v, v, v], axis=0)


def plane(x):
    return pl.ds(pl.multiple_of(x * BS, BS), BS)


def pick(flag, yes, no):
    return jnp.where(jnp.full(yes.shape, flag.astype(jnp.int32), jnp.int32) == 1, yes, no)


def low_high(place, axis, first, second):
    low = pick(place.even[axis], second, first) * place.low[axis].astype(F32)
    high = pick(place.even[axis], first, second) * place.high[axis].astype(F32)
    return low, high


def group_matrix():
    return jnp.where(
        row_ids(LANES) // 4 == lane_ids(LANES) // 4, jnp.float32(1.0), jnp.float32(0.0)
    )


def group_sum(v, ones):
    return lax.dot_general(
        v, ones, (((1,), (0,)), ((), ())), precision=lax.Precision.HIGHEST, preferred_element_type=F32
    )


def by_fours(ref, base):
    total = ref[pl.ds(base, 8, stride=4), :]
    for j in range(1, 4):
        total = total + ref[pl.ds(base + j, 8, stride=4), :]
    return total


def weights_kernel(new_owner, src, inv, owned, src_t, f0, fy, fz, fzs, c0, fx, fyf, czu, czd):
    row, lane = row_ids(BS), lane_ids(BS)

    def load(ref, x, offset):
        return jnp.concatenate(
            [ref[pl.ds(offset + x * BS + k, 8, stride=4), :] for k in range(4)], axis=0
        )

    def body(xc, carry):
        before, here = carry
        total_up = jnp.zeros((8, LANES), F32)
        total_down = jnp.zeros((8, LANES), F32)
        for j in range(4):
            x = xc * 4 + j
            src_t[plane(x), :] = load(src, x, 0)
            inside = (x < BS - 1).astype(F32)
            after = load(inv, jnp.minimum(x + 1, BS - 1), 0) * inside
            one = load(inv, x, ROWS)
            two = load(inv, x, 2 * ROWS)
            one_n = jnp.where(row == BS - 1, 0.0, next_y(one))
            one_p = jnp.where(row == 0, 0.0, prev_y(one))
            two_n = jnp.where(lane == LANES - 1, 0.0, next_z(two))
            two_p = jnp.where(lane == 0, 0.0, prev_z(two))
            up0 = 0.5 * (here + after)
            upy = 0.5 * (one + one_n)
            upz = 0.5 * (two + two_n)
            downz = 0.5 * (two + two_p)
            f0[plane(x), :] = up0 * inside
            fy[plane(x), :] = jnp.where(row == BS - 1, 0.0, upy)
            fz[plane(x), :] = jnp.where(lane == LANES - 1, 0.0, upz)
            fzs[plane(x), :] = jnp.where(lane % BS == BS - 1, 0.0, upz)
            c0[plane(x), :] = up0 + upy + upz + 0.5 * (here + before) + 0.5 * (one + one_p) + downz
            total_up = total_up + fold(upz)
            total_down = total_down + fold(downz)
            before, here = here, after
        at = pl.ds(pl.multiple_of(xc * 8, 8), 8)
        czu[at, :] = total_up
        czd[at, :] = total_down
        return before, here

    lax.fori_loop(0, XC, body, (ZERO(), load(inv, 0, 0)))
    fx[0:BS, :] = load(inv, 0, 0)
    fx[BS : 2 * BS, :] = load(inv, BS - 1, 0)
    for g in range(4):
        fyf[8 * g : 8 * g + 8, :] = inv[pl.ds(ROWS + 256 * g, 8, stride=BS), :]
        fyf[BS + 8 * g : BS + 8 * g + 8, :] = inv[pl.ds(ROWS + 256 * g + 31, 8, stride=BS), :]
    device = Place().device
    owner = new_owner[...]
    block = lax.broadcasted_iota(jnp.int32, owner.shape, 0) * owner.shape[1]
    block = block + lax.broadcasted_iota(jnp.int32, owner.shape, 1)
    home, place = block // BLK, block % BLK
    leaving = jnp.where(owner > home, BLK - place, jnp.where(owner < home, place + 1, 0))
    owned[0] = jnp.sum((owner < device).astype(F32)).astype(jnp.int32)
    owned[1] = jnp.sum((owner == device).astype(F32)).astype(jnp.int32)
    owned[2] = jnp.max(leaving.astype(F32)).astype(jnp.int32)


def add_faces_y(ref, low, high):
    for g in range(4):
        at = pl.ds(256 * g, 8, stride=BS)
        ref[at, :] = ref[at, :] + low[8 * g : 8 * g + 8]
        at = pl.ds(256 * g + 31, 8, stride=BS)
        ref[at, :] = ref[at, :] + high[8 * g : 8 * g + 8]


def add_faces_x(ref, low, high):
    ref[0:BS, :] = ref[0:BS, :] + low
    ref[ROWS - BS : ROWS, :] = ref[ROWS - BS : ROWS, :] + high


def send_faces(place, p, sa, sb, sc, sd):
    even = place.even[0]
    for g in range(4):
        low = p[pl.ds(256 * g, 8, stride=BS), :]
        high = p[pl.ds(256 * g + 31, 8, stride=BS), :]
        sa[8 * g : 8 * g + 8, :] = pick(even, high, low)
        sb[8 * g : 8 * g + 8, :] = pick(even, low, high)
    low = p[0:BS, :]
    high = p[ROWS - BS : ROWS, :]
    sc[...] = pick(place.even[1], high, low)
    sd[...] = pick(place.even[1], low, high)


def sweep_limits(levels, level_sweeps):
    block = lane_ids(BS) // BS
    limit = jnp.zeros((BS, LANES), jnp.int32)
    for b in range(BLK):
        limit = jnp.where(block == b, level_sweeps[levels[b]], limit)
    return limit


def relax(limit, r, e, f0, fy, fzs, d, finish):
    def sweep(i, load, store):
        active = limit > i

        def body(x, carry):
            t0, here = carry
            at = plane(x)
            after = load(plane(jnp.minimum(x + 1, BS - 1)))
            w0, wy, wz = f0[at, :], fy[at, :], fzs[at, :]
            t1 = w0 * here
            total = r[at, :] + t0 + w0 * after
            total = total + wy * next_y(here) + prev_y(wy * here)
            total = total + wz * next_z(here) + prev_z(wz * here)
            store(at, jnp.where(active, KEEP * here + d[at, :] * total, here))
            return t1, after

        lax.fori_loop(0, BS, body, (ZERO(), load(plane(0))), unroll=UNROLL)

    def first(at):
        return d[at, :] * r[at, :]

    def held(at):
        return e[at, :]

    def keep(at, value):
        e[at, :] = value

    def middle(i, _):
        sweep(i, held, keep)
        return 0

    sweep(1, first, keep)
    lax.fori_loop(2, SWEEP_MAX - 1, middle, 0)
    sweep(SWEEP_MAX - 1, held, finish)


def first_kernel(
    levels, level_sweeps, src, f0, fy, fzs, c0, fx, fyf, ra, rb, rc, rd,
    c, d, gx, gy, p, sa, sb, sc, sd, e,
):
    def natural(ref):
        return jnp.concatenate([ref[pl.ds(k, 8, stride=4), :] for k in range(4)], axis=0)

    place = Place()
    xlo, xhi = low_high(place, 1, natural(rc), natural(rd))
    ylo, yhi = low_high(place, 0, ra[...], rb[...])
    gx[0:BS, :] = 0.5 * (fx[0:BS, :] + xlo)
    gx[BS : 2 * BS, :] = 0.5 * (fx[BS : 2 * BS, :] + xhi)
    gy[0:BS, :] = 0.5 * (fyf[0:BS, :] + ylo)
    gy[BS : 2 * BS, :] = 0.5 * (fyf[BS : 2 * BS, :] + yhi)
    add_faces_x(c, 0.5 * xlo, 0.5 * xhi)
    add_faces_y(c, 0.5 * ylo, 0.5 * yhi)

    def begin(x, _):
        at = plane(x)
        d[at, :] = RELAX / c[at, :]
        return 0

    lax.fori_loop(0, BS, begin, 0, unroll=UNROLL)

    def finish(at, value):
        p[at, :] = value

    relax(sweep_limits(levels, level_sweeps), src, e, f0, fy, fzs, d, finish)
    send_faces(place, p, sa, sb, sc, sd)


def residual_plane(src, c, f0, fy, fz, at, t0, here, after):
    w0, wy, wz = f0[at, :], fy[at, :], fz[at, :]
    total = src[at, :] - c[at, :] * here + t0 + w0 * after
    total = total + wy * next_y(here) + prev_y(wy * here)
    total = total + wz * next_z(here) + prev_z(wz * here)
    return total, w0 * here


def coarse_rhs_kernel(src, c, f0, fy, fz, p, q, scr):
    def body(xc, carry):
        t0, here = carry
        total = jnp.zeros((8, LANES), F32)
        for j in range(4):
            x = xc * 4 + j
            after = p[plane(jnp.minimum(x + 1, BS - 1)), :]
            r, t0 = residual_plane(src, c, f0, fy, fz, plane(x), t0, here, after)
            total = total + fold(r)
            here = after
        scr[pl.ds(pl.multiple_of(xc * 8, 8), 8), :] = total
        return t0, here

    lax.fori_loop(0, XC, body, (ZERO(), p[0:BS, :]))
    q[...] = group_sum(scr[...], group_matrix()) * PART


def coarse_weights_kernel(f0, fy, gx, gy, czu, czd, packed, scr, cy):
    ones = group_matrix()
    lane = lane_ids(CROWS)
    row = row_ids(CROWS)
    for xc in range(XC):
        scr[8 * xc : 8 * xc + 8, :] = fold(f0[(4 * xc + 3) * BS : (4 * xc + 4) * BS, :])
        total = fy[4 * xc * BS + 24 : 4 * xc * BS + 32, :]
        for j in range(1, 4):
            at = (4 * xc + j) * BS
            total = total + fy[at + 24 : at + 32, :]
        cy[8 * xc : 8 * xc + 8, :] = total
    c0 = group_sum(scr[...], ones) * PART
    cy[pl.ds(7, 8, stride=8), :] = by_fours(gy, BS)
    up_y = group_sum(cy[...], ones) * PART
    gxlo = group_sum(fold(gx[0:BS, :]), ones) * PART
    gxhi = group_sum(fold(gx[BS : 2 * BS, :]), ones) * PART
    up_z = group_sum(jnp.where(lane % 4 == 3, czu[...], 0.0), ones) * PART
    down_z = group_sum(jnp.where(lane % 4 == 0, czd[...], 0.0), ones) * PART
    up_0 = jnp.concatenate([c0[0 : CROWS - 8], gxhi], axis=0)
    down_0 = jnp.concatenate([gxlo, c0[0 : CROWS - 8]], axis=0)
    cy[...] = jnp.concatenate(
        [pltpu.roll(up_y[8 * xc : 8 * xc + 8], 1, 0) for xc in range(XC)], axis=0
    )
    cy[pl.ds(0, 8, stride=8), :] = group_sum(by_fours(gy, 0), ones) * PART
    scale = RELAX / (up_0 + up_y + up_z + down_0 + cy[...] + down_z)
    couple_y = jnp.where(row % 8 == 7, up_y * Place().high[0].astype(F32), up_y)
    couple_z = jnp.where(lane >= LANES - 4, 0.0, up_z)
    slot = lane % 4
    packed[...] = jnp.where(
        slot == 0, c0, jnp.where(slot == 1, couple_y, jnp.where(slot == 2, couple_z, scale))
    )


def coarse_faces_kernel(qi, gx, gy, ra, rc, rd, sb, *rest):
    packed, (ma, mb, scr) = rest[:-3], rest[-3:]
    place = Place()
    xlo, xhi = low_high(place, 1, rc[...], rd[...])
    even = place.even[0]
    own = jnp.where(jnp.full(ra.shape, even.astype(jnp.int32)) == 1, gy[BS : 2 * BS, :], gy[0:BS, :])
    scr[...] = own * ra[...]
    faces = jnp.concatenate(
        [fold(gx[0:BS, :] * xlo), fold(gx[BS : 2 * BS, :] * xhi), by_fours(scr, 0)], axis=0
    )
    faces = group_sum(faces, group_matrix()) * PART
    ma[0:CROWS, :] = qi[...]
    ma[0:8, :] = ma[0:8, :] + faces[0:8]
    ma[CROWS - 8 : CROWS, :] = ma[CROWS - 8 : CROWS, :] + faces[8:16]
    nothing = jnp.zeros((8, LANES), F32)
    at = pl.ds(0, 8, stride=8)
    ma[at, :] = ma[at, :] + pick(even, nothing, faces[16:24])
    at = pl.ds(7, 8, stride=8)
    ma[at, :] = ma[at, :] + pick(even, faces[16:24], nothing)
    mb[0:CROWS, :] = ma[0:CROWS, :]
    mb[CROWS : CROWS + BS, :] = sb[...]
    for w in packed:
        ma[CROWS : 2 * CROWS, :] = w[...]
        mb[CROWS + BS : 2 * CROWS + BS, :] = w[...]


def joined(place, own, first, second):
    low, high = low_high(place, 0, first, second)
    parts = []
    for xc in range(XC):
        at = slice(8 * xc, 8 * xc + 8)
        parts += [low[at], own[at], high[at]]
    return jnp.concatenate(parts, axis=0)


def coarse_solve(place, ma, qa, qb, sb, gy, weights, c, cyb, sa, sc, sd, scr, two):
    even = place.even[0]
    w0, wy, wz, scale = weights
    scr[...] = joined(place, ma[0:CROWS, :], qa[0:CROWS, :], qb[0:CROWS, :])
    side = pick(even, gy[0:BS, :], gy[BS : 2 * BS, :])
    there = jnp.where(even, place.low[0].astype(F32), place.high[0].astype(F32))
    two[0:BS, :] = side * qb[CROWS : CROWS + BS, :] * there
    two[BS : 2 * BS, :] = side * sb[...]
    faces = jnp.concatenate([by_fours(two, 0), by_fours(two, BS)], axis=0)
    faces = group_sum(faces, group_matrix()) * PART
    mine, theirs = faces[0:8], faces[8:16]
    nothing = jnp.zeros((8, LANES), F32)
    for row, value in (
        (8, pick(even, mine, nothing)),
        (7, pick(even, theirs, nothing)),
        (15, pick(even, nothing, mine)),
        (16, pick(even, nothing, theirs)),
    ):
        at = pl.ds(row, 8, stride=24)
        scr[at, :] = scr[at, :] + value
    rhs = scr[...]

    def up_x(v):
        return jnp.concatenate([v[24:], v[:24]], axis=0)

    def down_x(v):
        return jnp.concatenate([v[-24:], v[:-24]], axis=0)

    def by_plane(v, shift):
        return jnp.concatenate(
            [pltpu.roll(v[24 * xc : 24 * xc + 24], shift, 0) for xc in range(XC)], axis=0
        )

    field = scale * rhs
    for _ in range(CSWEEPS - 1):
        total = rhs + w0 * up_x(field) + down_x(w0 * field)
        total = total + wy * by_plane(field, 23) + by_plane(wy * field, 1)
        total = total + wz * pltpu.roll(field, LANES - 4, 1) + pltpu.roll(wz * field, 4, 1)
        field = KEEP * field + scale * total
    scr[...] = field
    for xc in range(XC):
        c[8 * xc : 8 * xc + 8, :] = field[24 * xc + 8 : 24 * xc + 16]
    cyb[...] = pick(even, scr[pl.ds(7, 8, stride=24), :], scr[pl.ds(16, 8, stride=24), :])
    sa[...] = pick(even, scr[pl.ds(15, 8, stride=24), :], scr[pl.ds(8, 8, stride=24), :])
    low, high = field[8:16], field[24 * 7 + 8 : 24 * 7 + 16]
    sc[...] = pick(place.even[1], high, low)
    sd[...] = pick(place.even[1], low, high)


def first_coarse_kernel(ma, qa, qb, sb, gy, c, cyb, sa, sc, sd, wide, scr, two):
    place = Place()
    packed = joined(
        place, ma[CROWS : 2 * CROWS, :], qa[CROWS : 2 * CROWS, :], qb[CROWS + BS :, :]
    )
    ones = group_matrix()
    slot = lane_ids(3 * CROWS) % 4
    weights = [group_sum(jnp.where(slot == j, packed, 0.0), ones) for j in range(4)]
    for j in range(4):
        wide[3 * CROWS * j : 3 * CROWS * (j + 1), :] = weights[j]
    coarse_solve(place, ma, qa, qb, sb, gy, weights, c, cyb, sa, sc, sd, scr, two)


def later_coarse_kernel(ma, qa, qb, sb, gy, wide, c, cyb, sa, sc, sd, scr, two):
    weights = [wide[3 * CROWS * j : 3 * CROWS * (j + 1), :] for j in range(4)]
    coarse_solve(Place(), ma, qa, qb, sb, gy, weights, c, cyb, sa, sc, sd, scr, two)


def spread_rows(scr, value):
    for j in range(4):
        scr[pl.ds(j, 8, stride=4), :] = value
    return scr[...]


def correct_kernel(src, c, f0, fy, fz, p, gy, qb, cc, cyb, p2, r, scr):
    def body(xc, carry):
        t0, here = carry
        add = tiled(cc[pl.ds(pl.multiple_of(xc * 8, 8), 8), :])
        later = pl.ds(pl.multiple_of(jnp.minimum(xc + 1, XC - 1) * 8, 8), 8)
        add_next = tiled(cc[later, :])
        for j in range(4):
            x = xc * 4 + j
            at = plane(x)
            after = p[plane(jnp.minimum(x + 1, BS - 1)), :] + (add if j < 3 else add_next)
            p2[at, :] = here
            r[at, :], t0 = residual_plane(src, c, f0, fy, fz, at, t0, here, after)
            here = after
        return t0, here

    lax.fori_loop(0, XC, body, (ZERO(), p[0:BS, :] + tiled(cc[0:8, :])))
    halo = qb[CROWS : CROWS + BS, :] + spread_rows(scr, cyb[...])
    ylo, yhi = low_high(Place(), 0, ZERO(), halo)
    add_faces_y(r, gy[0:BS, :] * ylo, gy[BS : 2 * BS, :] * yhi)


def residual_kernel(src, c, f0, fy, fz, p, r):
    def body(x, carry):
        t0, here = carry
        at = plane(x)
        after = p[plane(jnp.minimum(x + 1, BS - 1)), :]
        r[at, :], t1 = residual_plane(src, c, f0, fy, fz, at, t0, here, after)
        return t1, after

    lax.fori_loop(0, BS, body, (ZERO(), p[0:BS, :]), unroll=UNROLL)


def add_all(place, gx, gy, ra, rb, rc, rd, ref):
    xlo, xhi = low_high(place, 1, rc, rd)
    add_faces_x(ref, gx[0:BS, :] * xlo, gx[BS : 2 * BS, :] * xhi)
    ylo, yhi = low_high(place, 0, ra, rb)
    add_faces_y(ref, gy[0:BS, :] * ylo, gy[BS : 2 * BS, :] * yhi)


def finish_smooth(place, limit, r, f0, fy, fzs, d, p, p_out, sends, e):
    def finish(at, value):
        p_out[at, :] = p[at, :] + value

    relax(limit, r, e, f0, fy, fzs, d, finish)
    send_faces(place, p_out, *sends)


def smooth_corrected_kernel(
    levels, level_sweeps, ri, f0, fy, fzs, d, p, gx, gy, ra, rc, rd, ka, kc, kd,
    r, p_out, sa, sb, sc, sd, e, scr,
):
    place = Place()
    near = ra[...] + spread_rows(scr, ka[...])
    add_all(place, gx, gy, near, ZERO(), rc[...] + tiled(kc[...]), rd[...] + tiled(kd[...]), r)
    limit = sweep_limits(levels, level_sweeps)
    finish_smooth(place, limit, r, f0, fy, fzs, d, p, p_out, (sa, sb, sc, sd), e)


def smooth_kernel(
    levels, level_sweeps, ri, f0, fy, fzs, d, p, gx, gy, ra, rb, rc, rd,
    r, p_out, sa, sb, sc, sd, e,
):
    place = Place()
    add_all(place, gx, gy, ra[...], rb[...], rc[...], rd[...], r)
    limit = sweep_limits(levels, level_sweeps)
    finish_smooth(place, limit, r, f0, fy, fzs, d, p, p_out, (sa, sb, sc, sd), e)


def plane_to_blocks(v, x, out):
    lane = lane_ids(8)
    half = lane < 64
    even = (lane // BS) % 2 == 0
    v = [v[8 * k : 8 * k + 8] for k in range(4)]
    u = [None] * 4
    for k in range(2):
        low, high = v[k], v[k + 2]
        u[k] = jnp.where(half, low, pltpu.roll(high, 64, 1))
        u[k + 2] = jnp.where(half, pltpu.roll(low, 64, 1), high)
    for b in (0, 2):
        low, high = u[b], u[b + 1]
        first = jnp.where(even, low, pltpu.roll(high, BS, 1))
        second = jnp.where(even, pltpu.roll(low, LANES - BS, 1), high)
        out[pl.ds(pl.multiple_of(b * 256 + x * 8, 8), 8), :] = first
        out[pl.ds(pl.multiple_of((b + 1) * 256 + x * 8, 8), 8), :] = second


def last_residual_kernel(src, c, f0, fy, fz, p, r, blocks):
    def body(x, carry):
        t0, here = carry
        at = plane(x)
        after = p[plane(jnp.minimum(x + 1, BS - 1)), :]
        r[at, :], t1 = residual_plane(src, c, f0, fy, fz, at, t0, here, after)
        plane_to_blocks(here, x, blocks)
        return t1, after

    lax.fori_loop(0, BS, body, (ZERO(), p[0:BS, :]), unroll=UNROLL)


def final_kernel(ri, gx, gy, ra, rb, rc, rd, pblocks, r, blocks, sa, sb, *, count):
    place = Place()
    even = place.even[0]
    add_all(place, gx, gy, ra[...], rb[...], rc[...], rd[...], r)

    def body(x, _):
        plane_to_blocks(r[plane(x), :], x, blocks)
        return 0

    lax.fori_loop(0, BS, body, 0, unroll=UNROLL)
    size, last = count * 256, (BLK - count) * 256

    def send(t, _):
        for n, ref in enumerate((pblocks, blocks)):
            at = pl.ds(pl.multiple_of(n * size + t * 32, 32), 32)
            low = ref[pl.ds(pl.multiple_of(t * 32, 32), 32), :]
            high = ref[pl.ds(pl.multiple_of(last + t * 32, 32), 32), :]
            sa[at, :] = pick(even, high, low)
            sb[at, :] = pick(even, low, high)
        return 0

    lax.fori_loop(0, size // 32, send, 0)


def place_kernel(owned, own_p, own_r, ra, rb, out_p, out_r, nothing, sems, *, count):
    place = Place()
    even = place.even[0]
    nothing[...] = jnp.zeros_like(nothing)
    start, held = owned[0], owned[1]

    def copy(ref, base, out, n, j):
        rows = ref.at[pl.ds(pl.multiple_of(base, 256), 256), :]
        pltpu.make_async_copy(rows, out.at[:, j, :], sems.at[n, j]).start()

    outs = ((0, own_p, out_p), (1, own_r, out_r))
    for j in range(CAP):
        where = start + j - place.device * BLK
        used = j < held
        mine = used & (where >= 0) & (where < BLK)
        low = used & (where < 0)
        high = used & (where >= BLK)
        own_base = jnp.clip(where, 0, BLK - 1) * 256
        base = jnp.where(
            low, jnp.clip(where + count, 0, count - 1), jnp.clip(where - BLK, 0, count - 1)
        ) * 256
        from_a = (low & jnp.logical_not(even)) | (high & even)
        from_b = (low & even) | (high & jnp.logical_not(even))

        @pl.when(mine)
        def _():
            for n, own, out in outs:
                copy(own, own_base, out, n, j)

        @pl.when(from_a)
        def _():
            for n, own, out in outs:
                copy(ra, base + n * count * 256, out, n, j)

        @pl.when(from_b)
        def _():
            for n, own, out in outs:
                copy(rb, base + n * count * 256, out, n, j)

        @pl.when(jnp.logical_not(used))
        def _():
            for n, own, out in outs:
                pltpu.make_async_copy(nothing, out.at[:, j, :], sems.at[n, j]).start()

    for n, own, out in outs:
        for j in range(CAP):
            pltpu.make_async_copy(nothing, out.at[:, j, :], sems.at[n, j]).wait()


BOTH = ("region", "member")


def swap_near(value):
    return lax.ppermute(value, "member", [(i, i ^ 1) for i in range(lax.axis_size("member"))])


def swap_far(value):
    regions, members = lax.axis_size("region"), lax.axis_size("member")
    pairs = []
    for r in range(regions):
        for m in range(members):
            other = m + 1 if m % 2 else m - 1
            inside = 0 <= other < members
            target = r * members + other if inside else (r ^ 1) * members + m
            pairs.append((r * members + m, target))
    return lax.ppermute(value, BOTH, pairs)


def swap_regions(inner, outer):
    regions, members = lax.axis_size("region"), lax.axis_size("member")
    pairs = []
    for r in range(regions):
        other = r + 1 if r % 2 else r - 1
        inside = 0 <= other < regions
        for m in range(members):
            target = other * members + m if inside else r * members + (m ^ 1)
            pairs.append((r * members + m, target))
    inner = lax.ppermute(inner, "region", [(i, i ^ 1) for i in range(regions)])
    return inner, lax.ppermute(outer, BOTH, pairs)


def swap_blocks(first, second):
    count = lax.axis_size(BOTH)
    inner = [(i, i ^ 1) for i in range(count)]
    outer = [(i, (i + 1) % count if i % 2 else (i - 1) % count) for i in range(count)]
    return lax.ppermute(first, BOTH, inner), lax.ppermute(second, BOTH, outer)


def swap_faces(sa, sb, sc, sd):
    return (swap_near(sa), swap_far(sb), *swap_regions(sc, sd))


FULL, TWO, CFIELD = (ROWS, LANES), (2 * BS, LANES), (CROWS, LANES)
FACE, CFACE = (BS, LANES), (8, LANES)


def set_up(new_owner, src, inv):
    outs = [jax.ShapeDtypeStruct((3,), jnp.int32)] + [
        jax.ShapeDtypeStruct(s, F32) for s in [FULL] * 6 + [TWO] * 2 + [CFIELD] * 2
    ]
    vm, sm = pl.BlockSpec(memory_space=pltpu.VMEM), pl.BlockSpec(memory_space=pltpu.SMEM)
    return pl.pallas_call(
        weights_kernel,
        out_shape=outs,
        in_specs=[vm] * 3,
        out_specs=[sm] + [vm] * 10,
        compiler_params=pltpu.CompilerParams(vmem_limit_bytes=48 << 20),
        cost_estimate=pl.CostEstimate(flops=4000000, bytes_accessed=6 << 20, transcendentals=0),
    )(new_owner.reshape(-1, min(LANES, new_owner.size)), src, inv)


def place_blocks(count, owned, *arrays):
    anywhere = pl.BlockSpec(memory_space=pl.ANY)
    slots = jax.ShapeDtypeStruct((256, CAP, LANES), F32)
    outs = pl.pallas_call(
        functools.partial(place_kernel, count=count),
        out_shape=[slots, slots],
        in_specs=[pl.BlockSpec(memory_space=pltpu.SMEM)] + [anywhere] * 4,
        out_specs=[anywhere] * 2,
        scratch_shapes=[vmem(256, LANES), pltpu.SemaphoreType.DMA((2, CAP))],
    )(owned, *arrays)
    return tuple(o.transpose(1, 0, 2).reshape(CAP, 256 * LANES) for o in outs)


def on_device(source, inverse_density, block_level, level_sweeps, new_owner):
    region, member = lax.axis_index("region"), lax.axis_index("member")
    levels = (block_level, level_sweeps)
    edge = jnp.where(member % 2 == 0, BS - 1, 0)
    ia = lax.dynamic_slice_in_dim(inverse_density[1], edge, 1, axis=1)[:, 0]
    ib = lax.dynamic_slice_in_dim(inverse_density[1], BS - 1 - edge, 1, axis=1)[:, 0]
    edge = jnp.where(region % 2 == 0, BS - 1, 0)
    ic = lax.dynamic_slice_in_dim(inverse_density[0], edge, 1, axis=0)[0]
    id_ = lax.dynamic_slice_in_dim(inverse_density[0], BS - 1 - edge, 1, axis=0)[0]
    halos = swap_faces(ia, ib, ic, id_)
    owned, src, f0, fy, fz, fzs, c0, fx, fyf, czu, czd = set_up(
        new_owner, source.reshape(ROWS, LANES), inverse_density.reshape(3 * ROWS, LANES)
    )
    c, d, gx, gy, p, *sends = call(
        first_kernel,
        [FULL, FULL, TWO, TWO, FULL] + [FACE] * 4,
        [src, f0, fy, fzs, c0, fx, fyf, *halos],
        levels,
        [vmem(*FULL)],
        {4: 0},
    )
    fine = [src, c, f0, fy, fz]
    wide = None
    for cycle in range(CYCLES):
        if cycle > 0:
            halos = swap_faces(*sends)
            (ri,) = call(residual_kernel, [FULL], [*fine, p])
            _, p, *sends = call(
                smooth_kernel,
                [FULL, FULL] + [FACE] * 4,
                [ri, f0, fy, fzs, d, p, gx, gy, *halos],
                levels,
                [vmem(*FULL)],
                {0: 0},
            )
        sa, sb, sc, sd = sends
        ra = swap_near(sa)
        rc, rd = swap_regions(sc, sd)
        (qi,) = call(coarse_rhs_kernel, [CFIELD], [*fine, p], scratch=[vmem(*CFIELD)])
        packed, rows = [], CROWS
        if wide is None:
            packed = call(
                coarse_weights_kernel,
                [CFIELD],
                [f0, fy, gx, gy, czu, czd],
                scratch=[vmem(*CFIELD)] * 2,
            )
            rows = 2 * CROWS
        ma, mb = call(
            coarse_faces_kernel,
            [(rows, LANES), (rows + BS, LANES)],
            [qi, gx, gy, ra, rc, rd, sb, *packed],
            scratch=[vmem(*FACE)],
        )
        qa, qb = swap_near(ma), swap_far(mb)
        outs = [CFIELD] + [CFACE] * 4
        arrays = [ma, qa, qb, sb, gy]
        scratch = [vmem(3 * CROWS, LANES), vmem(*TWO)]
        if wide is None:
            cc, cyb, ta, tc, td, wide = call(
                first_coarse_kernel, outs + [(12 * CROWS, LANES)], arrays, scratch=scratch
            )
        else:
            cc, cyb, ta, tc, td = call(later_coarse_kernel, outs, [*arrays, wide], scratch=scratch)
        ka = swap_near(ta)
        kc, kd = swap_regions(tc, td)
        p, ri = call(
            correct_kernel, [FULL, FULL], [*fine, p, gy, qb, cc, cyb], scratch=[vmem(*FACE)]
        )
        _, p, *sends = call(
            smooth_corrected_kernel,
            [FULL, FULL] + [FACE] * 4,
            [ri, f0, fy, fzs, d, p, gx, gy, ra, rc, rd, ka, kc, kd],
            levels,
            [vmem(*FULL), vmem(*FACE)],
            {0: 0},
        )

    def tail(count, p, sends, fine, gx, gy, owned):
        halos = swap_faces(*sends)
        ri, blocks_p = call(last_residual_kernel, [FULL, FULL], [*fine, p])
        part = (2 * count * 256, LANES)
        _, blocks_r, sa, sb = call(
            functools.partial(final_kernel, count=count),
            [FULL, FULL, part, part],
            [ri, gx, gy, *halos, blocks_p],
            aliases={0: 0},
        )
        return place_blocks(count, owned, blocks_p, blocks_r, *swap_blocks(sa, sb))

    return lax.cond(
        owned[2] <= 1,
        functools.partial(tail, 1),
        functools.partial(tail, BLK),
        p, sends, fine, gx, gy, owned,
    )


def solution(mesh):
    placed = (
        P("region", "member", None),
        P(None, "region", "member", None),
        P(("region", "member")),
        P(),
        P(),
    )
    return jax.shard_map(
        on_device,
        mesh=mesh,
        in_specs=placed,
        out_specs=(P(("region", "member"), None), P(("region", "member"), None)),
        check_vma=False,
    )
```

```python
import functools

import jax
import jax.numpy as jnp
from jax import lax
from jax.experimental import pallas as pl
from jax.experimental.pallas import tpu as pltpu
from jax.sharding import PartitionSpec as P


BS = 32
BLK = 4
CSWEEPS = 8
CYCLES = 2
CAP = 6
SWEEP_MAX = 6
RELAX = 0.8
KEEP = 0.2
PART = 1.0 / 64.0
LANES = 128
ROWS = BS * BS
XC = BS // 4
CROWS = XC * XC
ZERO = functools.partial(jnp.zeros, (BS, LANES), jnp.float32)
F32 = jnp.float32


def vmem(*shape):
    return pltpu.VMEM(shape, F32)


def call(body, out_rows, args, scalars=(), scratch=(), aliases=None, flops=2e6, mib=48):
    outs = [jax.ShapeDtypeStruct(s, F32) for s in out_rows]
    moved = sum(a.size * 4 for a in args) + sum(o.size * 4 for o in outs)
    return pl.pallas_call(
        body,
        out_shape=outs,
        in_specs=[pl.BlockSpec(memory_space=pltpu.SMEM)] * len(scalars)
        + [pl.BlockSpec(memory_space=pltpu.VMEM)] * len(args),
        out_specs=[pl.BlockSpec(memory_space=pltpu.VMEM)] * len(outs),
        scratch_shapes=list(scratch),
        input_output_aliases={len(scalars) + k: v for k, v in (aliases or {}).items()},
        compiler_params=pltpu.CompilerParams(vmem_limit_bytes=mib << 20),
        cost_estimate=pl.CostEstimate(flops=int(flops), bytes_accessed=int(moved), transcendentals=0),
    )(*scalars, *args)


class Place:
    def __init__(self):
        region, member = lax.axis_index("region"), lax.axis_index("member")
        self.device = region * lax.axis_size("member") + member
        self.even = (member % 2 == 0, region % 2 == 0)
        self.low = (member > 0, region > 0)
        self.high = (member < lax.axis_size("member") - 1, region < lax.axis_size("region") - 1)


def lane_ids(rows):
    return lax.broadcasted_iota(jnp.int32, (rows, LANES), 1)


def row_ids(rows):
    return lax.broadcasted_iota(jnp.int32, (rows, LANES), 0)


def next_y(v):
    return jnp.concatenate([v[8:32], pltpu.roll(v[0:8], 7, 0)], axis=0)


def prev_y(v):
    return jnp.concatenate([pltpu.roll(v[24:32], 1, 0), v[0:24]], axis=0)


def next_z(v):
    return pltpu.roll(v, LANES - 1, 1)


def prev_z(v):
    return pltpu.roll(v, 1, 1)


def fold(v):
    return v[0:8] + v[8:16] + v[16:24] + v[24:32]


def tiled(v):
    return jnp.concatenate([v, v, v, v], axis=0)


def plane(x):
    return slice(x * BS, (x + 1) * BS)


def after_plane(x):
    return plane(min(x + 1, BS - 1))


def pick(flag, yes, no):
    return jnp.where(jnp.full(yes.shape, flag.astype(jnp.int32), jnp.int32) == 1, yes, no)


def low_high(place, axis, first, second):
    low = pick(place.even[axis], second, first) * place.low[axis].astype(F32)
    high = pick(place.even[axis], first, second) * place.high[axis].astype(F32)
    return low, high


def group_matrix():
    return jnp.where(
        row_ids(LANES) // 4 == lane_ids(LANES) // 4, jnp.float32(1.0), jnp.float32(0.0)
    )


def group_sum(v, ones):
    return lax.dot_general(
        v, ones, (((1,), (0,)), ((), ())), precision=lax.Precision.HIGHEST, preferred_element_type=F32
    )


def by_fours(ref, base):
    total = ref[pl.ds(base, 8, stride=4), :]
    for j in range(1, 4):
        total = total + ref[pl.ds(base + j, 8, stride=4), :]
    return total


def weights_kernel(new_owner, src, inv, owned, src_t, f0, fy, fz, fzs, c0, fx, fyf, czu, czd):
    row, lane = row_ids(BS), lane_ids(BS)

    def load(ref, x, offset):
        return jnp.concatenate(
            [ref[pl.ds(offset + x * BS + k, 8, stride=4), :] for k in range(4)], axis=0
        )

    before, here = ZERO(), load(inv, 0, 0)
    for xc in range(XC):
        total_up = jnp.zeros((8, LANES), F32)
        total_down = jnp.zeros((8, LANES), F32)
        for j in range(4):
            x = xc * 4 + j
            src_t[plane(x), :] = load(src, x, 0)
            after = load(inv, x + 1, 0) if x < BS - 1 else ZERO()
            one = load(inv, x, ROWS)
            two = load(inv, x, 2 * ROWS)
            one_n = jnp.where(row == BS - 1, 0.0, next_y(one))
            one_p = jnp.where(row == 0, 0.0, prev_y(one))
            two_n = jnp.where(lane == LANES - 1, 0.0, next_z(two))
            two_p = jnp.where(lane == 0, 0.0, prev_z(two))
            up0 = 0.5 * (here + after)
            upy = 0.5 * (one + one_n)
            upz = 0.5 * (two + two_n)
            downz = 0.5 * (two + two_p)
            f0[plane(x), :] = up0 if x < BS - 1 else ZERO()
            fy[plane(x), :] = jnp.where(row == BS - 1, 0.0, upy)
            fz[plane(x), :] = jnp.where(lane == LANES - 1, 0.0, upz)
            fzs[plane(x), :] = jnp.where(lane % BS == BS - 1, 0.0, upz)
            c0[plane(x), :] = up0 + upy + upz + 0.5 * (here + before) + 0.5 * (one + one_p) + downz
            total_up = total_up + fold(upz)
            total_down = total_down + fold(downz)
            before, here = here, after
        czu[8 * xc : 8 * xc + 8, :] = total_up
        czd[8 * xc : 8 * xc + 8, :] = total_down
    fx[0:BS, :] = load(inv, 0, 0)
    fx[BS : 2 * BS, :] = load(inv, BS - 1, 0)
    for g in range(4):
        fyf[8 * g : 8 * g + 8, :] = inv[pl.ds(ROWS + 256 * g, 8, stride=BS), :]
        fyf[BS + 8 * g : BS + 8 * g + 8, :] = inv[pl.ds(ROWS + 256 * g + 31, 8, stride=BS), :]
    device = Place().device
    owner = new_owner[...]
    block = lax.broadcasted_iota(jnp.int32, owner.shape, 0) * owner.shape[1]
    block = block + lax.broadcasted_iota(jnp.int32, owner.shape, 1)
    home, place = block // BLK, block % BLK
    leaving = jnp.where(owner > home, BLK - place, jnp.where(owner < home, place + 1, 0))
    owned[0] = jnp.sum((owner < device).astype(F32)).astype(jnp.int32)
    owned[1] = jnp.sum((owner == device).astype(F32)).astype(jnp.int32)
    owned[2] = jnp.max(leaving.astype(F32)).astype(jnp.int32)


def add_faces_y(ref, low, high):
    for g in range(4):
        at = pl.ds(256 * g, 8, stride=BS)
        ref[at, :] = ref[at, :] + low[8 * g : 8 * g + 8]
        at = pl.ds(256 * g + 31, 8, stride=BS)
        ref[at, :] = ref[at, :] + high[8 * g : 8 * g + 8]


def add_faces_x(ref, low, high):
    ref[0:BS, :] = ref[0:BS, :] + low
    ref[ROWS - BS : ROWS, :] = ref[ROWS - BS : ROWS, :] + high


def send_faces(place, p, sa, sb, sc, sd):
    even = place.even[0]
    for g in range(4):
        low = p[pl.ds(256 * g, 8, stride=BS), :]
        high = p[pl.ds(256 * g + 31, 8, stride=BS), :]
        sa[8 * g : 8 * g + 8, :] = pick(even, high, low)
        sb[8 * g : 8 * g + 8, :] = pick(even, low, high)
    low = p[0:BS, :]
    high = p[ROWS - BS : ROWS, :]
    sc[...] = pick(place.even[1], high, low)
    sd[...] = pick(place.even[1], low, high)


def sweep_limits(levels, level_sweeps):
    block = lane_ids(BS) // BS
    limit = jnp.zeros((BS, LANES), jnp.int32)
    for b in range(BLK):
        limit = jnp.where(block == b, level_sweeps[levels[b]], limit)
    return limit


def relax(limit, r, e, f0, fy, fzs, d, finish):
    def sweep(i, load, store):
        active = limit > i

        t0, here = ZERO(), load(plane(0))
        for x in range(BS):
            at = plane(x)
            after = load(after_plane(x))
            w0, wy, wz = f0[at, :], fy[at, :], fzs[at, :]
            t1 = w0 * here
            total = r[at, :] + t0 + w0 * after
            total = total + wy * next_y(here) + prev_y(wy * here)
            total = total + wz * next_z(here) + prev_z(wz * here)
            store(at, jnp.where(active, KEEP * here + d[at, :] * total, here))
            t0, here = t1, after

    def first(at):
        return d[at, :] * r[at, :]

    def held(at):
        return e[at, :]

    def keep(at, value):
        e[at, :] = value

    def middle(i, _):
        sweep(i, held, keep)
        return 0

    sweep(1, first, keep)
    lax.fori_loop(2, SWEEP_MAX - 1, middle, 0)
    sweep(SWEEP_MAX - 1, held, finish)


def first_kernel(
    levels, level_sweeps, src, f0, fy, fzs, c0, fx, fyf, ra, rb, rc, rd,
    c, d, gx, gy, p, sa, sb, sc, sd, e,
):
    def natural(ref):
        return jnp.concatenate([ref[pl.ds(k, 8, stride=4), :] for k in range(4)], axis=0)

    place = Place()
    xlo, xhi = low_high(place, 1, natural(rc), natural(rd))
    ylo, yhi = low_high(place, 0, ra[...], rb[...])
    gx[0:BS, :] = 0.5 * (fx[0:BS, :] + xlo)
    gx[BS : 2 * BS, :] = 0.5 * (fx[BS : 2 * BS, :] + xhi)
    gy[0:BS, :] = 0.5 * (fyf[0:BS, :] + ylo)
    gy[BS : 2 * BS, :] = 0.5 * (fyf[BS : 2 * BS, :] + yhi)
    add_faces_x(c, 0.5 * xlo, 0.5 * xhi)
    add_faces_y(c, 0.5 * ylo, 0.5 * yhi)

    for x in range(BS):
        at = plane(x)
        d[at, :] = RELAX / c[at, :]

    def finish(at, value):
        p[at, :] = value

    relax(sweep_limits(levels, level_sweeps), src, e, f0, fy, fzs, d, finish)
    send_faces(place, p, sa, sb, sc, sd)


def residual_plane(src, c, f0, fy, fz, at, t0, here, after):
    w0, wy, wz = f0[at, :], fy[at, :], fz[at, :]
    total = src[at, :] - c[at, :] * here + t0 + w0 * after
    total = total + wy * next_y(here) + prev_y(wy * here)
    total = total + wz * next_z(here) + prev_z(wz * here)
    return total, w0 * here


def coarse_rhs_kernel(src, c, f0, fy, fz, p, q, scr):
    t0, here = ZERO(), p[0:BS, :]
    for xc in range(XC):
        total = jnp.zeros((8, LANES), F32)
        for j in range(4):
            x = xc * 4 + j
            after = p[after_plane(x), :]
            r, t0 = residual_plane(src, c, f0, fy, fz, plane(x), t0, here, after)
            total = total + fold(r)
            here = after
        scr[8 * xc : 8 * xc + 8, :] = total
    q[...] = group_sum(scr[...], group_matrix()) * PART


def coarse_weights_kernel(f0, fy, gx, gy, czu, czd, packed, scr, cy):
    ones = group_matrix()
    lane = lane_ids(CROWS)
    row = row_ids(CROWS)
    for xc in range(XC):
        scr[8 * xc : 8 * xc + 8, :] = fold(f0[(4 * xc + 3) * BS : (4 * xc + 4) * BS, :])
        total = fy[4 * xc * BS + 24 : 4 * xc * BS + 32, :]
        for j in range(1, 4):
            at = (4 * xc + j) * BS
            total = total + fy[at + 24 : at + 32, :]
        cy[8 * xc : 8 * xc + 8, :] = total
    c0 = group_sum(scr[...], ones) * PART
    cy[pl.ds(7, 8, stride=8), :] = by_fours(gy, BS)
    up_y = group_sum(cy[...], ones) * PART
    gxlo = group_sum(fold(gx[0:BS, :]), ones) * PART
    gxhi = group_sum(fold(gx[BS : 2 * BS, :]), ones) * PART
    up_z = group_sum(jnp.where(lane % 4 == 3, czu[...], 0.0), ones) * PART
    down_z = group_sum(jnp.where(lane % 4 == 0, czd[...], 0.0), ones) * PART
    up_0 = jnp.concatenate([c0[0 : CROWS - 8], gxhi], axis=0)
    down_0 = jnp.concatenate([gxlo, c0[0 : CROWS - 8]], axis=0)
    cy[...] = jnp.concatenate(
        [pltpu.roll(up_y[8 * xc : 8 * xc + 8], 1, 0) for xc in range(XC)], axis=0
    )
    cy[pl.ds(0, 8, stride=8), :] = group_sum(by_fours(gy, 0), ones) * PART
    scale = RELAX / (up_0 + up_y + up_z + down_0 + cy[...] + down_z)
    couple_y = jnp.where(row % 8 == 7, up_y * Place().high[0].astype(F32), up_y)
    couple_z = jnp.where(lane >= LANES - 4, 0.0, up_z)
    slot = lane % 4
    packed[...] = jnp.where(
        slot == 0, c0, jnp.where(slot == 1, couple_y, jnp.where(slot == 2, couple_z, scale))
    )


def coarse_faces_kernel(qi, gx, gy, ra, rc, rd, sb, *rest):
    packed, (ma, mb, scr) = rest[:-3], rest[-3:]
    place = Place()
    xlo, xhi = low_high(place, 1, rc[...], rd[...])
    even = place.even[0]
    own = jnp.where(jnp.full(ra.shape, even.astype(jnp.int32)) == 1, gy[BS : 2 * BS, :], gy[0:BS, :])
    scr[...] = own * ra[...]
    faces = jnp.concatenate(
        [fold(gx[0:BS, :] * xlo), fold(gx[BS : 2 * BS, :] * xhi), by_fours(scr, 0)], axis=0
    )
    faces = group_sum(faces, group_matrix()) * PART
    ma[0:CROWS, :] = qi[...]
    ma[0:8, :] = ma[0:8, :] + faces[0:8]
    ma[CROWS - 8 : CROWS, :] = ma[CROWS - 8 : CROWS, :] + faces[8:16]
    nothing = jnp.zeros((8, LANES), F32)
    at = pl.ds(0, 8, stride=8)
    ma[at, :] = ma[at, :] + pick(even, nothing, faces[16:24])
    at = pl.ds(7, 8, stride=8)
    ma[at, :] = ma[at, :] + pick(even, faces[16:24], nothing)
    mb[0:CROWS, :] = ma[0:CROWS, :]
    mb[CROWS : CROWS + BS, :] = sb[...]
    for w in packed:
        ma[CROWS : 2 * CROWS, :] = w[...]
        mb[CROWS + BS : 2 * CROWS + BS, :] = w[...]


def joined(place, own, first, second):
    low, high = low_high(place, 0, first, second)
    parts = []
    for xc in range(XC):
        at = slice(8 * xc, 8 * xc + 8)
        parts += [low[at], own[at], high[at]]
    return jnp.concatenate(parts, axis=0)


def coarse_solve(place, ma, qa, qb, sb, gy, weights, c, cyb, sa, sc, sd, scr, two):
    even = place.even[0]
    w0, wy, wz, scale = weights
    scr[...] = joined(place, ma[0:CROWS, :], qa[0:CROWS, :], qb[0:CROWS, :])
    side = pick(even, gy[0:BS, :], gy[BS : 2 * BS, :])
    there = jnp.where(even, place.low[0].astype(F32), place.high[0].astype(F32))
    two[0:BS, :] = side * qb[CROWS : CROWS + BS, :] * there
    two[BS : 2 * BS, :] = side * sb[...]
    faces = jnp.concatenate([by_fours(two, 0), by_fours(two, BS)], axis=0)
    faces = group_sum(faces, group_matrix()) * PART
    mine, theirs = faces[0:8], faces[8:16]
    nothing = jnp.zeros((8, LANES), F32)
    for row, value in (
        (8, pick(even, mine, nothing)),
        (7, pick(even, theirs, nothing)),
        (15, pick(even, nothing, mine)),
        (16, pick(even, nothing, theirs)),
    ):
        at = pl.ds(row, 8, stride=24)
        scr[at, :] = scr[at, :] + value
    rhs = scr[...]

    def up_x(v):
        return jnp.concatenate([v[24:], v[:24]], axis=0)

    def down_x(v):
        return jnp.concatenate([v[-24:], v[:-24]], axis=0)

    def by_plane(v, shift):
        return jnp.concatenate(
            [pltpu.roll(v[24 * xc : 24 * xc + 24], shift, 0) for xc in range(XC)], axis=0
        )

    field = scale * rhs
    for _ in range(CSWEEPS - 1):
        total = rhs + w0 * up_x(field) + down_x(w0 * field)
        total = total + wy * by_plane(field, 23) + by_plane(wy * field, 1)
        total = total + wz * pltpu.roll(field, LANES - 4, 1) + pltpu.roll(wz * field, 4, 1)
        field = KEEP * field + scale * total
    scr[...] = field
    for xc in range(XC):
        c[8 * xc : 8 * xc + 8, :] = field[24 * xc + 8 : 24 * xc + 16]
    cyb[...] = pick(even, scr[pl.ds(7, 8, stride=24), :], scr[pl.ds(16, 8, stride=24), :])
    sa[...] = pick(even, scr[pl.ds(15, 8, stride=24), :], scr[pl.ds(8, 8, stride=24), :])
    low, high = field[8:16], field[24 * 7 + 8 : 24 * 7 + 16]
    sc[...] = pick(place.even[1], high, low)
    sd[...] = pick(place.even[1], low, high)


def first_coarse_kernel(ma, qa, qb, sb, gy, c, cyb, sa, sc, sd, wide, scr, two):
    place = Place()
    packed = joined(
        place, ma[CROWS : 2 * CROWS, :], qa[CROWS : 2 * CROWS, :], qb[CROWS + BS :, :]
    )
    ones = group_matrix()
    slot = lane_ids(3 * CROWS) % 4
    weights = [group_sum(jnp.where(slot == j, packed, 0.0), ones) for j in range(4)]
    for j in range(4):
        wide[3 * CROWS * j : 3 * CROWS * (j + 1), :] = weights[j]
    coarse_solve(place, ma, qa, qb, sb, gy, weights, c, cyb, sa, sc, sd, scr, two)


def later_coarse_kernel(ma, qa, qb, sb, gy, wide, c, cyb, sa, sc, sd, scr, two):
    weights = [wide[3 * CROWS * j : 3 * CROWS * (j + 1), :] for j in range(4)]
    coarse_solve(Place(), ma, qa, qb, sb, gy, weights, c, cyb, sa, sc, sd, scr, two)


def spread_rows(scr, value):
    for j in range(4):
        scr[pl.ds(j, 8, stride=4), :] = value
    return scr[...]


def correct_kernel(src, c, f0, fy, fz, p, gy, qb, cc, cyb, p2, r, scr):
    def corrected(x):
        return p[plane(x), :] + tiled(cc[8 * (x // 4) : 8 * (x // 4) + 8, :])

    t0, here = ZERO(), corrected(0)
    for x in range(BS):
        at = plane(x)
        after = corrected(min(x + 1, BS - 1))
        p2[at, :] = here
        r[at, :], t0 = residual_plane(src, c, f0, fy, fz, at, t0, here, after)
        here = after
    halo = qb[CROWS : CROWS + BS, :] + spread_rows(scr, cyb[...])
    ylo, yhi = low_high(Place(), 0, ZERO(), halo)
    add_faces_y(r, gy[0:BS, :] * ylo, gy[BS : 2 * BS, :] * yhi)


def residual_kernel(src, c, f0, fy, fz, p, r):
    t0, here = ZERO(), p[0:BS, :]
    for x in range(BS):
        at = plane(x)
        after = p[after_plane(x), :]
        r[at, :], t0 = residual_plane(src, c, f0, fy, fz, at, t0, here, after)
        here = after


def add_all(place, gx, gy, ra, rb, rc, rd, ref):
    xlo, xhi = low_high(place, 1, rc, rd)
    add_faces_x(ref, gx[0:BS, :] * xlo, gx[BS : 2 * BS, :] * xhi)
    ylo, yhi = low_high(place, 0, ra, rb)
    add_faces_y(ref, gy[0:BS, :] * ylo, gy[BS : 2 * BS, :] * yhi)


def finish_smooth(place, limit, r, f0, fy, fzs, d, p, p_out, sends, e):
    def finish(at, value):
        p_out[at, :] = p[at, :] + value

    relax(limit, r, e, f0, fy, fzs, d, finish)
    send_faces(place, p_out, *sends)


def smooth_corrected_kernel(
    levels, level_sweeps, ri, f0, fy, fzs, d, p, gx, gy, ra, rc, rd, ka, kc, kd,
    r, p_out, sa, sb, sc, sd, e, scr,
):
    place = Place()
    near = ra[...] + spread_rows(scr, ka[...])
    add_all(place, gx, gy, near, ZERO(), rc[...] + tiled(kc[...]), rd[...] + tiled(kd[...]), r)
    limit = sweep_limits(levels, level_sweeps)
    finish_smooth(place, limit, r, f0, fy, fzs, d, p, p_out, (sa, sb, sc, sd), e)


def smooth_kernel(
    levels, level_sweeps, ri, f0, fy, fzs, d, p, gx, gy, ra, rb, rc, rd,
    r, p_out, sa, sb, sc, sd, e,
):
    place = Place()
    add_all(place, gx, gy, ra[...], rb[...], rc[...], rd[...], r)
    limit = sweep_limits(levels, level_sweeps)
    finish_smooth(place, limit, r, f0, fy, fzs, d, p, p_out, (sa, sb, sc, sd), e)


def plane_to_blocks(v, x, out):
    lane = lane_ids(8)
    half = lane < 64
    even = (lane // BS) % 2 == 0
    v = [v[8 * k : 8 * k + 8] for k in range(4)]
    u = [None] * 4
    for k in range(2):
        low, high = v[k], v[k + 2]
        u[k] = jnp.where(half, low, pltpu.roll(high, 64, 1))
        u[k + 2] = jnp.where(half, pltpu.roll(low, 64, 1), high)
    for b in (0, 2):
        low, high = u[b], u[b + 1]
        first = jnp.where(even, low, pltpu.roll(high, BS, 1))
        second = jnp.where(even, pltpu.roll(low, LANES - BS, 1), high)
        out[b * 256 + x * 8 : b * 256 + x * 8 + 8, :] = first
        out[(b + 1) * 256 + x * 8 : (b + 1) * 256 + x * 8 + 8, :] = second


def last_residual_kernel(src, c, f0, fy, fz, p, r, blocks):
    t0, here = ZERO(), p[0:BS, :]
    for x in range(BS):
        at = plane(x)
        after = p[after_plane(x), :]
        r[at, :], t0 = residual_plane(src, c, f0, fy, fz, at, t0, here, after)
        plane_to_blocks(here, x, blocks)
        here = after


def final_kernel(ri, gx, gy, ra, rb, rc, rd, pblocks, r, blocks, sa, sb, *, count):
    place = Place()
    even = place.even[0]
    add_all(place, gx, gy, ra[...], rb[...], rc[...], rd[...], r)

    for x in range(BS):
        plane_to_blocks(r[plane(x), :], x, blocks)
    size, last = count * 256, (BLK - count) * 256
    for n, ref in enumerate((pblocks, blocks)):
        for t in range(0, size, 32):
            low, high = ref[t : t + 32, :], ref[last + t : last + t + 32, :]
            at = slice(n * size + t, n * size + t + 32)
            sa[at, :] = pick(even, high, low)
            sb[at, :] = pick(even, low, high)


def place_kernel(owned, own_p, own_r, ra, rb, out_p, out_r, *, count):
    place = Place()
    even = place.even[0]
    start, held = owned[0], owned[1]
    fields = ((0, own_p, out_p), (1, own_r, out_r))

    def fill(ref, base, out, j):
        for t in range(0, 256, 8):
            out[t : t + 8, j, :] = ref[pl.ds(pl.multiple_of(base + t, 8), 8), :]

    for j in range(CAP):
        where = start + j - place.device * BLK
        used = j < held
        mine = used & (where >= 0) & (where < BLK)
        low = used & (where < 0)
        high = used & (where >= BLK)
        own_base = jnp.clip(where, 0, BLK - 1) * 256
        base = jnp.where(
            low, jnp.clip(where + count, 0, count - 1), jnp.clip(where - BLK, 0, count - 1)
        ) * 256
        from_a = (low & jnp.logical_not(even)) | (high & even)
        from_b = (low & even) | (high & jnp.logical_not(even))

        @pl.when(mine)
        def _():
            for n, own, out in fields:
                fill(own, own_base, out, j)

        @pl.when(from_a)
        def _():
            for n, own, out in fields:
                fill(ra, base + n * count * 256, out, j)

        @pl.when(from_b)
        def _():
            for n, own, out in fields:
                fill(rb, base + n * count * 256, out, j)

        @pl.when(jnp.logical_not(used))
        def _():
            for n, own, out in fields:
                for t in range(0, 256, 8):
                    out[t : t + 8, j, :] = jnp.zeros((8, LANES), F32)


BOTH = ("region", "member")


def swap_near(value):
    return lax.ppermute(value, "member", [(i, i ^ 1) for i in range(lax.axis_size("member"))])


def swap_far(value):
    regions, members = lax.axis_size("region"), lax.axis_size("member")
    pairs = []
    for r in range(regions):
        for m in range(members):
            other = m + 1 if m % 2 else m - 1
            inside = 0 <= other < members
            target = r * members + other if inside else (r ^ 1) * members + m
            pairs.append((r * members + m, target))
    return lax.ppermute(value, BOTH, pairs)


def swap_regions(inner, outer):
    regions, members = lax.axis_size("region"), lax.axis_size("member")
    pairs = []
    for r in range(regions):
        other = r + 1 if r % 2 else r - 1
        inside = 0 <= other < regions
        for m in range(members):
            target = other * members + m if inside else r * members + (m ^ 1)
            pairs.append((r * members + m, target))
    inner = lax.ppermute(inner, "region", [(i, i ^ 1) for i in range(regions)])
    return inner, lax.ppermute(outer, BOTH, pairs)


def swap_blocks(first, second):
    count = lax.axis_size(BOTH)
    inner = [(i, i ^ 1) for i in range(count)]
    outer = [(i, (i + 1) % count if i % 2 else (i - 1) % count) for i in range(count)]
    return lax.ppermute(first, BOTH, inner), lax.ppermute(second, BOTH, outer)


def swap_faces(sa, sb, sc, sd):
    return (swap_near(sa), swap_far(sb), *swap_regions(sc, sd))


FULL, TWO, CFIELD = (ROWS, LANES), (2 * BS, LANES), (CROWS, LANES)
FACE, CFACE = (BS, LANES), (8, LANES)


def set_up(new_owner, src, inv):
    outs = [jax.ShapeDtypeStruct((3,), jnp.int32)] + [
        jax.ShapeDtypeStruct(s, F32) for s in [FULL] * 6 + [TWO] * 2 + [CFIELD] * 2
    ]
    vm, sm = pl.BlockSpec(memory_space=pltpu.VMEM), pl.BlockSpec(memory_space=pltpu.SMEM)
    return pl.pallas_call(
        weights_kernel,
        out_shape=outs,
        in_specs=[vm] * 3,
        out_specs=[sm] + [vm] * 10,
        compiler_params=pltpu.CompilerParams(vmem_limit_bytes=48 << 20),
        cost_estimate=pl.CostEstimate(flops=4000000, bytes_accessed=6 << 20, transcendentals=0),
    )(new_owner.reshape(-1, min(LANES, new_owner.size)), src, inv)


def place_blocks(count, owned, *arrays):
    slots = (256, CAP, LANES)
    outs = call(functools.partial(place_kernel, count=count), [slots, slots], arrays, [owned])
    return tuple(o.transpose(1, 0, 2).reshape(CAP, 256 * LANES) for o in outs)


def on_device(source, inverse_density, block_level, level_sweeps, new_owner):
    region, member = lax.axis_index("region"), lax.axis_index("member")
    levels = (block_level, level_sweeps)
    edge = jnp.where(member % 2 == 0, BS - 1, 0)
    ia = lax.dynamic_slice_in_dim(inverse_density[1], edge, 1, axis=1)[:, 0]
    ib = lax.dynamic_slice_in_dim(inverse_density[1], BS - 1 - edge, 1, axis=1)[:, 0]
    edge = jnp.where(region % 2 == 0, BS - 1, 0)
    ic = lax.dynamic_slice_in_dim(inverse_density[0], edge, 1, axis=0)[0]
    id_ = lax.dynamic_slice_in_dim(inverse_density[0], BS - 1 - edge, 1, axis=0)[0]
    halos = swap_faces(ia, ib, ic, id_)
    owned, src, f0, fy, fz, fzs, c0, fx, fyf, czu, czd = set_up(
        new_owner, source.reshape(ROWS, LANES), inverse_density.reshape(3 * ROWS, LANES)
    )
    c, d, gx, gy, p, *sends = call(
        first_kernel,
        [FULL, FULL, TWO, TWO, FULL] + [FACE] * 4,
        [src, f0, fy, fzs, c0, fx, fyf, *halos],
        levels,
        [vmem(*FULL)],
        {4: 0},
    )
    fine = [src, c, f0, fy, fz]
    wide = None
    for cycle in range(CYCLES):
        if cycle > 0:
            halos = swap_faces(*sends)
            (ri,) = call(residual_kernel, [FULL], [*fine, p])
            _, p, *sends = call(
                smooth_kernel,
                [FULL, FULL] + [FACE] * 4,
                [ri, f0, fy, fzs, d, p, gx, gy, *halos],
                levels,
                [vmem(*FULL)],
                {0: 0},
            )
        sa, sb, sc, sd = sends
        ra = swap_near(sa)
        rc, rd = swap_regions(sc, sd)
        (qi,) = call(coarse_rhs_kernel, [CFIELD], [*fine, p], scratch=[vmem(*CFIELD)])
        packed, rows = [], CROWS
        if wide is None:
            packed = call(
                coarse_weights_kernel,
                [CFIELD],
                [f0, fy, gx, gy, czu, czd],
                scratch=[vmem(*CFIELD)] * 2,
            )
            rows = 2 * CROWS
        ma, mb = call(
            coarse_faces_kernel,
            [(rows, LANES), (rows + BS, LANES)],
            [qi, gx, gy, ra, rc, rd, sb, *packed],
            scratch=[vmem(*FACE)],
        )
        qa, qb = swap_near(ma), swap_far(mb)
        outs = [CFIELD] + [CFACE] * 4
        arrays = [ma, qa, qb, sb, gy]
        scratch = [vmem(3 * CROWS, LANES), vmem(*TWO)]
        if wide is None:
            cc, cyb, ta, tc, td, wide = call(
                first_coarse_kernel, outs + [(12 * CROWS, LANES)], arrays, scratch=scratch
            )
        else:
            cc, cyb, ta, tc, td = call(later_coarse_kernel, outs, [*arrays, wide], scratch=scratch)
        ka = swap_near(ta)
        kc, kd = swap_regions(tc, td)
        p, ri = call(
            correct_kernel, [FULL, FULL], [*fine, p, gy, qb, cc, cyb], scratch=[vmem(*FACE)]
        )
        _, p, *sends = call(
            smooth_corrected_kernel,
            [FULL, FULL] + [FACE] * 4,
            [ri, f0, fy, fzs, d, p, gx, gy, ra, rc, rd, ka, kc, kd],
            levels,
            [vmem(*FULL), vmem(*FACE)],
            {0: 0},
        )

    def tail(count, p, sends, fine, gx, gy, owned):
        halos = swap_faces(*sends)
        ri, blocks_p = call(last_residual_kernel, [FULL, FULL], [*fine, p])
        part = (2 * count * 256, LANES)
        _, blocks_r, sa, sb = call(
            functools.partial(final_kernel, count=count),
            [FULL, FULL, part, part],
            [ri, gx, gy, *halos, blocks_p],
            aliases={0: 0},
        )
        return place_blocks(count, owned, blocks_p, blocks_r, *swap_blocks(sa, sb))

    return lax.cond(
        owned[2] <= 1,
        functools.partial(tail, 1),
        functools.partial(tail, BLK),
        p, sends, fine, gx, gy, owned,
    )


def solution(mesh):
    placed = (
        P("region", "member", None),
        P(None, "region", "member", None),
        P(("region", "member")),
        P(),
        P(),
    )
    return jax.shard_map(
        on_device,
        mesh=mesh,
        in_specs=placed,
        out_specs=(P(("region", "member"), None), P(("region", "member"), None)),
        check_vma=False,
    )
```

```python
import functools

import jax
import jax.numpy as jnp
from jax import lax
from jax.experimental import pallas as pl
from jax.experimental.pallas import tpu as pltpu
from jax.sharding import PartitionSpec as P


BS = 32
BLK = 4
CSWEEPS = 8
CYCLES = 2
CAP = 6
SWEEP_MAX = 6
RELAX = 0.8
KEEP = 0.2
PART = 1.0 / 64.0
STEP = 264
LANES = 128
ROWS = BS * BS
XC = BS // 4
CROWS = XC * XC
ZERO = functools.partial(jnp.zeros, (BS, LANES), jnp.float32)
F32 = jnp.float32


def vmem(*shape):
    return pltpu.VMEM(shape, F32)


def call(body, out_rows, args, scalars=(), scratch=(), aliases=None, flops=2e6, mib=48):
    outs = [jax.ShapeDtypeStruct(s, F32) for s in out_rows]
    moved = sum(a.size * 4 for a in args) + sum(o.size * 4 for o in outs)
    return pl.pallas_call(
        body,
        out_shape=outs,
        in_specs=[pl.BlockSpec(memory_space=pltpu.SMEM)] * len(scalars)
        + [pl.BlockSpec(memory_space=pltpu.VMEM)] * len(args),
        out_specs=[pl.BlockSpec(memory_space=pltpu.VMEM)] * len(outs),
        scratch_shapes=list(scratch),
        input_output_aliases={len(scalars) + k: v for k, v in (aliases or {}).items()},
        compiler_params=pltpu.CompilerParams(vmem_limit_bytes=mib << 20),
        cost_estimate=pl.CostEstimate(flops=int(flops), bytes_accessed=int(moved), transcendentals=0),
    )(*scalars, *args)


class Place:
    def __init__(self):
        region, member = lax.axis_index("region"), lax.axis_index("member")
        self.device = region * lax.axis_size("member") + member
        self.even = (member % 2 == 0, region % 2 == 0)
        self.low = (member > 0, region > 0)
        self.high = (member < lax.axis_size("member") - 1, region < lax.axis_size("region") - 1)


def lane_ids(rows):
    return lax.broadcasted_iota(jnp.int32, (rows, LANES), 1)


def row_ids(rows):
    return lax.broadcasted_iota(jnp.int32, (rows, LANES), 0)


def next_y(v):
    return jnp.concatenate([v[8:32], pltpu.roll(v[0:8], 7, 0)], axis=0)


def prev_y(v):
    return jnp.concatenate([pltpu.roll(v[24:32], 1, 0), v[0:24]], axis=0)


def next_z(v):
    return pltpu.roll(v, LANES - 1, 1)


def prev_z(v):
    return pltpu.roll(v, 1, 1)


def fold(v):
    return v[0:8] + v[8:16] + v[16:24] + v[24:32]


def tiled(v):
    return jnp.concatenate([v, v, v, v], axis=0)


def plane(x):
    return slice(x * BS, (x + 1) * BS)


def after_plane(x):
    return plane(min(x + 1, BS - 1))


def pick(flag, yes, no):
    return jnp.where(jnp.full(yes.shape, flag.astype(jnp.int32), jnp.int32) == 1, yes, no)


def low_high(place, axis, first, second):
    low = pick(place.even[axis], second, first) * place.low[axis].astype(F32)
    high = pick(place.even[axis], first, second) * place.high[axis].astype(F32)
    return low, high


def group_matrix():
    return jnp.where(
        row_ids(LANES) // 4 == lane_ids(LANES) // 4, jnp.float32(1.0), jnp.float32(0.0)
    )


def group_sum(v, ones):
    return lax.dot_general(
        v, ones, (((1,), (0,)), ((), ())), precision=lax.Precision.HIGHEST, preferred_element_type=F32
    )


def by_fours(ref, base):
    total = ref[pl.ds(base, 8, stride=4), :]
    for j in range(1, 4):
        total = total + ref[pl.ds(base + j, 8, stride=4), :]
    return total


def weights_kernel(new_owner, src, inv, owned, most, src_t, f0, fy, fz, fzs, c0, fx, fyf, czu, czd):
    row, lane = row_ids(BS), lane_ids(BS)

    def load(ref, x, offset):
        return jnp.concatenate(
            [ref[pl.ds(offset + x * BS + k, 8, stride=4), :] for k in range(4)], axis=0
        )

    before, here = ZERO(), load(inv, 0, 0)
    for xc in range(XC):
        total_up = jnp.zeros((8, LANES), F32)
        total_down = jnp.zeros((8, LANES), F32)
        for j in range(4):
            x = xc * 4 + j
            src_t[plane(x), :] = load(src, x, 0)
            after = load(inv, x + 1, 0) if x < BS - 1 else ZERO()
            one = load(inv, x, ROWS)
            two = load(inv, x, 2 * ROWS)
            one_n = jnp.where(row == BS - 1, 0.0, next_y(one))
            one_p = jnp.where(row == 0, 0.0, prev_y(one))
            two_n = jnp.where(lane == LANES - 1, 0.0, next_z(two))
            two_p = jnp.where(lane == 0, 0.0, prev_z(two))
            up0 = 0.5 * (here + after)
            upy = 0.5 * (one + one_n)
            upz = 0.5 * (two + two_n)
            downz = 0.5 * (two + two_p)
            f0[plane(x), :] = up0 if x < BS - 1 else ZERO()
            fy[plane(x), :] = jnp.where(row == BS - 1, 0.0, upy)
            fz[plane(x), :] = jnp.where(lane == LANES - 1, 0.0, upz)
            fzs[plane(x), :] = jnp.where(lane % BS == BS - 1, 0.0, upz)
            c0[plane(x), :] = up0 + upy + upz + 0.5 * (here + before) + 0.5 * (one + one_p) + downz
            total_up = total_up + fold(upz)
            total_down = total_down + fold(downz)
            before, here = here, after
        czu[8 * xc : 8 * xc + 8, :] = total_up
        czd[8 * xc : 8 * xc + 8, :] = total_down
    fx[0:BS, :] = load(inv, 0, 0)
    fx[BS : 2 * BS, :] = load(inv, BS - 1, 0)
    for g in range(4):
        fyf[8 * g : 8 * g + 8, :] = inv[pl.ds(ROWS + 256 * g, 8, stride=BS), :]
        fyf[BS + 8 * g : BS + 8 * g + 8, :] = inv[pl.ds(ROWS + 256 * g + 31, 8, stride=BS), :]
    device = Place().device
    owner = new_owner[...]
    block = lax.broadcasted_iota(jnp.int32, owner.shape, 0) * owner.shape[1]
    block = block + lax.broadcasted_iota(jnp.int32, owner.shape, 1)
    home, place = block // BLK, block % BLK
    leaving = jnp.where(owner > home, BLK - place, jnp.where(owner < home, place + 1, 0))
    owned[0] = jnp.sum((owner < device).astype(F32)).astype(jnp.int32)
    owned[1] = jnp.sum((owner == device).astype(F32)).astype(jnp.int32)
    most[0] = jnp.max(leaving.astype(F32)).astype(jnp.int32)


def add_faces_y(ref, low, high):
    for g in range(4):
        at = pl.ds(256 * g, 8, stride=BS)
        ref[at, :] = ref[at, :] + low[8 * g : 8 * g + 8]
        at = pl.ds(256 * g + 31, 8, stride=BS)
        ref[at, :] = ref[at, :] + high[8 * g : 8 * g + 8]


def add_faces_x(ref, low, high):
    ref[0:BS, :] = ref[0:BS, :] + low
    ref[ROWS - BS : ROWS, :] = ref[ROWS - BS : ROWS, :] + high


def send_faces(place, p, sa, sb, sc, sd):
    even = place.even[0]
    for g in range(4):
        low = p[pl.ds(256 * g, 8, stride=BS), :]
        high = p[pl.ds(256 * g + 31, 8, stride=BS), :]
        sa[8 * g : 8 * g + 8, :] = pick(even, high, low)
        sb[8 * g : 8 * g + 8, :] = pick(even, low, high)
    low = p[0:BS, :]
    high = p[ROWS - BS : ROWS, :]
    sc[...] = pick(place.even[1], high, low)
    sd[...] = pick(place.even[1], low, high)


def sweep_limits(levels, level_sweeps):
    block = lane_ids(BS) // BS
    limit = jnp.zeros((BS, LANES), jnp.int32)
    for b in range(BLK):
        limit = jnp.where(block == b, level_sweeps[levels[b]], limit)
    return limit


def relax(limit, r, e, f0, fy, fzs, d, finish):
    def sweep(i, load, store):
        active = limit > i

        t0, here = ZERO(), load(plane(0))
        for x in range(BS):
            at = plane(x)
            after = load(after_plane(x))
            w0, wy, wz = f0[at, :], fy[at, :], fzs[at, :]
            t1 = w0 * here
            total = r[at, :] + t0 + w0 * after
            total = total + wy * next_y(here) + prev_y(wy * here)
            total = total + wz * next_z(here) + prev_z(wz * here)
            store(at, jnp.where(active, KEEP * here + d[at, :] * total, here))
            t0, here = t1, after

    def first(at):
        return d[at, :] * r[at, :]

    def held(at):
        return e[at, :]

    def keep(at, value):
        e[at, :] = value

    sweep(1, first, keep)
    for i in range(2, SWEEP_MAX - 1):
        sweep(i, held, keep)
    sweep(SWEEP_MAX - 1, held, finish)


def first_kernel(
    levels, level_sweeps, src, f0, fy, fzs, c0, fx, fyf, ra, rb, rc, rd,
    c, d, gx, gy, p, sa, sb, sc, sd, e,
):
    def natural(ref):
        return jnp.concatenate([ref[pl.ds(k, 8, stride=4), :] for k in range(4)], axis=0)

    place = Place()
    xlo, xhi = low_high(place, 1, natural(rc), natural(rd))
    ylo, yhi = low_high(place, 0, ra[...], rb[...])
    gx[0:BS, :] = 0.5 * (fx[0:BS, :] + xlo)
    gx[BS : 2 * BS, :] = 0.5 * (fx[BS : 2 * BS, :] + xhi)
    gy[0:BS, :] = 0.5 * (fyf[0:BS, :] + ylo)
    gy[BS : 2 * BS, :] = 0.5 * (fyf[BS : 2 * BS, :] + yhi)
    add_faces_x(c, 0.5 * xlo, 0.5 * xhi)
    add_faces_y(c, 0.5 * ylo, 0.5 * yhi)

    for x in range(BS):
        at = plane(x)
        d[at, :] = RELAX / c[at, :]

    def finish(at, value):
        p[at, :] = value

    relax(sweep_limits(levels, level_sweeps), src, e, f0, fy, fzs, d, finish)
    send_faces(place, p, sa, sb, sc, sd)


def residual_plane(src, c, f0, fy, fz, at, t0, here, after):
    w0, wy, wz = f0[at, :], fy[at, :], fz[at, :]
    total = src[at, :] - c[at, :] * here + t0 + w0 * after
    total = total + wy * next_y(here) + prev_y(wy * here)
    total = total + wz * next_z(here) + prev_z(wz * here)
    return total, w0 * here


def coarse_rhs_kernel(src, c, f0, fy, fz, p, q, scr):
    t0, here = ZERO(), p[0:BS, :]
    for xc in range(XC):
        total = jnp.zeros((8, LANES), F32)
        for j in range(4):
            x = xc * 4 + j
            after = p[after_plane(x), :]
            r, t0 = residual_plane(src, c, f0, fy, fz, plane(x), t0, here, after)
            total = total + fold(r)
            here = after
        scr[8 * xc : 8 * xc + 8, :] = total
    q[...] = group_sum(scr[...], group_matrix()) * PART


def coarse_weights_kernel(f0, fy, gx, gy, czu, czd, packed, scr, cy):
    ones = group_matrix()
    lane = lane_ids(CROWS)
    row = row_ids(CROWS)
    for xc in range(XC):
        scr[8 * xc : 8 * xc + 8, :] = fold(f0[(4 * xc + 3) * BS : (4 * xc + 4) * BS, :])
        total = fy[4 * xc * BS + 24 : 4 * xc * BS + 32, :]
        for j in range(1, 4):
            at = (4 * xc + j) * BS
            total = total + fy[at + 24 : at + 32, :]
        cy[8 * xc : 8 * xc + 8, :] = total
    c0 = group_sum(scr[...], ones) * PART
    cy[pl.ds(7, 8, stride=8), :] = by_fours(gy, BS)
    up_y = group_sum(cy[...], ones) * PART
    gxlo = group_sum(fold(gx[0:BS, :]), ones) * PART
    gxhi = group_sum(fold(gx[BS : 2 * BS, :]), ones) * PART
    up_z = group_sum(jnp.where(lane % 4 == 3, czu[...], 0.0), ones) * PART
    down_z = group_sum(jnp.where(lane % 4 == 0, czd[...], 0.0), ones) * PART
    up_0 = jnp.concatenate([c0[0 : CROWS - 8], gxhi], axis=0)
    down_0 = jnp.concatenate([gxlo, c0[0 : CROWS - 8]], axis=0)
    cy[...] = jnp.concatenate(
        [pltpu.roll(up_y[8 * xc : 8 * xc + 8], 1, 0) for xc in range(XC)], axis=0
    )
    cy[pl.ds(0, 8, stride=8), :] = group_sum(by_fours(gy, 0), ones) * PART
    scale = RELAX / (up_0 + up_y + up_z + down_0 + cy[...] + down_z)
    couple_y = jnp.where(row % 8 == 7, up_y * Place().high[0].astype(F32), up_y)
    couple_z = jnp.where(lane >= LANES - 4, 0.0, up_z)
    slot = lane % 4
    packed[...] = jnp.where(
        slot == 0, c0, jnp.where(slot == 1, couple_y, jnp.where(slot == 2, couple_z, scale))
    )


def coarse_faces_kernel(qi, gx, gy, ra, rc, rd, sb, *rest):
    packed, (ma, mb, scr) = rest[:-3], rest[-3:]
    place = Place()
    xlo, xhi = low_high(place, 1, rc[...], rd[...])
    even = place.even[0]
    own = jnp.where(jnp.full(ra.shape, even.astype(jnp.int32)) == 1, gy[BS : 2 * BS, :], gy[0:BS, :])
    scr[...] = own * ra[...]
    faces = jnp.concatenate(
        [fold(gx[0:BS, :] * xlo), fold(gx[BS : 2 * BS, :] * xhi), by_fours(scr, 0)], axis=0
    )
    faces = group_sum(faces, group_matrix()) * PART
    ma[0:CROWS, :] = qi[...]
    ma[0:8, :] = ma[0:8, :] + faces[0:8]
    ma[CROWS - 8 : CROWS, :] = ma[CROWS - 8 : CROWS, :] + faces[8:16]
    nothing = jnp.zeros((8, LANES), F32)
    at = pl.ds(0, 8, stride=8)
    ma[at, :] = ma[at, :] + pick(even, nothing, faces[16:24])
    at = pl.ds(7, 8, stride=8)
    ma[at, :] = ma[at, :] + pick(even, faces[16:24], nothing)
    mb[0:CROWS, :] = ma[0:CROWS, :]
    mb[CROWS : CROWS + BS, :] = sb[...]
    for w in packed:
        ma[CROWS : 2 * CROWS, :] = w[...]
        mb[CROWS + BS : 2 * CROWS + BS, :] = w[...]


def joined(place, own, first, second):
    low, high = low_high(place, 0, first, second)
    parts = []
    for xc in range(XC):
        at = slice(8 * xc, 8 * xc + 8)
        parts += [low[at], own[at], high[at]]
    return jnp.concatenate(parts, axis=0)


def coarse_solve(place, ma, qa, qb, sb, gy, weights, c, cyb, sa, sc, sd, scr, two):
    even = place.even[0]
    w0, wy, wz, scale = weights
    scr[...] = joined(place, ma[0:CROWS, :], qa[0:CROWS, :], qb[0:CROWS, :])
    side = pick(even, gy[0:BS, :], gy[BS : 2 * BS, :])
    there = jnp.where(even, place.low[0].astype(F32), place.high[0].astype(F32))
    two[0:BS, :] = side * qb[CROWS : CROWS + BS, :] * there
    two[BS : 2 * BS, :] = side * sb[...]
    faces = jnp.concatenate([by_fours(two, 0), by_fours(two, BS)], axis=0)
    faces = group_sum(faces, group_matrix()) * PART
    mine, theirs = faces[0:8], faces[8:16]
    nothing = jnp.zeros((8, LANES), F32)
    for row, value in (
        (8, pick(even, mine, nothing)),
        (7, pick(even, theirs, nothing)),
        (15, pick(even, nothing, mine)),
        (16, pick(even, nothing, theirs)),
    ):
        at = pl.ds(row, 8, stride=24)
        scr[at, :] = scr[at, :] + value
    rhs = scr[...]

    def up_x(v):
        return jnp.concatenate([v[24:], v[:24]], axis=0)

    def down_x(v):
        return jnp.concatenate([v[-24:], v[:-24]], axis=0)

    def by_plane(v, shift):
        return jnp.concatenate(
            [pltpu.roll(v[24 * xc : 24 * xc + 24], shift, 0) for xc in range(XC)], axis=0
        )

    field = scale * rhs
    for _ in range(CSWEEPS - 1):
        total = rhs + w0 * up_x(field) + down_x(w0 * field)
        total = total + wy * by_plane(field, 23) + by_plane(wy * field, 1)
        total = total + wz * pltpu.roll(field, LANES - 4, 1) + pltpu.roll(wz * field, 4, 1)
        field = KEEP * field + scale * total
    scr[...] = field
    for xc in range(XC):
        c[8 * xc : 8 * xc + 8, :] = field[24 * xc + 8 : 24 * xc + 16]
    cyb[...] = pick(even, scr[pl.ds(7, 8, stride=24), :], scr[pl.ds(16, 8, stride=24), :])
    sa[...] = pick(even, scr[pl.ds(15, 8, stride=24), :], scr[pl.ds(8, 8, stride=24), :])
    low, high = field[8:16], field[24 * 7 + 8 : 24 * 7 + 16]
    sc[...] = pick(place.even[1], high, low)
    sd[...] = pick(place.even[1], low, high)


def first_coarse_kernel(ma, qa, qb, sb, gy, c, cyb, sa, sc, sd, wide, scr, two):
    place = Place()
    packed = joined(
        place, ma[CROWS : 2 * CROWS, :], qa[CROWS : 2 * CROWS, :], qb[CROWS + BS :, :]
    )
    ones = group_matrix()
    slot = lane_ids(3 * CROWS) % 4
    weights = [group_sum(jnp.where(slot == j, packed, 0.0), ones) for j in range(4)]
    for j in range(4):
        wide[3 * CROWS * j : 3 * CROWS * (j + 1), :] = weights[j]
    coarse_solve(place, ma, qa, qb, sb, gy, weights, c, cyb, sa, sc, sd, scr, two)


def later_coarse_kernel(ma, qa, qb, sb, gy, wide, c, cyb, sa, sc, sd, scr, two):
    weights = [wide[3 * CROWS * j : 3 * CROWS * (j + 1), :] for j in range(4)]
    coarse_solve(Place(), ma, qa, qb, sb, gy, weights, c, cyb, sa, sc, sd, scr, two)


def spread_rows(scr, value):
    for j in range(4):
        scr[pl.ds(j, 8, stride=4), :] = value
    return scr[...]


def correct_kernel(src, c, f0, fy, fz, p, gy, qb, cc, cyb, p2, r, scr):
    def corrected(x):
        return p[plane(x), :] + tiled(cc[8 * (x // 4) : 8 * (x // 4) + 8, :])

    t0, here = ZERO(), corrected(0)
    for x in range(BS):
        at = plane(x)
        after = corrected(min(x + 1, BS - 1))
        p2[at, :] = here
        r[at, :], t0 = residual_plane(src, c, f0, fy, fz, at, t0, here, after)
        here = after
    halo = qb[CROWS : CROWS + BS, :] + spread_rows(scr, cyb[...])
    ylo, yhi = low_high(Place(), 0, ZERO(), halo)
    add_faces_y(r, gy[0:BS, :] * ylo, gy[BS : 2 * BS, :] * yhi)


def residual_kernel(src, c, f0, fy, fz, p, r):
    t0, here = ZERO(), p[0:BS, :]
    for x in range(BS):
        at = plane(x)
        after = p[after_plane(x), :]
        r[at, :], t0 = residual_plane(src, c, f0, fy, fz, at, t0, here, after)
        here = after


def add_all(place, gx, gy, ra, rb, rc, rd, ref):
    xlo, xhi = low_high(place, 1, rc, rd)
    add_faces_x(ref, gx[0:BS, :] * xlo, gx[BS : 2 * BS, :] * xhi)
    ylo, yhi = low_high(place, 0, ra, rb)
    add_faces_y(ref, gy[0:BS, :] * ylo, gy[BS : 2 * BS, :] * yhi)


def finish_smooth(place, limit, r, f0, fy, fzs, d, p, p_out, sends, e):
    def finish(at, value):
        p_out[at, :] = p[at, :] + value

    relax(limit, r, e, f0, fy, fzs, d, finish)
    send_faces(place, p_out, *sends)


def smooth_corrected_kernel(
    levels, level_sweeps, ri, f0, fy, fzs, d, p, gx, gy, ra, rc, rd, ka, kc, kd,
    r, p_out, sa, sb, sc, sd, e, scr,
):
    place = Place()
    near = ra[...] + spread_rows(scr, ka[...])
    add_all(place, gx, gy, near, ZERO(), rc[...] + tiled(kc[...]), rd[...] + tiled(kd[...]), r)
    limit = sweep_limits(levels, level_sweeps)
    finish_smooth(place, limit, r, f0, fy, fzs, d, p, p_out, (sa, sb, sc, sd), e)


def smooth_kernel(
    levels, level_sweeps, ri, f0, fy, fzs, d, p, gx, gy, ra, rb, rc, rd,
    r, p_out, sa, sb, sc, sd, e,
):
    place = Place()
    add_all(place, gx, gy, ra[...], rb[...], rc[...], rd[...], r)
    limit = sweep_limits(levels, level_sweeps)
    finish_smooth(place, limit, r, f0, fy, fzs, d, p, p_out, (sa, sb, sc, sd), e)


def plane_to_blocks(v, x, out, base):
    lane = lane_ids(8)
    half = lane < 64
    even = (lane // BS) % 2 == 0
    v = [v[8 * k : 8 * k + 8] for k in range(4)]
    u = [None] * 4
    for k in range(2):
        low, high = v[k], v[k + 2]
        u[k] = jnp.where(half, low, pltpu.roll(high, 64, 1))
        u[k + 2] = jnp.where(half, pltpu.roll(low, 64, 1), high)
    for b in (0, 2):
        low, high = u[b], u[b + 1]
        first = jnp.where(even, low, pltpu.roll(high, BS, 1))
        second = jnp.where(even, pltpu.roll(low, LANES - BS, 1), high)
        at = base + b * STEP + x * 8
        out[at : at + 8, :] = first
        out[at + STEP : at + STEP + 8, :] = second


def last_residual_kernel(src, c, f0, fy, fz, p, r, blocks, *, count):
    t0, here = ZERO(), p[0:BS, :]
    for x in range(BS):
        at = plane(x)
        after = p[after_plane(x), :]
        r[at, :], t0 = residual_plane(src, c, f0, fy, fz, at, t0, here, after)
        plane_to_blocks(here, x, blocks, count * STEP)
        here = after


def final_kernel(ri, gx, gy, ra, rb, rc, rd, pblocks, r, blocks, sa, sb, *, count):
    place = Place()
    even = place.even[0]
    add_all(place, gx, gy, ra[...], rb[...], rc[...], rd[...], r)

    for x in range(BS):
        plane_to_blocks(r[plane(x), :], x, blocks, count * STEP)
    for n, ref in enumerate((pblocks, blocks)):
        for b in range(count):
            for t in range(0, 256, 32):
                low = (count + b) * STEP + t
                high = (BLK + b) * STEP + t
                low, high = ref[low : low + 32, :], ref[high : high + 32, :]
                at = slice((n * count + b) * 256 + t, (n * count + b) * 256 + t + 32)
                sa[at, :] = pick(even, high, low)
                sb[at, :] = pick(even, low, high)


def place_kernel(owned, in_p, in_r, ra, rb, out_p, out_r, seq_p, seq_r, *, count):
    place = Place()
    even = place.even[0]
    start, held = owned[0], owned[1]
    base = jnp.clip(start - place.device * BLK + count, 0, 2 * count) * STEP
    valid = row_ids(8) < held
    for n, (seq, out) in enumerate(((seq_p, out_p), (seq_r, out_r))):
        for b in range(count):
            for t in range(0, 256, 32):
                at = slice((n * count + b) * 256 + t, (n * count + b) * 256 + t + 32)
                low, high = b * STEP + t, (count + BLK + b) * STEP + t
                seq[low : low + 32, :] = pick(even, rb[at, :], ra[at, :])
                seq[high : high + 32, :] = pick(even, ra[at, :], rb[at, :])
        for t in range(256):
            rows = seq[pl.ds(base + t, 8, stride=STEP), :]
            out[t, :, :] = jnp.where(valid, rows, 0.0)[0:CAP]


BOTH = ("region", "member")


def swap_near(value):
    return lax.ppermute(value, "member", [(i, i ^ 1) for i in range(lax.axis_size("member"))])


def swap_far(value):
    regions, members = lax.axis_size("region"), lax.axis_size("member")
    pairs = []
    for r in range(regions):
        for m in range(members):
            other = m + 1 if m % 2 else m - 1
            inside = 0 <= other < members
            target = r * members + other if inside else (r ^ 1) * members + m
            pairs.append((r * members + m, target))
    return lax.ppermute(value, BOTH, pairs)


def swap_regions(inner, outer):
    regions, members = lax.axis_size("region"), lax.axis_size("member")
    pairs = []
    for r in range(regions):
        other = r + 1 if r % 2 else r - 1
        inside = 0 <= other < regions
        for m in range(members):
            target = other * members + m if inside else r * members + (m ^ 1)
            pairs.append((r * members + m, target))
    inner = lax.ppermute(inner, "region", [(i, i ^ 1) for i in range(regions)])
    return inner, lax.ppermute(outer, BOTH, pairs)


def swap_blocks(first, second):
    count = lax.axis_size(BOTH)
    inner = [(i, i ^ 1) for i in range(count)]
    outer = [(i, (i + 1) % count if i % 2 else (i - 1) % count) for i in range(count)]
    return lax.ppermute(first, BOTH, inner), lax.ppermute(second, BOTH, outer)


def swap_faces(sa, sb, sc, sd):
    return (swap_near(sa), swap_far(sb), *swap_regions(sc, sd))


FULL, TWO, CFIELD = (ROWS, LANES), (2 * BS, LANES), (CROWS, LANES)
FACE, CFACE = (BS, LANES), (8, LANES)


def set_up(new_owner, src, inv):
    outs = [jax.ShapeDtypeStruct((2,), jnp.int32), jax.ShapeDtypeStruct((1,), jnp.int32)] + [
        jax.ShapeDtypeStruct(s, F32) for s in [FULL] * 6 + [TWO] * 2 + [CFIELD] * 2
    ]
    vm, sm = pl.BlockSpec(memory_space=pltpu.VMEM), pl.BlockSpec(memory_space=pltpu.SMEM)
    return pl.pallas_call(
        weights_kernel,
        out_shape=outs,
        in_specs=[vm] * 3,
        out_specs=[sm] * 2 + [vm] * 10,
        compiler_params=pltpu.CompilerParams(vmem_limit_bytes=48 << 20),
        cost_estimate=pl.CostEstimate(flops=4000000, bytes_accessed=6 << 20, transcendentals=0),
    )(new_owner.reshape(-1, min(LANES, new_owner.size)), src, inv)


def row_shape(count):
    return ((2 * count + 8) * STEP, LANES)


def place_blocks(count, owned, *arrays):
    slots, row = (256, CAP, LANES), row_shape(count)
    body = functools.partial(place_kernel, count=count)
    outs = call(body, [slots, slots, row, row], arrays, [owned], aliases={0: 2, 1: 3})
    return tuple(o.transpose(1, 0, 2).reshape(CAP, 256 * LANES) for o in outs[:2])


def on_device(source, inverse_density, block_level, level_sweeps, new_owner):
    region, member = lax.axis_index("region"), lax.axis_index("member")
    levels = (block_level, level_sweeps)
    edge_y = jnp.where(member % 2 == 0, BS - 1, 0)
    edge_x = jnp.where(region % 2 == 0, BS - 1, 0)

    def face(direction, x, y):
        extent = (1, BS, 1, LANES) if direction == 1 else (1, 1, BS, LANES)
        return lax.dynamic_slice(inverse_density, (direction, x, y, 0), extent).reshape(FACE)

    faces = (
        face(1, 0, edge_y), face(1, 0, BS - 1 - edge_y), face(0, edge_x, 0), face(0, BS - 1 - edge_x, 0)
    )
    halos = swap_faces(*lax.optimization_barrier(faces))
    owned, most, src, f0, fy, fz, fzs, c0, fx, fyf, czu, czd = set_up(
        new_owner, source.reshape(ROWS, LANES), inverse_density.reshape(3 * ROWS, LANES)
    )
    c, d, gx, gy, p, *sends = call(
        first_kernel,
        [FULL, FULL, TWO, TWO, FULL] + [FACE] * 4,
        [src, f0, fy, fzs, c0, fx, fyf, *halos],
        levels,
        [vmem(*FULL)],
        {4: 0},
    )
    fine = [src, c, f0, fy, fz]
    wide = None
    for cycle in range(CYCLES):
        if cycle > 0:
            halos = swap_faces(*sends)
            (ri,) = call(residual_kernel, [FULL], [*fine, p])
            _, p, *sends = call(
                smooth_kernel,
                [FULL, FULL] + [FACE] * 4,
                [ri, f0, fy, fzs, d, p, gx, gy, *halos],
                levels,
                [vmem(*FULL)],
                {0: 0},
            )
        sa, sb, sc, sd = sends
        ra = swap_near(sa)
        rc, rd = swap_regions(sc, sd)
        (qi,) = call(coarse_rhs_kernel, [CFIELD], [*fine, p], scratch=[vmem(*CFIELD)])
        packed, rows = [], CROWS
        if wide is None:
            packed = call(
                coarse_weights_kernel,
                [CFIELD],
                [f0, fy, gx, gy, czu, czd],
                scratch=[vmem(*CFIELD)] * 2,
            )
            rows = 2 * CROWS
        ma, mb = call(
            coarse_faces_kernel,
            [(rows, LANES), (rows + BS, LANES)],
            [qi, gx, gy, ra, rc, rd, sb, *packed],
            scratch=[vmem(*FACE)],
        )
        qa, qb = swap_near(ma), swap_far(mb)
        outs = [CFIELD] + [CFACE] * 4
        arrays = [ma, qa, qb, sb, gy]
        scratch = [vmem(3 * CROWS, LANES), vmem(*TWO)]
        if wide is None:
            cc, cyb, ta, tc, td, wide = call(
                first_coarse_kernel, outs + [(12 * CROWS, LANES)], arrays, scratch=scratch
            )
        else:
            cc, cyb, ta, tc, td = call(later_coarse_kernel, outs, [*arrays, wide], scratch=scratch)
        ka = swap_near(ta)
        kc, kd = swap_regions(tc, td)
        p, ri = call(
            correct_kernel, [FULL, FULL], [*fine, p, gy, qb, cc, cyb], scratch=[vmem(*FACE)]
        )
        _, p, *sends = call(
            smooth_corrected_kernel,
            [FULL, FULL] + [FACE] * 4,
            [ri, f0, fy, fzs, d, p, gx, gy, ra, rc, rd, ka, kc, kd],
            levels,
            [vmem(*FULL), vmem(*FACE)],
            {0: 0},
        )

    def tail(count, p, sends, fine, gx, gy, owned):
        halos = swap_faces(*sends)
        row = row_shape(count)
        body = functools.partial(last_residual_kernel, count=count)
        ri, blocks_p = call(body, [FULL, row], [*fine, p])
        part = (2 * count * 256, LANES)
        _, blocks_r, sa, sb = call(
            functools.partial(final_kernel, count=count),
            [FULL, row, part, part],
            [ri, gx, gy, *halos, blocks_p],
            aliases={0: 0},
        )
        return place_blocks(count, owned, blocks_p, blocks_r, *swap_blocks(sa, sb))

    return lax.cond(
        most.reshape(()) <= 1,
        functools.partial(tail, 1),
        functools.partial(tail, BLK),
        p, sends, fine, gx, gy, owned,
    )


def solution(mesh):
    placed = (
        P("region", "member", None),
        P(None, "region", "member", None),
        P(("region", "member")),
        P(),
        P(),
    )
    return jax.shard_map(
        on_device,
        mesh=mesh,
        in_specs=placed,
        out_specs=(P(("region", "member"), None), P(("region", "member"), None)),
        check_vma=False,
    )
```

```python
import functools

import jax
import jax.numpy as jnp
from jax import lax
from jax.experimental import pallas as pl
from jax.experimental.pallas import tpu as pltpu
from jax.sharding import PartitionSpec as P


BS = 32
BLK = 4
CSWEEPS = 8
CYCLES = 2
CAP = 6
SWEEP_MAX = 6
RELAX = 0.8
KEEP = 0.2
PART = 1.0 / 64.0
PIECES = 4
PIECE = 256 // PIECES
STEP = 264
LANES = 128
ROWS = BS * BS
XC = BS // 4
CROWS = XC * XC
ZERO = functools.partial(jnp.zeros, (BS, LANES), jnp.float32)
F32 = jnp.float32


def vmem(*shape):
    return pltpu.VMEM(shape, F32)


def call(body, out_rows, args, scalars=(), scratch=(), aliases=None, flops=2e6, mib=48):
    outs = [jax.ShapeDtypeStruct(s, F32) for s in out_rows]
    moved = sum(a.size * 4 for a in args) + sum(o.size * 4 for o in outs)
    return pl.pallas_call(
        body,
        out_shape=outs,
        in_specs=[pl.BlockSpec(memory_space=pltpu.SMEM)] * len(scalars)
        + [pl.BlockSpec(memory_space=pltpu.VMEM)] * len(args),
        out_specs=[pl.BlockSpec(memory_space=pltpu.VMEM)] * len(outs),
        scratch_shapes=list(scratch),
        input_output_aliases={len(scalars) + k: v for k, v in (aliases or {}).items()},
        compiler_params=pltpu.CompilerParams(vmem_limit_bytes=mib << 20),
        cost_estimate=pl.CostEstimate(flops=int(flops), bytes_accessed=int(moved), transcendentals=0),
    )(*scalars, *args)


class Place:
    def __init__(self):
        region, member = lax.axis_index("region"), lax.axis_index("member")
        self.device = region * lax.axis_size("member") + member
        self.even = (member % 2 == 0, region % 2 == 0)
        self.low = (member > 0, region > 0)
        self.high = (member < lax.axis_size("member") - 1, region < lax.axis_size("region") - 1)


def lane_ids(rows):
    return lax.broadcasted_iota(jnp.int32, (rows, LANES), 1)


def row_ids(rows):
    return lax.broadcasted_iota(jnp.int32, (rows, LANES), 0)


def next_y(v):
    return jnp.concatenate([v[8:32], pltpu.roll(v[0:8], 7, 0)], axis=0)


def prev_y(v):
    return jnp.concatenate([pltpu.roll(v[24:32], 1, 0), v[0:24]], axis=0)


def next_z(v):
    return pltpu.roll(v, LANES - 1, 1)


def prev_z(v):
    return pltpu.roll(v, 1, 1)


def fold(v):
    return v[0:8] + v[8:16] + v[16:24] + v[24:32]


def tiled(v):
    return jnp.concatenate([v, v, v, v], axis=0)


def plane(x):
    return slice(x * BS, (x + 1) * BS)


def after_plane(x):
    return plane(min(x + 1, BS - 1))


def pick(flag, yes, no):
    return jnp.where(jnp.full(yes.shape, flag.astype(jnp.int32), jnp.int32) == 1, yes, no)


def low_high(place, axis, first, second):
    low = pick(place.even[axis], second, first) * place.low[axis].astype(F32)
    high = pick(place.even[axis], first, second) * place.high[axis].astype(F32)
    return low, high


def group_matrix():
    return jnp.where(
        row_ids(LANES) // 4 == lane_ids(LANES) // 4, jnp.float32(1.0), jnp.float32(0.0)
    )


def group_sum(v, ones):
    return lax.dot_general(
        v, ones, (((1,), (0,)), ((), ())), precision=lax.Precision.HIGHEST, preferred_element_type=F32
    )


def by_fours(ref, base):
    total = ref[pl.ds(base, 8, stride=4), :]
    for j in range(1, 4):
        total = total + ref[pl.ds(base + j, 8, stride=4), :]
    return total


def weights_kernel(new_owner, src, inv, owned, most, src_t, f0, fy, fz, fzs, c0, fx, fyf, czu, czd):
    row, lane = row_ids(BS), lane_ids(BS)

    def load(ref, x, offset):
        return jnp.concatenate(
            [ref[pl.ds(offset + x * BS + k, 8, stride=4), :] for k in range(4)], axis=0
        )

    before, here = ZERO(), load(inv, 0, 0)
    for xc in range(XC):
        total_up = jnp.zeros((8, LANES), F32)
        total_down = jnp.zeros((8, LANES), F32)
        for j in range(4):
            x = xc * 4 + j
            src_t[plane(x), :] = load(src, x, 0)
            after = load(inv, x + 1, 0) if x < BS - 1 else ZERO()
            one = load(inv, x, ROWS)
            two = load(inv, x, 2 * ROWS)
            one_n = jnp.where(row == BS - 1, 0.0, next_y(one))
            one_p = jnp.where(row == 0, 0.0, prev_y(one))
            two_n = jnp.where(lane == LANES - 1, 0.0, next_z(two))
            two_p = jnp.where(lane == 0, 0.0, prev_z(two))
            up0 = 0.5 * (here + after)
            upy = 0.5 * (one + one_n)
            upz = 0.5 * (two + two_n)
            downz = 0.5 * (two + two_p)
            f0[plane(x), :] = up0 if x < BS - 1 else ZERO()
            fy[plane(x), :] = jnp.where(row == BS - 1, 0.0, upy)
            fz[plane(x), :] = jnp.where(lane == LANES - 1, 0.0, upz)
            fzs[plane(x), :] = jnp.where(lane % BS == BS - 1, 0.0, upz)
            c0[plane(x), :] = up0 + upy + upz + 0.5 * (here + before) + 0.5 * (one + one_p) + downz
            total_up = total_up + fold(upz)
            total_down = total_down + fold(downz)
            before, here = here, after
        czu[8 * xc : 8 * xc + 8, :] = total_up
        czd[8 * xc : 8 * xc + 8, :] = total_down
    fx[0:BS, :] = load(inv, 0, 0)
    fx[BS : 2 * BS, :] = load(inv, BS - 1, 0)
    for g in range(4):
        fyf[8 * g : 8 * g + 8, :] = inv[pl.ds(ROWS + 256 * g, 8, stride=BS), :]
        fyf[BS + 8 * g : BS + 8 * g + 8, :] = inv[pl.ds(ROWS + 256 * g + 31, 8, stride=BS), :]
    device = Place().device
    owner = new_owner[...]
    block = lax.broadcasted_iota(jnp.int32, owner.shape, 0) * owner.shape[1]
    block = block + lax.broadcasted_iota(jnp.int32, owner.shape, 1)
    home, place = block // BLK, block % BLK
    leaving = jnp.where(owner > home, BLK - place, jnp.where(owner < home, place + 1, 0))
    owned[0] = jnp.sum((owner < device).astype(F32)).astype(jnp.int32)
    owned[1] = jnp.sum((owner == device).astype(F32)).astype(jnp.int32)
    most[0] = jnp.max(leaving.astype(F32)).astype(jnp.int32)


def add_faces_y(ref, low, high):
    for g in range(4):
        at = pl.ds(256 * g, 8, stride=BS)
        ref[at, :] = ref[at, :] + low[8 * g : 8 * g + 8]
        at = pl.ds(256 * g + 31, 8, stride=BS)
        ref[at, :] = ref[at, :] + high[8 * g : 8 * g + 8]


def add_faces_x(ref, low, high):
    ref[0:BS, :] = ref[0:BS, :] + low
    ref[ROWS - BS : ROWS, :] = ref[ROWS - BS : ROWS, :] + high


def send_faces(place, p, sa, sb, sc, sd):
    even = place.even[0]
    for g in range(4):
        low = p[pl.ds(256 * g, 8, stride=BS), :]
        high = p[pl.ds(256 * g + 31, 8, stride=BS), :]
        sa[8 * g : 8 * g + 8, :] = pick(even, high, low)
        sb[8 * g : 8 * g + 8, :] = pick(even, low, high)
    low = p[0:BS, :]
    high = p[ROWS - BS : ROWS, :]
    sc[...] = pick(place.even[1], high, low)
    sd[...] = pick(place.even[1], low, high)


def sweep_limits(levels, level_sweeps):
    block = lane_ids(BS) // BS
    limit = jnp.zeros((BS, LANES), jnp.int32)
    for b in range(BLK):
        limit = jnp.where(block == b, level_sweeps[levels[b]], limit)
    return limit


def relax(limit, r, e, f0, fy, fzs, d, finish):
    def sweep(i, load, store):
        active = limit > i

        t0, here = ZERO(), load(plane(0))
        for x in range(BS):
            at = plane(x)
            after = load(after_plane(x))
            w0, wy, wz = f0[at, :], fy[at, :], fzs[at, :]
            t1 = w0 * here
            total = r[at, :] + t0 + w0 * after
            total = total + wy * next_y(here) + prev_y(wy * here)
            total = total + wz * next_z(here) + prev_z(wz * here)
            store(at, jnp.where(active, KEEP * here + d[at, :] * total, here))
            t0, here = t1, after

    def first(at):
        return d[at, :] * r[at, :]

    def held(at):
        return e[at, :]

    def keep(at, value):
        e[at, :] = value

    sweep(1, first, keep)
    for i in range(2, SWEEP_MAX - 1):
        sweep(i, held, keep)
    sweep(SWEEP_MAX - 1, held, finish)


def first_kernel(
    levels, level_sweeps, src, f0, fy, fzs, c0, fx, fyf, ra, rb, rc, rd,
    c, d, gx, gy, p, sa, sb, sc, sd, e,
):
    def natural(ref):
        return jnp.concatenate([ref[pl.ds(k, 8, stride=4), :] for k in range(4)], axis=0)

    place = Place()
    xlo, xhi = low_high(place, 1, natural(rc), natural(rd))
    ylo, yhi = low_high(place, 0, ra[...], rb[...])
    gx[0:BS, :] = 0.5 * (fx[0:BS, :] + xlo)
    gx[BS : 2 * BS, :] = 0.5 * (fx[BS : 2 * BS, :] + xhi)
    gy[0:BS, :] = 0.5 * (fyf[0:BS, :] + ylo)
    gy[BS : 2 * BS, :] = 0.5 * (fyf[BS : 2 * BS, :] + yhi)
    add_faces_x(c, 0.5 * xlo, 0.5 * xhi)
    add_faces_y(c, 0.5 * ylo, 0.5 * yhi)

    for x in range(BS):
        at = plane(x)
        d[at, :] = RELAX / c[at, :]

    def finish(at, value):
        p[at, :] = value

    relax(sweep_limits(levels, level_sweeps), src, e, f0, fy, fzs, d, finish)
    send_faces(place, p, sa, sb, sc, sd)


def residual_plane(src, c, f0, fy, fz, at, t0, here, after):
    w0, wy, wz = f0[at, :], fy[at, :], fz[at, :]
    total = src[at, :] - c[at, :] * here + t0 + w0 * after
    total = total + wy * next_y(here) + prev_y(wy * here)
    total = total + wz * next_z(here) + prev_z(wz * here)
    return total, w0 * here


def coarse_rhs_kernel(src, c, f0, fy, fz, p, q, scr):
    t0, here = ZERO(), p[0:BS, :]
    for xc in range(XC):
        total = jnp.zeros((8, LANES), F32)
        for j in range(4):
            x = xc * 4 + j
            after = p[after_plane(x), :]
            r, t0 = residual_plane(src, c, f0, fy, fz, plane(x), t0, here, after)
            total = total + fold(r)
            here = after
        scr[8 * xc : 8 * xc + 8, :] = total
    q[...] = group_sum(scr[...], group_matrix()) * PART


def coarse_weights_kernel(f0, fy, gx, gy, czu, czd, packed, scr, cy):
    ones = group_matrix()
    lane = lane_ids(CROWS)
    row = row_ids(CROWS)
    for xc in range(XC):
        scr[8 * xc : 8 * xc + 8, :] = fold(f0[(4 * xc + 3) * BS : (4 * xc + 4) * BS, :])
        total = fy[4 * xc * BS + 24 : 4 * xc * BS + 32, :]
        for j in range(1, 4):
            at = (4 * xc + j) * BS
            total = total + fy[at + 24 : at + 32, :]
        cy[8 * xc : 8 * xc + 8, :] = total
    c0 = group_sum(scr[...], ones) * PART
    cy[pl.ds(7, 8, stride=8), :] = by_fours(gy, BS)
    up_y = group_sum(cy[...], ones) * PART
    gxlo = group_sum(fold(gx[0:BS, :]), ones) * PART
    gxhi = group_sum(fold(gx[BS : 2 * BS, :]), ones) * PART
    up_z = group_sum(jnp.where(lane % 4 == 3, czu[...], 0.0), ones) * PART
    down_z = group_sum(jnp.where(lane % 4 == 0, czd[...], 0.0), ones) * PART
    up_0 = jnp.concatenate([c0[0 : CROWS - 8], gxhi], axis=0)
    down_0 = jnp.concatenate([gxlo, c0[0 : CROWS - 8]], axis=0)
    cy[...] = jnp.concatenate(
        [pltpu.roll(up_y[8 * xc : 8 * xc + 8], 1, 0) for xc in range(XC)], axis=0
    )
    cy[pl.ds(0, 8, stride=8), :] = group_sum(by_fours(gy, 0), ones) * PART
    scale = RELAX / (up_0 + up_y + up_z + down_0 + cy[...] + down_z)
    couple_y = jnp.where(row % 8 == 7, up_y * Place().high[0].astype(F32), up_y)
    couple_z = jnp.where(lane >= LANES - 4, 0.0, up_z)
    slot = lane % 4
    packed[...] = jnp.where(
        slot == 0, c0, jnp.where(slot == 1, couple_y, jnp.where(slot == 2, couple_z, scale))
    )


def coarse_faces_kernel(qi, gx, gy, ra, rc, rd, sb, *rest):
    packed, (ma, mb, scr) = rest[:-3], rest[-3:]
    place = Place()
    xlo, xhi = low_high(place, 1, rc[...], rd[...])
    even = place.even[0]
    own = jnp.where(jnp.full(ra.shape, even.astype(jnp.int32)) == 1, gy[BS : 2 * BS, :], gy[0:BS, :])
    scr[...] = own * ra[...]
    faces = jnp.concatenate(
        [fold(gx[0:BS, :] * xlo), fold(gx[BS : 2 * BS, :] * xhi), by_fours(scr, 0)], axis=0
    )
    faces = group_sum(faces, group_matrix()) * PART
    ma[0:CROWS, :] = qi[...]
    ma[0:8, :] = ma[0:8, :] + faces[0:8]
    ma[CROWS - 8 : CROWS, :] = ma[CROWS - 8 : CROWS, :] + faces[8:16]
    nothing = jnp.zeros((8, LANES), F32)
    at = pl.ds(0, 8, stride=8)
    ma[at, :] = ma[at, :] + pick(even, nothing, faces[16:24])
    at = pl.ds(7, 8, stride=8)
    ma[at, :] = ma[at, :] + pick(even, faces[16:24], nothing)
    mb[0:CROWS, :] = ma[0:CROWS, :]
    mb[CROWS : CROWS + BS, :] = sb[...]
    for w in packed:
        ma[CROWS : 2 * CROWS, :] = w[...]
        mb[CROWS + BS : 2 * CROWS + BS, :] = w[...]


def joined(place, own, first, second):
    low, high = low_high(place, 0, first, second)
    parts = []
    for xc in range(XC):
        at = slice(8 * xc, 8 * xc + 8)
        parts += [low[at], own[at], high[at]]
    return jnp.concatenate(parts, axis=0)


def coarse_solve(place, ma, qa, qb, sb, gy, weights, c, cyb, sa, sc, sd, scr, two):
    even = place.even[0]
    w0, wy, wz, scale = weights
    scr[...] = joined(place, ma[0:CROWS, :], qa[0:CROWS, :], qb[0:CROWS, :])
    side = pick(even, gy[0:BS, :], gy[BS : 2 * BS, :])
    there = jnp.where(even, place.low[0].astype(F32), place.high[0].astype(F32))
    two[0:BS, :] = side * qb[CROWS : CROWS + BS, :] * there
    two[BS : 2 * BS, :] = side * sb[...]
    faces = jnp.concatenate([by_fours(two, 0), by_fours(two, BS)], axis=0)
    faces = group_sum(faces, group_matrix()) * PART
    mine, theirs = faces[0:8], faces[8:16]
    nothing = jnp.zeros((8, LANES), F32)
    for row, value in (
        (8, pick(even, mine, nothing)),
        (7, pick(even, theirs, nothing)),
        (15, pick(even, nothing, mine)),
        (16, pick(even, nothing, theirs)),
    ):
        at = pl.ds(row, 8, stride=24)
        scr[at, :] = scr[at, :] + value
    rhs = scr[...]

    def up_x(v):
        return jnp.concatenate([v[24:], v[:24]], axis=0)

    def down_x(v):
        return jnp.concatenate([v[-24:], v[:-24]], axis=0)

    def by_plane(v, shift):
        return jnp.concatenate(
            [pltpu.roll(v[24 * xc : 24 * xc + 24], shift, 0) for xc in range(XC)], axis=0
        )

    field = scale * rhs
    for _ in range(CSWEEPS - 1):
        total = rhs + w0 * up_x(field) + down_x(w0 * field)
        total = total + wy * by_plane(field, 23) + by_plane(wy * field, 1)
        total = total + wz * pltpu.roll(field, LANES - 4, 1) + pltpu.roll(wz * field, 4, 1)
        field = KEEP * field + scale * total
    scr[...] = field
    for xc in range(XC):
        c[8 * xc : 8 * xc + 8, :] = field[24 * xc + 8 : 24 * xc + 16]
    cyb[...] = pick(even, scr[pl.ds(7, 8, stride=24), :], scr[pl.ds(16, 8, stride=24), :])
    sa[...] = pick(even, scr[pl.ds(15, 8, stride=24), :], scr[pl.ds(8, 8, stride=24), :])
    low, high = field[8:16], field[24 * 7 + 8 : 24 * 7 + 16]
    sc[...] = pick(place.even[1], high, low)
    sd[...] = pick(place.even[1], low, high)


def first_coarse_kernel(ma, qa, qb, sb, gy, c, cyb, sa, sc, sd, wide, scr, two):
    place = Place()
    packed = joined(
        place, ma[CROWS : 2 * CROWS, :], qa[CROWS : 2 * CROWS, :], qb[CROWS + BS :, :]
    )
    ones = group_matrix()
    slot = lane_ids(3 * CROWS) % 4
    weights = [group_sum(jnp.where(slot == j, packed, 0.0), ones) for j in range(4)]
    for j in range(4):
        wide[3 * CROWS * j : 3 * CROWS * (j + 1), :] = weights[j]
    coarse_solve(place, ma, qa, qb, sb, gy, weights, c, cyb, sa, sc, sd, scr, two)


def later_coarse_kernel(ma, qa, qb, sb, gy, wide, c, cyb, sa, sc, sd, scr, two):
    weights = [wide[3 * CROWS * j : 3 * CROWS * (j + 1), :] for j in range(4)]
    coarse_solve(Place(), ma, qa, qb, sb, gy, weights, c, cyb, sa, sc, sd, scr, two)


def spread_rows(scr, value):
    for j in range(4):
        scr[pl.ds(j, 8, stride=4), :] = value
    return scr[...]


def correct_kernel(src, c, f0, fy, fz, p, gy, qb, cc, cyb, p2, r, scr):
    def corrected(x):
        return p[plane(x), :] + tiled(cc[8 * (x // 4) : 8 * (x // 4) + 8, :])

    t0, here = ZERO(), corrected(0)
    for x in range(BS):
        at = plane(x)
        after = corrected(min(x + 1, BS - 1))
        p2[at, :] = here
        r[at, :], t0 = residual_plane(src, c, f0, fy, fz, at, t0, here, after)
        here = after
    halo = qb[CROWS : CROWS + BS, :] + spread_rows(scr, cyb[...])
    ylo, yhi = low_high(Place(), 0, ZERO(), halo)
    add_faces_y(r, gy[0:BS, :] * ylo, gy[BS : 2 * BS, :] * yhi)


def residual_kernel(src, c, f0, fy, fz, p, r):
    t0, here = ZERO(), p[0:BS, :]
    for x in range(BS):
        at = plane(x)
        after = p[after_plane(x), :]
        r[at, :], t0 = residual_plane(src, c, f0, fy, fz, at, t0, here, after)
        here = after


def add_all(place, gx, gy, ra, rb, rc, rd, ref):
    xlo, xhi = low_high(place, 1, rc, rd)
    add_faces_x(ref, gx[0:BS, :] * xlo, gx[BS : 2 * BS, :] * xhi)
    ylo, yhi = low_high(place, 0, ra, rb)
    add_faces_y(ref, gy[0:BS, :] * ylo, gy[BS : 2 * BS, :] * yhi)


def finish_smooth(place, limit, r, f0, fy, fzs, d, p, p_out, sends, e):
    def finish(at, value):
        p_out[at, :] = p[at, :] + value

    relax(limit, r, e, f0, fy, fzs, d, finish)
    send_faces(place, p_out, *sends)


def smooth_corrected_kernel(
    levels, level_sweeps, ri, f0, fy, fzs, d, p, gx, gy, ra, rc, rd, ka, kc, kd,
    r, p_out, sa, sb, sc, sd, e, scr,
):
    place = Place()
    near = ra[...] + spread_rows(scr, ka[...])
    add_all(place, gx, gy, near, ZERO(), rc[...] + tiled(kc[...]), rd[...] + tiled(kd[...]), r)
    limit = sweep_limits(levels, level_sweeps)
    finish_smooth(place, limit, r, f0, fy, fzs, d, p, p_out, (sa, sb, sc, sd), e)


def smooth_kernel(
    levels, level_sweeps, ri, f0, fy, fzs, d, p, gx, gy, ra, rb, rc, rd,
    r, p_out, sa, sb, sc, sd, e,
):
    place = Place()
    add_all(place, gx, gy, ra[...], rb[...], rc[...], rd[...], r)
    limit = sweep_limits(levels, level_sweeps)
    finish_smooth(place, limit, r, f0, fy, fzs, d, p, p_out, (sa, sb, sc, sd), e)


def plane_to_blocks(v, x, out, base):
    lane = lane_ids(8)
    half = lane < 64
    even = (lane // BS) % 2 == 0
    v = [v[8 * k : 8 * k + 8] for k in range(4)]
    u = [None] * 4
    for k in range(2):
        low, high = v[k], v[k + 2]
        u[k] = jnp.where(half, low, pltpu.roll(high, 64, 1))
        u[k + 2] = jnp.where(half, pltpu.roll(low, 64, 1), high)
    for b in (0, 2):
        low, high = u[b], u[b + 1]
        first = jnp.where(even, low, pltpu.roll(high, BS, 1))
        second = jnp.where(even, pltpu.roll(low, LANES - BS, 1), high)
        at = base + b * STEP + x * 8
        out[at : at + 8, :] = first
        out[at + STEP : at + STEP + 8, :] = second


def last_residual_kernel(src, c, f0, fy, fz, p, r, blocks, *, count):
    t0, here = ZERO(), p[0:BS, :]
    for x in range(BS):
        at = plane(x)
        after = p[after_plane(x), :]
        r[at, :], t0 = residual_plane(src, c, f0, fy, fz, at, t0, here, after)
        plane_to_blocks(here, x, blocks, count * STEP)
        here = after


def final_kernel(ri, gx, gy, ra, rb, rc, rd, pblocks, r, blocks, sa, sb, *, count):
    place = Place()
    even = place.even[0]
    add_all(place, gx, gy, ra[...], rb[...], rc[...], rd[...], r)

    for x in range(BS):
        plane_to_blocks(r[plane(x), :], x, blocks, count * STEP)
    for n, ref in enumerate((pblocks, blocks)):
        for b in range(count):
            for t in range(0, 256, 32):
                low = (count + b) * STEP + t
                high = (BLK + b) * STEP + t
                low, high = ref[low : low + 32, :], ref[high : high + 32, :]
                at = slice((n * count + b) * 256 + t, (n * count + b) * 256 + t + 32)
                sa[at, :] = pick(even, high, low)
                sb[at, :] = pick(even, low, high)


def place_kernel(owned, in_p, in_r, ra, rb, out_p, out_r, seq_p, seq_r, held_p, held_r, sems, *, count):
    place = Place()
    even = place.even[0]
    start, held = owned[0], owned[1]
    base = jnp.clip(start - place.device * BLK + count, 0, 2 * count) * STEP
    valid = row_ids(8) < held
    copies = []
    fields = ((seq_p, held_p, out_p), (seq_r, held_r, out_r))
    for n, (seq, tiles, out) in enumerate(fields):
        for b in range(count):
            for t in range(0, 256, 32):
                at = slice((n * count + b) * 256 + t, (n * count + b) * 256 + t + 32)
                low, high = b * STEP + t, (count + BLK + b) * STEP + t
                seq[low : low + 32, :] = pick(even, rb[at, :], ra[at, :])
                seq[high : high + 32, :] = pick(even, ra[at, :], rb[at, :])
        for part in range(PIECES):
            for t in range(part * PIECE, (part + 1) * PIECE):
                rows = seq[pl.ds(base + t, 8, stride=STEP), :]
                tiles[t, :, :] = jnp.where(valid, rows, 0.0)[0:CAP]
            at = pl.ds(part * PIECE, PIECE)
            copy = pltpu.make_async_copy(tiles.at[at], out.at[at], sems.at[n, part])
            copy.start()
            copies.append(copy)
    for copy in copies:
        copy.wait()


BOTH = ("region", "member")


def swap_near(value):
    return lax.ppermute(value, "member", [(i, i ^ 1) for i in range(lax.axis_size("member"))])


def swap_far(value):
    regions, members = lax.axis_size("region"), lax.axis_size("member")
    pairs = []
    for r in range(regions):
        for m in range(members):
            other = m + 1 if m % 2 else m - 1
            inside = 0 <= other < members
            target = r * members + other if inside else (r ^ 1) * members + m
            pairs.append((r * members + m, target))
    return lax.ppermute(value, BOTH, pairs)


def swap_regions(inner, outer):
    regions, members = lax.axis_size("region"), lax.axis_size("member")
    pairs = []
    for r in range(regions):
        other = r + 1 if r % 2 else r - 1
        inside = 0 <= other < regions
        for m in range(members):
            target = other * members + m if inside else r * members + (m ^ 1)
            pairs.append((r * members + m, target))
    inner = lax.ppermute(inner, "region", [(i, i ^ 1) for i in range(regions)])
    return inner, lax.ppermute(outer, BOTH, pairs)


def swap_blocks(first, second):
    count = lax.axis_size(BOTH)
    inner = [(i, i ^ 1) for i in range(count)]
    outer = [(i, (i + 1) % count if i % 2 else (i - 1) % count) for i in range(count)]
    return lax.ppermute(first, BOTH, inner), lax.ppermute(second, BOTH, outer)


def swap_faces(sa, sb, sc, sd):
    return (swap_near(sa), swap_far(sb), *swap_regions(sc, sd))


FULL, TWO, CFIELD = (ROWS, LANES), (2 * BS, LANES), (CROWS, LANES)
FACE, CFACE = (BS, LANES), (8, LANES)


def set_up(new_owner, src, inv):
    outs = [jax.ShapeDtypeStruct((2,), jnp.int32), jax.ShapeDtypeStruct((1,), jnp.int32)] + [
        jax.ShapeDtypeStruct(s, F32) for s in [FULL] * 6 + [TWO] * 2 + [CFIELD] * 2
    ]
    vm, sm = pl.BlockSpec(memory_space=pltpu.VMEM), pl.BlockSpec(memory_space=pltpu.SMEM)
    return pl.pallas_call(
        weights_kernel,
        out_shape=outs,
        in_specs=[vm] * 3,
        out_specs=[sm] * 2 + [vm] * 10,
        compiler_params=pltpu.CompilerParams(vmem_limit_bytes=48 << 20),
        cost_estimate=pl.CostEstimate(flops=4000000, bytes_accessed=6 << 20, transcendentals=0),
    )(new_owner.reshape(-1, min(LANES, new_owner.size)), src, inv)


def row_shape(count):
    return ((2 * count + 8) * STEP, LANES)


def faces_kernel(inv, sa, sb, sc, sd, sems):
    place = Place()
    low, high = (0, BS - 1)

    def copies(first, second, axis):
        if axis == 0:
            pair = ((inv.at[1, :, first, :], sa), (inv.at[1, :, second, :], sb))
        else:
            pair = ((inv.at[0, first], sc), (inv.at[0, second], sd))
        return [
            pltpu.make_async_copy(source, to, sems.at[2 * axis + n])
            for n, (source, to) in enumerate(pair)
        ]

    for axis in range(2):

        @pl.when(place.even[axis])
        def _():
            for copy in copies(high, low, axis):
                copy.start()

        @pl.when(jnp.logical_not(place.even[axis]))
        def _():
            for copy in copies(low, high, axis):
                copy.start()

    for axis in range(2):
        for copy in copies(low, high, axis):
            copy.wait()


def density_faces(inverse_density):
    return pl.pallas_call(
        faces_kernel,
        out_shape=[jax.ShapeDtypeStruct(FACE, F32)] * 4,
        in_specs=[pl.BlockSpec(memory_space=pl.ANY)],
        out_specs=[pl.BlockSpec(memory_space=pltpu.VMEM)] * 4,
        scratch_shapes=[pltpu.SemaphoreType.DMA((4,))],
        cost_estimate=pl.CostEstimate(flops=2000000000, bytes_accessed=131072, transcendentals=0),
    )(inverse_density)


def place_blocks(count, owned, *arrays):
    slots, row = (256, CAP, LANES), row_shape(count)
    vm = pl.BlockSpec(memory_space=pltpu.VMEM)
    anywhere = pl.BlockSpec(memory_space=pl.ANY)
    outs = pl.pallas_call(
        functools.partial(place_kernel, count=count),
        out_shape=[jax.ShapeDtypeStruct(shape, F32) for shape in (slots, slots, row, row)],
        in_specs=[pl.BlockSpec(memory_space=pltpu.SMEM)] + [vm] * 4,
        out_specs=[anywhere] * 2 + [vm] * 2,
        scratch_shapes=[vmem(*slots), vmem(*slots), pltpu.SemaphoreType.DMA((2, PIECES))],
        input_output_aliases={1: 2, 2: 3},
        compiler_params=pltpu.CompilerParams(vmem_limit_bytes=48 << 20),
        cost_estimate=pl.CostEstimate(flops=2000000, bytes_accessed=6 << 20, transcendentals=0),
    )(owned, *arrays)
    return tuple(o.transpose(1, 0, 2).reshape(CAP, 256 * LANES) for o in outs[:2])


def on_device(source, inverse_density, block_level, level_sweeps, new_owner):
    levels = (block_level, level_sweeps)
    halos = swap_faces(*density_faces(inverse_density))
    owned, most, src, f0, fy, fz, fzs, c0, fx, fyf, czu, czd = set_up(
        new_owner, source.reshape(ROWS, LANES), inverse_density.reshape(3 * ROWS, LANES)
    )
    c, d, gx, gy, p, *sends = call(
        first_kernel,
        [FULL, FULL, TWO, TWO, FULL] + [FACE] * 4,
        [src, f0, fy, fzs, c0, fx, fyf, *halos],
        levels,
        [vmem(*FULL)],
        {4: 0},
    )
    fine = [src, c, f0, fy, fz]
    wide = None
    for cycle in range(CYCLES):
        if cycle > 0:
            halos = swap_faces(*sends)
            (ri,) = call(residual_kernel, [FULL], [*fine, p])
            _, p, *sends = call(
                smooth_kernel,
                [FULL, FULL] + [FACE] * 4,
                [ri, f0, fy, fzs, d, p, gx, gy, *halos],
                levels,
                [vmem(*FULL)],
                {0: 0},
            )
        sa, sb, sc, sd = sends
        ra = swap_near(sa)
        rc, rd = swap_regions(sc, sd)
        (qi,) = call(coarse_rhs_kernel, [CFIELD], [*fine, p], scratch=[vmem(*CFIELD)])
        packed, rows = [], CROWS
        if wide is None:
            packed = call(
                coarse_weights_kernel,
                [CFIELD],
                [f0, fy, gx, gy, czu, czd],
                scratch=[vmem(*CFIELD)] * 2,
            )
            rows = 2 * CROWS
        ma, mb = call(
            coarse_faces_kernel,
            [(rows, LANES), (rows + BS, LANES)],
            [qi, gx, gy, ra, rc, rd, sb, *packed],
            scratch=[vmem(*FACE)],
        )
        qa, qb = swap_near(ma), swap_far(mb)
        outs = [CFIELD] + [CFACE] * 4
        arrays = [ma, qa, qb, sb, gy]
        scratch = [vmem(3 * CROWS, LANES), vmem(*TWO)]
        if wide is None:
            cc, cyb, ta, tc, td, wide = call(
                first_coarse_kernel, outs + [(12 * CROWS, LANES)], arrays, scratch=scratch
            )
        else:
            cc, cyb, ta, tc, td = call(later_coarse_kernel, outs, [*arrays, wide], scratch=scratch)
        ka = swap_near(ta)
        kc, kd = swap_regions(tc, td)
        p, ri = call(
            correct_kernel, [FULL, FULL], [*fine, p, gy, qb, cc, cyb], scratch=[vmem(*FACE)]
        )
        _, p, *sends = call(
            smooth_corrected_kernel,
            [FULL, FULL] + [FACE] * 4,
            [ri, f0, fy, fzs, d, p, gx, gy, ra, rc, rd, ka, kc, kd],
            levels,
            [vmem(*FULL), vmem(*FACE)],
            {0: 0},
        )

    def tail(count, p, sends, fine, gx, gy, owned):
        halos = swap_faces(*sends)
        row = row_shape(count)
        body = functools.partial(last_residual_kernel, count=count)
        ri, blocks_p = call(body, [FULL, row], [*fine, p])
        part = (2 * count * 256, LANES)
        _, blocks_r, sa, sb = call(
            functools.partial(final_kernel, count=count),
            [FULL, row, part, part],
            [ri, gx, gy, *halos, blocks_p],
            aliases={0: 0},
        )
        return place_blocks(count, owned, blocks_p, blocks_r, *swap_blocks(sa, sb))

    return lax.cond(
        most.reshape(()) <= 1,
        functools.partial(tail, 1),
        functools.partial(tail, BLK),
        p, sends, fine, gx, gy, owned,
    )


def solution(mesh):
    placed = (
        P("region", "member", None),
        P(None, "region", "member", None),
        P(("region", "member")),
        P(),
        P(),
    )
    return jax.shard_map(
        on_device,
        mesh=mesh,
        in_specs=placed,
        out_specs=(P(("region", "member"), None), P(("region", "member"), None)),
        check_vma=False,
    )
```

```python
import functools

import jax
import jax.numpy as jnp
from jax import lax
from jax.experimental import pallas as pl
from jax.experimental.pallas import tpu as pltpu
from jax.sharding import PartitionSpec as P


BS = 32
BLK = 4
CSWEEPS = 8
CYCLES = 2
CAP = 6
SWEEP_MAX = 6
RELAX = 0.8
KEEP = 0.2
PART = 1.0 / 64.0
PIECES = 4
PIECE = 256 // PIECES
STEP = 264
LANES = 128
ROWS = BS * BS
XC = BS // 4
CROWS = XC * XC
ZERO = functools.partial(jnp.zeros, (BS, LANES), jnp.float32)
F32 = jnp.float32


def vmem(*shape):
    return pltpu.VMEM(shape, F32)


def call(body, out_rows, args, scalars=(), scratch=(), aliases=None, flops=2e6, mib=48):
    outs = [jax.ShapeDtypeStruct(s, F32) for s in out_rows]
    moved = sum(a.size * 4 for a in args) + sum(o.size * 4 for o in outs)
    return pl.pallas_call(
        body,
        out_shape=outs,
        in_specs=[pl.BlockSpec(memory_space=pltpu.SMEM)] * len(scalars)
        + [pl.BlockSpec(memory_space=pltpu.VMEM)] * len(args),
        out_specs=[pl.BlockSpec(memory_space=pltpu.VMEM)] * len(outs),
        scratch_shapes=list(scratch),
        input_output_aliases={len(scalars) + k: v for k, v in (aliases or {}).items()},
        compiler_params=pltpu.CompilerParams(vmem_limit_bytes=mib << 20),
        cost_estimate=pl.CostEstimate(flops=int(flops), bytes_accessed=int(moved), transcendentals=0),
    )(*scalars, *args)


class Place:
    def __init__(self):
        region, member = lax.axis_index("region"), lax.axis_index("member")
        self.device = region * lax.axis_size("member") + member
        self.even = (member % 2 == 0, region % 2 == 0)
        self.low = (member > 0, region > 0)
        self.high = (member < lax.axis_size("member") - 1, region < lax.axis_size("region") - 1)


def lane_ids(rows):
    return lax.broadcasted_iota(jnp.int32, (rows, LANES), 1)


def row_ids(rows):
    return lax.broadcasted_iota(jnp.int32, (rows, LANES), 0)


def next_y(v):
    return jnp.concatenate([v[8:32], pltpu.roll(v[0:8], 7, 0)], axis=0)


def prev_y(v):
    return jnp.concatenate([pltpu.roll(v[24:32], 1, 0), v[0:24]], axis=0)


def next_z(v):
    return pltpu.roll(v, LANES - 1, 1)


def prev_z(v):
    return pltpu.roll(v, 1, 1)


def fold(v):
    return v[0:8] + v[8:16] + v[16:24] + v[24:32]


def tiled(v):
    return jnp.concatenate([v, v, v, v], axis=0)


def plane(x):
    return slice(x * BS, (x + 1) * BS)


def after_plane(x):
    return plane(min(x + 1, BS - 1))


def pick(flag, yes, no):
    return jnp.where(jnp.full(yes.shape, flag.astype(jnp.int32), jnp.int32) == 1, yes, no)


def low_high(place, axis, first, second):
    low = pick(place.even[axis], second, first) * place.low[axis].astype(F32)
    high = pick(place.even[axis], first, second) * place.high[axis].astype(F32)
    return low, high


def group_matrix():
    return jnp.where(
        row_ids(LANES) // 4 == lane_ids(LANES) // 4, jnp.float32(1.0), jnp.float32(0.0)
    )


def group_sum(v, ones):
    return lax.dot_general(
        v, ones, (((1,), (0,)), ((), ())), precision=lax.Precision.HIGHEST, preferred_element_type=F32
    )


def by_fours(ref, base):
    total = ref[pl.ds(base, 8, stride=4), :]
    for j in range(1, 4):
        total = total + ref[pl.ds(base + j, 8, stride=4), :]
    return total


def weights_kernel(
    levels, level_sweeps, new_owner, src, inv,
    owned, most, src_t, f0, fy, fz, fzs, c0, fx, fyf, czu, czd, limit,
):
    row, lane = row_ids(BS), lane_ids(BS)

    def load(ref, x, offset):
        return jnp.concatenate(
            [ref[pl.ds(offset + x * BS + k, 8, stride=4), :] for k in range(4)], axis=0
        )

    before, here = ZERO(), load(inv, 0, 0)
    for xc in range(XC):
        total_up = jnp.zeros((8, LANES), F32)
        total_down = jnp.zeros((8, LANES), F32)
        for j in range(4):
            x = xc * 4 + j
            src_t[plane(x), :] = load(src, x, 0)
            after = load(inv, x + 1, 0) if x < BS - 1 else ZERO()
            one = load(inv, x, ROWS)
            two = load(inv, x, 2 * ROWS)
            one_n = jnp.where(row == BS - 1, 0.0, next_y(one))
            one_p = jnp.where(row == 0, 0.0, prev_y(one))
            two_n = jnp.where(lane == LANES - 1, 0.0, next_z(two))
            two_p = jnp.where(lane == 0, 0.0, prev_z(two))
            up0 = 0.5 * (here + after)
            upy = 0.5 * (one + one_n)
            upz = 0.5 * (two + two_n)
            downz = 0.5 * (two + two_p)
            f0[plane(x), :] = up0 if x < BS - 1 else ZERO()
            fy[plane(x), :] = jnp.where(row == BS - 1, 0.0, upy)
            fz[plane(x), :] = jnp.where(lane == LANES - 1, 0.0, upz)
            fzs[plane(x), :] = jnp.where(lane % BS == BS - 1, 0.0, upz)
            c0[plane(x), :] = up0 + upy + upz + 0.5 * (here + before) + 0.5 * (one + one_p) + downz
            total_up = total_up + fold(upz)
            total_down = total_down + fold(downz)
            before, here = here, after
        czu[8 * xc : 8 * xc + 8, :] = total_up
        czd[8 * xc : 8 * xc + 8, :] = total_down
    fx[0:BS, :] = load(inv, 0, 0)
    fx[BS : 2 * BS, :] = load(inv, BS - 1, 0)
    for g in range(4):
        fyf[8 * g : 8 * g + 8, :] = inv[pl.ds(ROWS + 256 * g, 8, stride=BS), :]
        fyf[BS + 8 * g : BS + 8 * g + 8, :] = inv[pl.ds(ROWS + 256 * g + 31, 8, stride=BS), :]
    limit[...] = sweep_limits(levels, level_sweeps)
    device = Place().device
    owner = new_owner[...]
    block = lax.broadcasted_iota(jnp.int32, owner.shape, 0) * owner.shape[1]
    block = block + lax.broadcasted_iota(jnp.int32, owner.shape, 1)
    home, place = block // BLK, block % BLK
    leaving = jnp.where(owner > home, BLK - place, jnp.where(owner < home, place + 1, 0))
    owned[0] = jnp.sum((owner < device).astype(F32)).astype(jnp.int32)
    owned[1] = jnp.sum((owner == device).astype(F32)).astype(jnp.int32)
    most[0] = jnp.max(leaving.astype(F32)).astype(jnp.int32)


def add_faces_y(ref, low, high):
    for g in range(4):
        at = pl.ds(256 * g, 8, stride=BS)
        ref[at, :] = ref[at, :] + low[8 * g : 8 * g + 8]
        at = pl.ds(256 * g + 31, 8, stride=BS)
        ref[at, :] = ref[at, :] + high[8 * g : 8 * g + 8]


def add_faces_x(ref, low, high):
    ref[0:BS, :] = ref[0:BS, :] + low
    ref[ROWS - BS : ROWS, :] = ref[ROWS - BS : ROWS, :] + high


def send_faces(place, p, sa, sb, sc, sd):
    even = place.even[0]
    for g in range(4):
        low = p[pl.ds(256 * g, 8, stride=BS), :]
        high = p[pl.ds(256 * g + 31, 8, stride=BS), :]
        sa[8 * g : 8 * g + 8, :] = pick(even, high, low)
        sb[8 * g : 8 * g + 8, :] = pick(even, low, high)
    low = p[0:BS, :]
    high = p[ROWS - BS : ROWS, :]
    sc[...] = pick(place.even[1], high, low)
    sd[...] = pick(place.even[1], low, high)


def sweep_limits(levels, level_sweeps):
    block = lane_ids(BS) // BS
    limit = jnp.zeros((BS, LANES), jnp.int32)
    for b in range(BLK):
        limit = jnp.where(block == b, level_sweeps[levels[b]], limit)
    return limit.astype(F32)


def relax(limit, r, e, f0, fy, fzs, d, finish):
    def sweep(i, load, store):
        active = limit > float(i)

        t0, here = ZERO(), load(plane(0))
        for x in range(BS):
            at = plane(x)
            after = load(after_plane(x))
            w0, wy, wz = f0[at, :], fy[at, :], fzs[at, :]
            t1 = w0 * here
            total = r[at, :] + t0 + w0 * after
            total = total + wy * next_y(here) + prev_y(wy * here)
            total = total + wz * next_z(here) + prev_z(wz * here)
            store(at, jnp.where(active, KEEP * here + d[at, :] * total, here))
            t0, here = t1, after

    def first(at):
        return d[at, :] * r[at, :]

    def held(at):
        return e[at, :]

    def keep(at, value):
        e[at, :] = value

    sweep(1, first, keep)
    for i in range(2, SWEEP_MAX - 1):
        sweep(i, held, keep)
    sweep(SWEEP_MAX - 1, held, finish)


def first_kernel(
    limit, src, f0, fy, fzs, c0, fx, fyf, ra, rb, rc, rd,
    c, d, gx, gy, p, sa, sb, sc, sd, e,
):
    def natural(ref):
        return jnp.concatenate([ref[pl.ds(k, 8, stride=4), :] for k in range(4)], axis=0)

    place = Place()
    xlo, xhi = low_high(place, 1, natural(rc), natural(rd))
    ylo, yhi = low_high(place, 0, ra[...], rb[...])
    gx[0:BS, :] = 0.5 * (fx[0:BS, :] + xlo)
    gx[BS : 2 * BS, :] = 0.5 * (fx[BS : 2 * BS, :] + xhi)
    gy[0:BS, :] = 0.5 * (fyf[0:BS, :] + ylo)
    gy[BS : 2 * BS, :] = 0.5 * (fyf[BS : 2 * BS, :] + yhi)
    add_faces_x(c, 0.5 * xlo, 0.5 * xhi)
    add_faces_y(c, 0.5 * ylo, 0.5 * yhi)

    for x in range(BS):
        at = plane(x)
        d[at, :] = RELAX / c[at, :]

    def finish(at, value):
        p[at, :] = value

    relax(limit[...], src, e, f0, fy, fzs, d, finish)
    send_faces(place, p, sa, sb, sc, sd)


def residual_plane(src, c, f0, fy, fz, at, t0, here, after):
    w0, wy, wz = f0[at, :], fy[at, :], fz[at, :]
    total = src[at, :] - c[at, :] * here + t0 + w0 * after
    total = total + wy * next_y(here) + prev_y(wy * here)
    total = total + wz * next_z(here) + prev_z(wz * here)
    return total, w0 * here


def coarse_rhs_kernel(src, c, f0, fy, fz, p, q, scr):
    t0, here = ZERO(), p[0:BS, :]
    for xc in range(XC):
        total = jnp.zeros((8, LANES), F32)
        for j in range(4):
            x = xc * 4 + j
            after = p[after_plane(x), :]
            r, t0 = residual_plane(src, c, f0, fy, fz, plane(x), t0, here, after)
            total = total + fold(r)
            here = after
        scr[8 * xc : 8 * xc + 8, :] = total
    q[...] = group_sum(scr[...], group_matrix()) * PART


def coarse_weights_kernel(f0, fy, gx, gy, czu, czd, packed, scr, cy):
    ones = group_matrix()
    lane = lane_ids(CROWS)
    row = row_ids(CROWS)
    for xc in range(XC):
        scr[8 * xc : 8 * xc + 8, :] = fold(f0[(4 * xc + 3) * BS : (4 * xc + 4) * BS, :])
        total = fy[4 * xc * BS + 24 : 4 * xc * BS + 32, :]
        for j in range(1, 4):
            at = (4 * xc + j) * BS
            total = total + fy[at + 24 : at + 32, :]
        cy[8 * xc : 8 * xc + 8, :] = total
    c0 = group_sum(scr[...], ones) * PART
    cy[pl.ds(7, 8, stride=8), :] = by_fours(gy, BS)
    up_y = group_sum(cy[...], ones) * PART
    gxlo = group_sum(fold(gx[0:BS, :]), ones) * PART
    gxhi = group_sum(fold(gx[BS : 2 * BS, :]), ones) * PART
    up_z = group_sum(jnp.where(lane % 4 == 3, czu[...], 0.0), ones) * PART
    down_z = group_sum(jnp.where(lane % 4 == 0, czd[...], 0.0), ones) * PART
    up_0 = jnp.concatenate([c0[0 : CROWS - 8], gxhi], axis=0)
    down_0 = jnp.concatenate([gxlo, c0[0 : CROWS - 8]], axis=0)
    cy[...] = jnp.concatenate(
        [pltpu.roll(up_y[8 * xc : 8 * xc + 8], 1, 0) for xc in range(XC)], axis=0
    )
    cy[pl.ds(0, 8, stride=8), :] = group_sum(by_fours(gy, 0), ones) * PART
    scale = RELAX / (up_0 + up_y + up_z + down_0 + cy[...] + down_z)
    couple_y = jnp.where(row % 8 == 7, up_y * Place().high[0].astype(F32), up_y)
    couple_z = jnp.where(lane >= LANES - 4, 0.0, up_z)
    slot = lane % 4
    packed[...] = jnp.where(
        slot == 0, c0, jnp.where(slot == 1, couple_y, jnp.where(slot == 2, couple_z, scale))
    )


def coarse_faces_kernel(qi, gx, gy, ra, rc, rd, sb, *rest):
    packed, (ma, mb, scr) = rest[:-3], rest[-3:]
    place = Place()
    xlo, xhi = low_high(place, 1, rc[...], rd[...])
    even = place.even[0]
    own = jnp.where(jnp.full(ra.shape, even.astype(jnp.int32)) == 1, gy[BS : 2 * BS, :], gy[0:BS, :])
    scr[...] = own * ra[...]
    faces = jnp.concatenate(
        [fold(gx[0:BS, :] * xlo), fold(gx[BS : 2 * BS, :] * xhi), by_fours(scr, 0)], axis=0
    )
    faces = group_sum(faces, group_matrix()) * PART
    ma[0:CROWS, :] = qi[...]
    ma[0:8, :] = ma[0:8, :] + faces[0:8]
    ma[CROWS - 8 : CROWS, :] = ma[CROWS - 8 : CROWS, :] + faces[8:16]
    nothing = jnp.zeros((8, LANES), F32)
    at = pl.ds(0, 8, stride=8)
    ma[at, :] = ma[at, :] + pick(even, nothing, faces[16:24])
    at = pl.ds(7, 8, stride=8)
    ma[at, :] = ma[at, :] + pick(even, faces[16:24], nothing)
    mb[0:CROWS, :] = ma[0:CROWS, :]
    mb[CROWS : CROWS + BS, :] = sb[...]
    for w in packed:
        ma[CROWS : 2 * CROWS, :] = w[...]
        mb[CROWS + BS : 2 * CROWS + BS, :] = w[...]


def joined(place, own, first, second):
    low, high = low_high(place, 0, first, second)
    parts = []
    for xc in range(XC):
        at = slice(8 * xc, 8 * xc + 8)
        parts += [low[at], own[at], high[at]]
    return jnp.concatenate(parts, axis=0)


def coarse_solve(place, ma, qa, qb, sb, gy, weights, c, cyb, sa, sc, sd, scr, two):
    even = place.even[0]
    w0, wy, wz, scale = weights
    scr[...] = joined(place, ma[0:CROWS, :], qa[0:CROWS, :], qb[0:CROWS, :])
    side = pick(even, gy[0:BS, :], gy[BS : 2 * BS, :])
    there = jnp.where(even, place.low[0].astype(F32), place.high[0].astype(F32))
    two[0:BS, :] = side * qb[CROWS : CROWS + BS, :] * there
    two[BS : 2 * BS, :] = side * sb[...]
    faces = jnp.concatenate([by_fours(two, 0), by_fours(two, BS)], axis=0)
    faces = group_sum(faces, group_matrix()) * PART
    mine, theirs = faces[0:8], faces[8:16]
    nothing = jnp.zeros((8, LANES), F32)
    for row, value in (
        (8, pick(even, mine, nothing)),
        (7, pick(even, theirs, nothing)),
        (15, pick(even, nothing, mine)),
        (16, pick(even, nothing, theirs)),
    ):
        at = pl.ds(row, 8, stride=24)
        scr[at, :] = scr[at, :] + value
    rhs = scr[...]

    def up_x(v):
        return jnp.concatenate([v[24:], v[:24]], axis=0)

    def down_x(v):
        return jnp.concatenate([v[-24:], v[:-24]], axis=0)

    def by_plane(v, shift):
        return jnp.concatenate(
            [pltpu.roll(v[24 * xc : 24 * xc + 24], shift, 0) for xc in range(XC)], axis=0
        )

    field = scale * rhs
    for _ in range(CSWEEPS - 1):
        total = rhs + w0 * up_x(field) + down_x(w0 * field)
        total = total + wy * by_plane(field, 23) + by_plane(wy * field, 1)
        total = total + wz * pltpu.roll(field, LANES - 4, 1) + pltpu.roll(wz * field, 4, 1)
        field = KEEP * field + scale * total
    scr[...] = field
    for xc in range(XC):
        c[8 * xc : 8 * xc + 8, :] = field[24 * xc + 8 : 24 * xc + 16]
    cyb[...] = pick(even, scr[pl.ds(7, 8, stride=24), :], scr[pl.ds(16, 8, stride=24), :])
    sa[...] = pick(even, scr[pl.ds(15, 8, stride=24), :], scr[pl.ds(8, 8, stride=24), :])
    low, high = field[8:16], field[24 * 7 + 8 : 24 * 7 + 16]
    sc[...] = pick(place.even[1], high, low)
    sd[...] = pick(place.even[1], low, high)


def first_coarse_kernel(ma, qa, qb, sb, gy, c, cyb, sa, sc, sd, wide, scr, two):
    place = Place()
    packed = joined(
        place, ma[CROWS : 2 * CROWS, :], qa[CROWS : 2 * CROWS, :], qb[CROWS + BS :, :]
    )
    ones = group_matrix()
    slot = lane_ids(3 * CROWS) % 4
    weights = [group_sum(jnp.where(slot == j, packed, 0.0), ones) for j in range(4)]
    for j in range(4):
        wide[3 * CROWS * j : 3 * CROWS * (j + 1), :] = weights[j]
    coarse_solve(place, ma, qa, qb, sb, gy, weights, c, cyb, sa, sc, sd, scr, two)


def later_coarse_kernel(ma, qa, qb, sb, gy, wide, c, cyb, sa, sc, sd, scr, two):
    weights = [wide[3 * CROWS * j : 3 * CROWS * (j + 1), :] for j in range(4)]
    coarse_solve(Place(), ma, qa, qb, sb, gy, weights, c, cyb, sa, sc, sd, scr, two)


def spread_rows(scr, value):
    for j in range(4):
        scr[pl.ds(j, 8, stride=4), :] = value
    return scr[...]


def correct_kernel(src, c, f0, fy, fz, p, gy, qb, cc, cyb, p2, r, scr):
    def corrected(x):
        return p[plane(x), :] + tiled(cc[8 * (x // 4) : 8 * (x // 4) + 8, :])

    t0, here = ZERO(), corrected(0)
    for x in range(BS):
        at = plane(x)
        after = corrected(min(x + 1, BS - 1))
        p2[at, :] = here
        r[at, :], t0 = residual_plane(src, c, f0, fy, fz, at, t0, here, after)
        here = after
    halo = qb[CROWS : CROWS + BS, :] + spread_rows(scr, cyb[...])
    ylo, yhi = low_high(Place(), 0, ZERO(), halo)
    add_faces_y(r, gy[0:BS, :] * ylo, gy[BS : 2 * BS, :] * yhi)


def residual_kernel(src, c, f0, fy, fz, p, r):
    t0, here = ZERO(), p[0:BS, :]
    for x in range(BS):
        at = plane(x)
        after = p[after_plane(x), :]
        r[at, :], t0 = residual_plane(src, c, f0, fy, fz, at, t0, here, after)
        here = after


def add_all(place, gx, gy, ra, rb, rc, rd, ref):
    xlo, xhi = low_high(place, 1, rc, rd)
    add_faces_x(ref, gx[0:BS, :] * xlo, gx[BS : 2 * BS, :] * xhi)
    ylo, yhi = low_high(place, 0, ra, rb)
    add_faces_y(ref, gy[0:BS, :] * ylo, gy[BS : 2 * BS, :] * yhi)


def finish_smooth(place, limit, r, f0, fy, fzs, d, p, p_out, sends, e):
    def finish(at, value):
        p_out[at, :] = p[at, :] + value

    relax(limit, r, e, f0, fy, fzs, d, finish)
    send_faces(place, p_out, *sends)


def smooth_corrected_kernel(
    ri, limit, f0, fy, fzs, d, p, gx, gy, ra, rc, rd, ka, kc, kd,
    r, p_out, sa, sb, sc, sd, e, scr,
):
    place = Place()
    near = ra[...] + spread_rows(scr, ka[...])
    add_all(place, gx, gy, near, ZERO(), rc[...] + tiled(kc[...]), rd[...] + tiled(kd[...]), r)
    finish_smooth(place, limit[...], r, f0, fy, fzs, d, p, p_out, (sa, sb, sc, sd), e)


def smooth_kernel(
    ri, limit, f0, fy, fzs, d, p, gx, gy, ra, rb, rc, rd,
    r, p_out, sa, sb, sc, sd, e,
):
    place = Place()
    add_all(place, gx, gy, ra[...], rb[...], rc[...], rd[...], r)
    finish_smooth(place, limit[...], r, f0, fy, fzs, d, p, p_out, (sa, sb, sc, sd), e)


def plane_to_blocks(v, x, out, base):
    lane = lane_ids(8)
    half = lane < 64
    even = (lane // BS) % 2 == 0
    v = [v[8 * k : 8 * k + 8] for k in range(4)]
    u = [None] * 4
    for k in range(2):
        low, high = v[k], v[k + 2]
        u[k] = jnp.where(half, low, pltpu.roll(high, 64, 1))
        u[k + 2] = jnp.where(half, pltpu.roll(low, 64, 1), high)
    for b in (0, 2):
        low, high = u[b], u[b + 1]
        first = jnp.where(even, low, pltpu.roll(high, BS, 1))
        second = jnp.where(even, pltpu.roll(low, LANES - BS, 1), high)
        at = base + b * STEP + x * 8
        out[at : at + 8, :] = first
        out[at + STEP : at + STEP + 8, :] = second


def last_residual_kernel(src, c, f0, fy, fz, p, r, blocks, *, count):
    t0, here = ZERO(), p[0:BS, :]
    for x in range(BS):
        at = plane(x)
        after = p[after_plane(x), :]
        r[at, :], t0 = residual_plane(src, c, f0, fy, fz, at, t0, here, after)
        here = after
    for x in range(BS):
        plane_to_blocks(p[plane(x), :], x, blocks, count * STEP)


def final_kernel(ri, gx, gy, ra, rb, rc, rd, pblocks, r, blocks, sa, sb, *, count):
    place = Place()
    even = place.even[0]
    add_all(place, gx, gy, ra[...], rb[...], rc[...], rd[...], r)

    for x in range(BS):
        plane_to_blocks(r[plane(x), :], x, blocks, count * STEP)
    for n, ref in enumerate((pblocks, blocks)):
        for b in range(count):
            for t in range(0, 256, 32):
                low = (count + b) * STEP + t
                high = (BLK + b) * STEP + t
                low, high = ref[low : low + 32, :], ref[high : high + 32, :]
                at = slice((n * count + b) * 256 + t, (n * count + b) * 256 + t + 32)
                sa[at, :] = pick(even, high, low)
                sb[at, :] = pick(even, low, high)


def place_kernel(owned, in_p, in_r, ra, rb, out_p, out_r, seq_p, seq_r, held_p, held_r, sems, *, count):
    place = Place()
    even = place.even[0]
    start, held = owned[0], owned[1]
    base = jnp.clip(start - place.device * BLK + count, 0, 2 * count) * STEP
    valid = row_ids(8) < held
    copies = []
    fields = ((seq_p, held_p, out_p), (seq_r, held_r, out_r))
    for n, (seq, tiles, out) in enumerate(fields):
        for b in range(count):
            for t in range(0, 256, 32):
                at = slice((n * count + b) * 256 + t, (n * count + b) * 256 + t + 32)
                low, high = b * STEP + t, (count + BLK + b) * STEP + t
                seq[low : low + 32, :] = pick(even, rb[at, :], ra[at, :])
                seq[high : high + 32, :] = pick(even, ra[at, :], rb[at, :])
        for part in range(PIECES):
            for t in range(part * PIECE, (part + 1) * PIECE):
                rows = seq[pl.ds(base + t, 8, stride=STEP), :]
                tiles[t, :, :] = jnp.where(valid, rows, 0.0)[0:CAP]
            at = pl.ds(part * PIECE, PIECE)
            copy = pltpu.make_async_copy(tiles.at[at], out.at[at], sems.at[n, part])
            copy.start()
            copies.append(copy)
    for copy in copies:
        copy.wait()


BOTH = ("region", "member")


def swap_near(value):
    return lax.ppermute(value, "member", [(i, i ^ 1) for i in range(lax.axis_size("member"))])


def swap_far(value):
    regions, members = lax.axis_size("region"), lax.axis_size("member")
    pairs = []
    for r in range(regions):
        for m in range(members):
            other = m + 1 if m % 2 else m - 1
            inside = 0 <= other < members
            target = r * members + other if inside else (r ^ 1) * members + m
            pairs.append((r * members + m, target))
    return lax.ppermute(value, BOTH, pairs)


def swap_regions(inner, outer):
    regions, members = lax.axis_size("region"), lax.axis_size("member")
    pairs = []
    for r in range(regions):
        other = r + 1 if r % 2 else r - 1
        inside = 0 <= other < regions
        for m in range(members):
            target = other * members + m if inside else r * members + (m ^ 1)
            pairs.append((r * members + m, target))
    inner = lax.ppermute(inner, "region", [(i, i ^ 1) for i in range(regions)])
    return inner, lax.ppermute(outer, BOTH, pairs)


def swap_blocks(first, second):
    count = lax.axis_size(BOTH)
    inner = [(i, i ^ 1) for i in range(count)]
    outer = [(i, (i + 1) % count if i % 2 else (i - 1) % count) for i in range(count)]
    return lax.ppermute(first, BOTH, inner), lax.ppermute(second, BOTH, outer)


def swap_faces(sa, sb, sc, sd):
    return (swap_near(sa), swap_far(sb), *swap_regions(sc, sd))


FULL, TWO, CFIELD = (ROWS, LANES), (2 * BS, LANES), (CROWS, LANES)
FACE, CFACE = (BS, LANES), (8, LANES)


def set_up(levels, new_owner, src, inv):
    outs = [jax.ShapeDtypeStruct((2,), jnp.int32), jax.ShapeDtypeStruct((1,), jnp.int32)] + [
        jax.ShapeDtypeStruct(s, F32) for s in [FULL] * 6 + [TWO] * 2 + [CFIELD] * 2 + [FACE]
    ]
    vm, sm = pl.BlockSpec(memory_space=pltpu.VMEM), pl.BlockSpec(memory_space=pltpu.SMEM)
    return pl.pallas_call(
        weights_kernel,
        out_shape=outs,
        in_specs=[sm] * 2 + [vm] * 3,
        out_specs=[sm] * 2 + [vm] * 11,
        compiler_params=pltpu.CompilerParams(vmem_limit_bytes=48 << 20),
        cost_estimate=pl.CostEstimate(flops=4000000, bytes_accessed=6 << 20, transcendentals=0),
    )(*levels, new_owner.reshape(-1, min(LANES, new_owner.size)), src, inv)


def row_shape(count):
    return ((2 * count + 8) * STEP, LANES)


def faces_kernel(inv, sa, sb, sc, sd, sems):
    place = Place()
    low, high = (0, BS - 1)

    def copies(first, second, axis):
        if axis == 0:
            pair = ((inv.at[1, :, first, :], sa), (inv.at[1, :, second, :], sb))
        else:
            pair = ((inv.at[0, first], sc), (inv.at[0, second], sd))
        return [
            pltpu.make_async_copy(source, to, sems.at[2 * axis + n])
            for n, (source, to) in enumerate(pair)
        ]

    for axis in range(2):

        @pl.when(place.even[axis])
        def _():
            for copy in copies(high, low, axis):
                copy.start()

        @pl.when(jnp.logical_not(place.even[axis]))
        def _():
            for copy in copies(low, high, axis):
                copy.start()

    for axis in range(2):
        for copy in copies(low, high, axis):
            copy.wait()


def density_faces(inverse_density):
    return pl.pallas_call(
        faces_kernel,
        out_shape=[jax.ShapeDtypeStruct(FACE, F32)] * 4,
        in_specs=[pl.BlockSpec(memory_space=pl.ANY)],
        out_specs=[pl.BlockSpec(memory_space=pltpu.VMEM)] * 4,
        scratch_shapes=[pltpu.SemaphoreType.DMA((4,))],
        compiler_params=pltpu.CompilerParams(vmem_limit_bytes=48 << 20),
        cost_estimate=pl.CostEstimate(flops=2000000000, bytes_accessed=131072, transcendentals=0),
    )(inverse_density)


def place_blocks(count, owned, *arrays):
    slots, row = (256, CAP, LANES), row_shape(count)
    vm = pl.BlockSpec(memory_space=pltpu.VMEM)
    anywhere = pl.BlockSpec(memory_space=pl.ANY)
    outs = pl.pallas_call(
        functools.partial(place_kernel, count=count),
        out_shape=[jax.ShapeDtypeStruct(shape, F32) for shape in (slots, slots, row, row)],
        in_specs=[pl.BlockSpec(memory_space=pltpu.SMEM)] + [vm] * 4,
        out_specs=[anywhere] * 2 + [vm] * 2,
        scratch_shapes=[vmem(*slots), vmem(*slots), pltpu.SemaphoreType.DMA((2, PIECES))],
        input_output_aliases={1: 2, 2: 3},
        compiler_params=pltpu.CompilerParams(vmem_limit_bytes=48 << 20),
        cost_estimate=pl.CostEstimate(flops=2000000, bytes_accessed=6 << 20, transcendentals=0),
    )(owned, *arrays)
    return tuple(o.transpose(1, 0, 2).reshape(CAP, 256 * LANES) for o in outs[:2])


def on_device(source, inverse_density, block_level, level_sweeps, new_owner):
    levels = (block_level, level_sweeps)
    halos = swap_faces(*density_faces(inverse_density))
    owned, most, src, f0, fy, fz, fzs, c0, fx, fyf, czu, czd, limit = set_up(
        levels, new_owner, source.reshape(ROWS, LANES), inverse_density.reshape(3 * ROWS, LANES)
    )
    c, d, gx, gy, p, *sends = call(
        first_kernel,
        [FULL, FULL, TWO, TWO, FULL] + [FACE] * 4,
        [limit, src, f0, fy, fzs, c0, fx, fyf, *halos],
        (),
        [vmem(*FULL)],
        {5: 0},
    )
    fine = [src, c, f0, fy, fz]
    wide = None
    for cycle in range(CYCLES):
        if cycle > 0:
            halos = swap_faces(*sends)
            (ri,) = call(residual_kernel, [FULL], [*fine, p])
            _, p, *sends = call(
                smooth_kernel,
                [FULL, FULL] + [FACE] * 4,
                [ri, limit, f0, fy, fzs, d, p, gx, gy, *halos],
                (),
                [vmem(*FULL)],
                {0: 0},
            )
        sa, sb, sc, sd = sends
        ra = swap_near(sa)
        rc, rd = swap_regions(sc, sd)
        (qi,) = call(coarse_rhs_kernel, [CFIELD], [*fine, p], scratch=[vmem(*CFIELD)])
        packed, rows = [], CROWS
        if wide is None:
            packed = call(
                coarse_weights_kernel,
                [CFIELD],
                [f0, fy, gx, gy, czu, czd],
                scratch=[vmem(*CFIELD)] * 2,
            )
            rows = 2 * CROWS
        ma, mb = call(
            coarse_faces_kernel,
            [(rows, LANES), (rows + BS, LANES)],
            [qi, gx, gy, ra, rc, rd, sb, *packed],
            scratch=[vmem(*FACE)],
        )
        qa, qb = swap_near(ma), swap_far(mb)
        outs = [CFIELD] + [CFACE] * 4
        arrays = [ma, qa, qb, sb, gy]
        scratch = [vmem(3 * CROWS, LANES), vmem(*TWO)]
        if wide is None:
            cc, cyb, ta, tc, td, wide = call(
                first_coarse_kernel, outs + [(12 * CROWS, LANES)], arrays, scratch=scratch
            )
        else:
            cc, cyb, ta, tc, td = call(later_coarse_kernel, outs, [*arrays, wide], scratch=scratch)
        ka = swap_near(ta)
        kc, kd = swap_regions(tc, td)
        p, ri = call(
            correct_kernel, [FULL, FULL], [*fine, p, gy, qb, cc, cyb], scratch=[vmem(*FACE)]
        )
        _, p, *sends = call(
            smooth_corrected_kernel,
            [FULL, FULL] + [FACE] * 4,
            [ri, limit, f0, fy, fzs, d, p, gx, gy, ra, rc, rd, ka, kc, kd],
            (),
            [vmem(*FULL), vmem(*FACE)],
            {0: 0},
        )

    def tail(count, p, sends, fine, gx, gy, owned):
        halos = swap_faces(*sends)
        row = row_shape(count)
        body = functools.partial(last_residual_kernel, count=count)
        ri, blocks_p = call(body, [FULL, row], [*fine, p])
        part = (2 * count * 256, LANES)
        _, blocks_r, sa, sb = call(
            functools.partial(final_kernel, count=count),
            [FULL, row, part, part],
            [ri, gx, gy, *halos, blocks_p],
            aliases={0: 0},
        )
        return place_blocks(count, owned, blocks_p, blocks_r, *swap_blocks(sa, sb))

    return lax.cond(
        most.reshape(()) <= 1,
        functools.partial(tail, 1),
        functools.partial(tail, BLK),
        p, sends, fine, gx, gy, owned,
    )


def solution(mesh):
    placed = (
        P("region", "member", None),
        P(None, "region", "member", None),
        P(("region", "member")),
        P(),
        P(),
    )
    return jax.shard_map(
        on_device,
        mesh=mesh,
        in_specs=placed,
        out_specs=(P(("region", "member"), None), P(("region", "member"), None)),
        check_vma=False,
    )
```

```python
import functools

import jax
import jax.numpy as jnp
from jax import lax
from jax.experimental import pallas as pl
from jax.experimental.pallas import tpu as pltpu
from jax.sharding import PartitionSpec as P


BS = 32
BLK = 4
CSWEEPS = 8
CYCLES = 2
CAP = 6
SWEEP_MAX = 6
RELAX = 0.8
KEEP = 0.2
PART = 1.0 / 64.0
PIECES = 4
PIECE = 256 // PIECES
STEP = 264
LANES = 128
ROWS = BS * BS
XC = BS // 4
CROWS = XC * XC
ZERO = functools.partial(jnp.zeros, (BS, LANES), jnp.float32)
F32 = jnp.float32


def vmem(*shape):
    return pltpu.VMEM(shape, F32)


def call(body, out_rows, args, scalars=(), scratch=(), aliases=None, flops=2e6, mib=48):
    outs = [jax.ShapeDtypeStruct(s, F32) for s in out_rows]
    moved = sum(a.size * 4 for a in args) + sum(o.size * 4 for o in outs)
    return pl.pallas_call(
        body,
        out_shape=outs,
        in_specs=[pl.BlockSpec(memory_space=pltpu.SMEM)] * len(scalars)
        + [pl.BlockSpec(memory_space=pltpu.VMEM)] * len(args),
        out_specs=[pl.BlockSpec(memory_space=pltpu.VMEM)] * len(outs),
        scratch_shapes=list(scratch),
        input_output_aliases={len(scalars) + k: v for k, v in (aliases or {}).items()},
        compiler_params=pltpu.CompilerParams(vmem_limit_bytes=mib << 20),
        cost_estimate=pl.CostEstimate(flops=int(flops), bytes_accessed=int(moved), transcendentals=0),
    )(*scalars, *args)


class Place:
    def __init__(self):
        region, member = lax.axis_index("region"), lax.axis_index("member")
        self.device = region * lax.axis_size("member") + member
        self.even = (member % 2 == 0, region % 2 == 0)
        self.low = (member > 0, region > 0)
        self.high = (member < lax.axis_size("member") - 1, region < lax.axis_size("region") - 1)


def lane_ids(rows):
    return lax.broadcasted_iota(jnp.int32, (rows, LANES), 1)


def row_ids(rows):
    return lax.broadcasted_iota(jnp.int32, (rows, LANES), 0)


def next_y(v):
    return jnp.concatenate([v[8:32], pltpu.roll(v[0:8], 7, 0)], axis=0)


def prev_y(v):
    return jnp.concatenate([pltpu.roll(v[24:32], 1, 0), v[0:24]], axis=0)


def next_z(v):
    return pltpu.roll(v, LANES - 1, 1)


def prev_z(v):
    return pltpu.roll(v, 1, 1)


def fold(v):
    return v[0:8] + v[8:16] + v[16:24] + v[24:32]


def tiled(v):
    return jnp.concatenate([v, v, v, v], axis=0)


def plane(x):
    return slice(x * BS, (x + 1) * BS)


def after_plane(x):
    return plane(min(x + 1, BS - 1))


def pick(flag, yes, no):
    return jnp.where(jnp.full(yes.shape, flag.astype(jnp.int32), jnp.int32) == 1, yes, no)


def low_high(place, axis, first, second):
    low = pick(place.even[axis], second, first) * place.low[axis].astype(F32)
    high = pick(place.even[axis], first, second) * place.high[axis].astype(F32)
    return low, high


def group_matrix():
    return jnp.where(
        row_ids(LANES) // 4 == lane_ids(LANES) // 4, jnp.float32(1.0), jnp.float32(0.0)
    )


def group_sum(v, ones):
    return lax.dot_general(
        v, ones, (((1,), (0,)), ((), ())), precision=lax.Precision.HIGHEST, preferred_element_type=F32
    )


def by_fours(ref, base):
    total = ref[pl.ds(base, 8, stride=4), :]
    for j in range(1, 4):
        total = total + ref[pl.ds(base + j, 8, stride=4), :]
    return total


def weights_kernel(
    levels, level_sweeps, new_owner, src, inv,
    owned, most, src_t, f0, fy, fz, fzs, c0, fx, fyf, czu, czd, limit,
):
    row, lane = row_ids(BS), lane_ids(BS)

    def load(ref, x, offset):
        return jnp.concatenate(
            [ref[pl.ds(offset + x * BS + k, 8, stride=4), :] for k in range(4)], axis=0
        )

    before, here = ZERO(), load(inv, 0, 0)
    for xc in range(XC):
        total_up = jnp.zeros((8, LANES), F32)
        total_down = jnp.zeros((8, LANES), F32)
        for j in range(4):
            x = xc * 4 + j
            src_t[plane(x), :] = load(src, x, 0)
            after = load(inv, x + 1, 0) if x < BS - 1 else ZERO()
            one = load(inv, x, ROWS)
            two = load(inv, x, 2 * ROWS)
            one_n = jnp.where(row == BS - 1, 0.0, next_y(one))
            one_p = jnp.where(row == 0, 0.0, prev_y(one))
            two_n = jnp.where(lane == LANES - 1, 0.0, next_z(two))
            two_p = jnp.where(lane == 0, 0.0, prev_z(two))
            up0 = 0.5 * (here + after)
            upy = 0.5 * (one + one_n)
            upz = 0.5 * (two + two_n)
            downz = 0.5 * (two + two_p)
            f0[plane(x), :] = up0 if x < BS - 1 else ZERO()
            fy[plane(x), :] = jnp.where(row == BS - 1, 0.0, upy)
            fz[plane(x), :] = jnp.where(lane == LANES - 1, 0.0, upz)
            fzs[plane(x), :] = jnp.where(lane % BS == BS - 1, 0.0, upz)
            c0[plane(x), :] = up0 + upy + upz + 0.5 * (here + before) + 0.5 * (one + one_p) + downz
            total_up = total_up + fold(upz)
            total_down = total_down + fold(downz)
            before, here = here, after
        czu[8 * xc : 8 * xc + 8, :] = total_up
        czd[8 * xc : 8 * xc + 8, :] = total_down
    fx[0:BS, :] = load(inv, 0, 0)
    fx[BS : 2 * BS, :] = load(inv, BS - 1, 0)
    for g in range(4):
        fyf[8 * g : 8 * g + 8, :] = inv[pl.ds(ROWS + 256 * g, 8, stride=BS), :]
        fyf[BS + 8 * g : BS + 8 * g + 8, :] = inv[pl.ds(ROWS + 256 * g + 31, 8, stride=BS), :]
    limit[...] = sweep_limits(levels, level_sweeps)
    device = Place().device
    owner = new_owner[...]
    block = lax.broadcasted_iota(jnp.int32, owner.shape, 0) * owner.shape[1]
    block = block + lax.broadcasted_iota(jnp.int32, owner.shape, 1)
    home, place = block // BLK, block % BLK
    leaving = jnp.where(owner > home, BLK - place, jnp.where(owner < home, place + 1, 0))
    owned[0:8, :] = jnp.full((8, LANES), jnp.sum((owner < device).astype(F32)))
    owned[8:16, :] = jnp.full((8, LANES), jnp.sum((owner == device).astype(F32)))
    most[0] = jnp.max(leaving.astype(F32)).astype(jnp.int32)


def add_faces_y(ref, low, high):
    for g in range(4):
        at = pl.ds(256 * g, 8, stride=BS)
        ref[at, :] = ref[at, :] + low[8 * g : 8 * g + 8]
        at = pl.ds(256 * g + 31, 8, stride=BS)
        ref[at, :] = ref[at, :] + high[8 * g : 8 * g + 8]


def add_faces_x(ref, low, high):
    ref[0:BS, :] = ref[0:BS, :] + low
    ref[ROWS - BS : ROWS, :] = ref[ROWS - BS : ROWS, :] + high


def send_faces(place, p, sa, sb, sc, sd):
    even = place.even[0]
    for g in range(4):
        low = p[pl.ds(256 * g, 8, stride=BS), :]
        high = p[pl.ds(256 * g + 31, 8, stride=BS), :]
        sa[8 * g : 8 * g + 8, :] = pick(even, high, low)
        sb[8 * g : 8 * g + 8, :] = pick(even, low, high)
    low = p[0:BS, :]
    high = p[ROWS - BS : ROWS, :]
    sc[...] = pick(place.even[1], high, low)
    sd[...] = pick(place.even[1], low, high)


def sweep_limits(levels, level_sweeps):
    block = lane_ids(BS) // BS
    limit = jnp.zeros((BS, LANES), jnp.int32)
    for b in range(BLK):
        limit = jnp.where(block == b, level_sweeps[levels[b]], limit)
    return limit.astype(F32)


def relax(limit, r, e, f0, fy, fzs, d, finish):
    def sweep(i, load, store):
        active = limit > float(i)

        t0, here = ZERO(), load(plane(0))
        for x in range(BS):
            at = plane(x)
            after = load(after_plane(x))
            w0, wy, wz = f0[at, :], fy[at, :], fzs[at, :]
            t1 = w0 * here
            total = r[at, :] + t0 + w0 * after
            total = total + wy * next_y(here) + prev_y(wy * here)
            total = total + wz * next_z(here) + prev_z(wz * here)
            store(at, jnp.where(active, KEEP * here + d[at, :] * total, here))
            t0, here = t1, after

    def first(at):
        return d[at, :] * r[at, :]

    def held(at):
        return e[at, :]

    def keep(at, value):
        e[at, :] = value

    sweep(1, first, keep)
    for i in range(2, SWEEP_MAX - 1):
        sweep(i, held, keep)
    sweep(SWEEP_MAX - 1, held, finish)


def first_kernel(
    limit, src, f0, fy, fzs, c0, fx, fyf, ra, rb, rc, rd,
    c, d, gx, gy, p, sa, sb, sc, sd, e,
):
    def natural(ref):
        return jnp.concatenate([ref[pl.ds(k, 8, stride=4), :] for k in range(4)], axis=0)

    place = Place()
    xlo, xhi = low_high(place, 1, natural(rc), natural(rd))
    ylo, yhi = low_high(place, 0, ra[...], rb[...])
    gx[0:BS, :] = 0.5 * (fx[0:BS, :] + xlo)
    gx[BS : 2 * BS, :] = 0.5 * (fx[BS : 2 * BS, :] + xhi)
    gy[0:BS, :] = 0.5 * (fyf[0:BS, :] + ylo)
    gy[BS : 2 * BS, :] = 0.5 * (fyf[BS : 2 * BS, :] + yhi)
    add_faces_x(c, 0.5 * xlo, 0.5 * xhi)
    add_faces_y(c, 0.5 * ylo, 0.5 * yhi)

    for x in range(BS):
        at = plane(x)
        d[at, :] = RELAX / c[at, :]

    def finish(at, value):
        p[at, :] = value

    relax(limit[...], src, e, f0, fy, fzs, d, finish)
    send_faces(place, p, sa, sb, sc, sd)


def residual_plane(src, c, f0, fy, fz, at, t0, here, after):
    w0, wy, wz = f0[at, :], fy[at, :], fz[at, :]
    total = src[at, :] - c[at, :] * here + t0 + w0 * after
    total = total + wy * next_y(here) + prev_y(wy * here)
    total = total + wz * next_z(here) + prev_z(wz * here)
    return total, w0 * here


def coarse_rhs_kernel(src, c, f0, fy, fz, p, q, scr):
    t0, here = ZERO(), p[0:BS, :]
    for xc in range(XC):
        total = jnp.zeros((8, LANES), F32)
        for j in range(4):
            x = xc * 4 + j
            after = p[after_plane(x), :]
            r, t0 = residual_plane(src, c, f0, fy, fz, plane(x), t0, here, after)
            total = total + fold(r)
            here = after
        scr[8 * xc : 8 * xc + 8, :] = total
    q[...] = group_sum(scr[...], group_matrix()) * PART


def coarse_weights_kernel(f0, fy, gx, gy, czu, czd, packed, scr, cy):
    ones = group_matrix()
    lane = lane_ids(CROWS)
    row = row_ids(CROWS)
    for xc in range(XC):
        scr[8 * xc : 8 * xc + 8, :] = fold(f0[(4 * xc + 3) * BS : (4 * xc + 4) * BS, :])
        total = fy[4 * xc * BS + 24 : 4 * xc * BS + 32, :]
        for j in range(1, 4):
            at = (4 * xc + j) * BS
            total = total + fy[at + 24 : at + 32, :]
        cy[8 * xc : 8 * xc + 8, :] = total
    c0 = group_sum(scr[...], ones) * PART
    cy[pl.ds(7, 8, stride=8), :] = by_fours(gy, BS)
    up_y = group_sum(cy[...], ones) * PART
    gxlo = group_sum(fold(gx[0:BS, :]), ones) * PART
    gxhi = group_sum(fold(gx[BS : 2 * BS, :]), ones) * PART
    up_z = group_sum(jnp.where(lane % 4 == 3, czu[...], 0.0), ones) * PART
    down_z = group_sum(jnp.where(lane % 4 == 0, czd[...], 0.0), ones) * PART
    up_0 = jnp.concatenate([c0[0 : CROWS - 8], gxhi], axis=0)
    down_0 = jnp.concatenate([gxlo, c0[0 : CROWS - 8]], axis=0)
    cy[...] = jnp.concatenate(
        [pltpu.roll(up_y[8 * xc : 8 * xc + 8], 1, 0) for xc in range(XC)], axis=0
    )
    cy[pl.ds(0, 8, stride=8), :] = group_sum(by_fours(gy, 0), ones) * PART
    scale = RELAX / (up_0 + up_y + up_z + down_0 + cy[...] + down_z)
    couple_y = jnp.where(row % 8 == 7, up_y * Place().high[0].astype(F32), up_y)
    couple_z = jnp.where(lane >= LANES - 4, 0.0, up_z)
    slot = lane % 4
    packed[...] = jnp.where(
        slot == 0, c0, jnp.where(slot == 1, couple_y, jnp.where(slot == 2, couple_z, scale))
    )


def coarse_faces_kernel(qi, gx, gy, ra, rc, rd, sb, *rest):
    packed, (ma, mb, scr) = rest[:-3], rest[-3:]
    place = Place()
    xlo, xhi = low_high(place, 1, rc[...], rd[...])
    even = place.even[0]
    own = jnp.where(jnp.full(ra.shape, even.astype(jnp.int32)) == 1, gy[BS : 2 * BS, :], gy[0:BS, :])
    scr[...] = own * ra[...]
    faces = jnp.concatenate(
        [fold(gx[0:BS, :] * xlo), fold(gx[BS : 2 * BS, :] * xhi), by_fours(scr, 0)], axis=0
    )
    faces = group_sum(faces, group_matrix()) * PART
    ma[0:CROWS, :] = qi[...]
    ma[0:8, :] = ma[0:8, :] + faces[0:8]
    ma[CROWS - 8 : CROWS, :] = ma[CROWS - 8 : CROWS, :] + faces[8:16]
    nothing = jnp.zeros((8, LANES), F32)
    at = pl.ds(0, 8, stride=8)
    ma[at, :] = ma[at, :] + pick(even, nothing, faces[16:24])
    at = pl.ds(7, 8, stride=8)
    ma[at, :] = ma[at, :] + pick(even, faces[16:24], nothing)
    mb[0:CROWS, :] = ma[0:CROWS, :]
    mb[CROWS : CROWS + BS, :] = sb[...]
    for w in packed:
        ma[CROWS : 2 * CROWS, :] = w[...]
        mb[CROWS + BS : 2 * CROWS + BS, :] = w[...]


def joined(place, own, first, second):
    low, high = low_high(place, 0, first, second)
    parts = []
    for xc in range(XC):
        at = slice(8 * xc, 8 * xc + 8)
        parts += [low[at], own[at], high[at]]
    return jnp.concatenate(parts, axis=0)


def coarse_solve(place, ma, qa, qb, sb, gy, weights, c, cyb, sa, sc, sd, scr, two):
    even = place.even[0]
    w0, wy, wz, scale = weights
    scr[...] = joined(place, ma[0:CROWS, :], qa[0:CROWS, :], qb[0:CROWS, :])
    side = pick(even, gy[0:BS, :], gy[BS : 2 * BS, :])
    there = jnp.where(even, place.low[0].astype(F32), place.high[0].astype(F32))
    two[0:BS, :] = side * qb[CROWS : CROWS + BS, :] * there
    two[BS : 2 * BS, :] = side * sb[...]
    faces = jnp.concatenate([by_fours(two, 0), by_fours(two, BS)], axis=0)
    faces = group_sum(faces, group_matrix()) * PART
    mine, theirs = faces[0:8], faces[8:16]
    nothing = jnp.zeros((8, LANES), F32)
    for row, value in (
        (8, pick(even, mine, nothing)),
        (7, pick(even, theirs, nothing)),
        (15, pick(even, nothing, mine)),
        (16, pick(even, nothing, theirs)),
    ):
        at = pl.ds(row, 8, stride=24)
        scr[at, :] = scr[at, :] + value
    rhs = scr[...]

    def up_x(v):
        return jnp.concatenate([v[24:], v[:24]], axis=0)

    def down_x(v):
        return jnp.concatenate([v[-24:], v[:-24]], axis=0)

    def by_plane(v, shift):
        return jnp.concatenate(
            [pltpu.roll(v[24 * xc : 24 * xc + 24], shift, 0) for xc in range(XC)], axis=0
        )

    field = scale * rhs
    for _ in range(CSWEEPS - 1):
        total = rhs + w0 * up_x(field) + down_x(w0 * field)
        total = total + wy * by_plane(field, 23) + by_plane(wy * field, 1)
        total = total + wz * pltpu.roll(field, LANES - 4, 1) + pltpu.roll(wz * field, 4, 1)
        field = KEEP * field + scale * total
    scr[...] = field
    for xc in range(XC):
        c[8 * xc : 8 * xc + 8, :] = field[24 * xc + 8 : 24 * xc + 16]
    cyb[...] = pick(even, scr[pl.ds(7, 8, stride=24), :], scr[pl.ds(16, 8, stride=24), :])
    sa[...] = pick(even, scr[pl.ds(15, 8, stride=24), :], scr[pl.ds(8, 8, stride=24), :])
    low, high = field[8:16], field[24 * 7 + 8 : 24 * 7 + 16]
    sc[...] = pick(place.even[1], high, low)
    sd[...] = pick(place.even[1], low, high)


def first_coarse_kernel(ma, qa, qb, sb, gy, c, cyb, sa, sc, sd, wide, scr, two):
    place = Place()
    packed = joined(
        place, ma[CROWS : 2 * CROWS, :], qa[CROWS : 2 * CROWS, :], qb[CROWS + BS :, :]
    )
    ones = group_matrix()
    slot = lane_ids(3 * CROWS) % 4
    weights = [group_sum(jnp.where(slot == j, packed, 0.0), ones) for j in range(4)]
    for j in range(4):
        wide[3 * CROWS * j : 3 * CROWS * (j + 1), :] = weights[j]
    coarse_solve(place, ma, qa, qb, sb, gy, weights, c, cyb, sa, sc, sd, scr, two)


def later_coarse_kernel(ma, qa, qb, sb, gy, wide, c, cyb, sa, sc, sd, scr, two):
    weights = [wide[3 * CROWS * j : 3 * CROWS * (j + 1), :] for j in range(4)]
    coarse_solve(Place(), ma, qa, qb, sb, gy, weights, c, cyb, sa, sc, sd, scr, two)


def spread_rows(scr, value):
    for j in range(4):
        scr[pl.ds(j, 8, stride=4), :] = value
    return scr[...]


def correct_kernel(src, c, f0, fy, fz, p, gy, qb, cc, cyb, p2, r, scr):
    def corrected(x):
        return p[plane(x), :] + tiled(cc[8 * (x // 4) : 8 * (x // 4) + 8, :])

    t0, here = ZERO(), corrected(0)
    for x in range(BS):
        at = plane(x)
        after = corrected(min(x + 1, BS - 1))
        p2[at, :] = here
        r[at, :], t0 = residual_plane(src, c, f0, fy, fz, at, t0, here, after)
        here = after
    halo = qb[CROWS : CROWS + BS, :] + spread_rows(scr, cyb[...])
    ylo, yhi = low_high(Place(), 0, ZERO(), halo)
    add_faces_y(r, gy[0:BS, :] * ylo, gy[BS : 2 * BS, :] * yhi)


def residual_kernel(src, c, f0, fy, fz, p, r):
    t0, here = ZERO(), p[0:BS, :]
    for x in range(BS):
        at = plane(x)
        after = p[after_plane(x), :]
        r[at, :], t0 = residual_plane(src, c, f0, fy, fz, at, t0, here, after)
        here = after


def add_all(place, gx, gy, ra, rb, rc, rd, ref):
    xlo, xhi = low_high(place, 1, rc, rd)
    add_faces_x(ref, gx[0:BS, :] * xlo, gx[BS : 2 * BS, :] * xhi)
    ylo, yhi = low_high(place, 0, ra, rb)
    add_faces_y(ref, gy[0:BS, :] * ylo, gy[BS : 2 * BS, :] * yhi)


def finish_smooth(place, limit, r, f0, fy, fzs, d, p, p_out, sends, e):
    def finish(at, value):
        p_out[at, :] = p[at, :] + value

    relax(limit, r, e, f0, fy, fzs, d, finish)
    send_faces(place, p_out, *sends)


def smooth_corrected_kernel(
    ri, limit, f0, fy, fzs, d, p, gx, gy, ra, rc, rd, ka, kc, kd,
    r, p_out, sa, sb, sc, sd, e, scr,
):
    place = Place()
    near = ra[...] + spread_rows(scr, ka[...])
    add_all(place, gx, gy, near, ZERO(), rc[...] + tiled(kc[...]), rd[...] + tiled(kd[...]), r)
    finish_smooth(place, limit[...], r, f0, fy, fzs, d, p, p_out, (sa, sb, sc, sd), e)


def smooth_kernel(
    ri, limit, f0, fy, fzs, d, p, gx, gy, ra, rb, rc, rd,
    r, p_out, sa, sb, sc, sd, e,
):
    place = Place()
    add_all(place, gx, gy, ra[...], rb[...], rc[...], rd[...], r)
    finish_smooth(place, limit[...], r, f0, fy, fzs, d, p, p_out, (sa, sb, sc, sd), e)


def plane_to_blocks(v, x, out, base):
    lane = lane_ids(8)
    half = lane < 64
    even = (lane // BS) % 2 == 0
    v = [v[8 * k : 8 * k + 8] for k in range(4)]
    u = [None] * 4
    for k in range(2):
        low, high = v[k], v[k + 2]
        u[k] = jnp.where(half, low, pltpu.roll(high, 64, 1))
        u[k + 2] = jnp.where(half, pltpu.roll(low, 64, 1), high)
    for b in (0, 2):
        low, high = u[b], u[b + 1]
        first = jnp.where(even, low, pltpu.roll(high, BS, 1))
        second = jnp.where(even, pltpu.roll(low, LANES - BS, 1), high)
        at = base + b * STEP + x * 8
        out[at : at + 8, :] = first
        out[at + STEP : at + STEP + 8, :] = second


def last_residual_kernel(src, c, f0, fy, fz, p, r, blocks):
    t0, here = ZERO(), p[0:BS, :]
    for x in range(BS):
        at = plane(x)
        after = p[after_plane(x), :]
        r[at, :], t0 = residual_plane(src, c, f0, fy, fz, at, t0, here, after)
        here = after
    for x in range(BS):
        plane_to_blocks(p[plane(x), :], x, blocks, BLK * STEP)


def final_kernel(ri, gx, gy, ra, rb, rc, rd, pblocks, r, blocks, sa, sb):
    place = Place()
    add_all(place, gx, gy, ra[...], rb[...], rc[...], rd[...], r)

    for x in range(BS):
        plane_to_blocks(r[plane(x), :], x, blocks, BLK * STEP)
    send_blocks_kernel(pblocks, blocks, sa, sb, count=1)


def send_blocks_kernel(pblocks, blocks, sa, sb, *, count):
    even = Place().even[0]
    for n, ref in enumerate((pblocks, blocks)):
        for b in range(count):
            for t in range(0, 256, 32):
                low = (BLK + b) * STEP + t
                high = (2 * BLK - count + b) * STEP + t
                low, high = ref[low : low + 32, :], ref[high : high + 32, :]
                at = slice((n * count + b) * 256 + t, (n * count + b) * 256 + t + 32)
                sa[at, :] = pick(even, high, low)
                sb[at, :] = pick(even, low, high)


def place_kernel(owned, in_p, in_r, ra, rb, out_p, out_r, seq_p, seq_r, held_p, held_r, sems, *, count):
    place = Place()
    even = place.even[0]
    start = jnp.max(owned[0:8, :]).astype(jnp.int32)
    base = jnp.clip(start - place.device * BLK + BLK, 0, 2 * BLK) * STEP
    valid = row_ids(8).astype(F32) < owned[8:16, :]
    copies = []
    fields = ((seq_p, held_p, out_p), (seq_r, held_r, out_r))
    for n, (seq, tiles, out) in enumerate(fields):
        for b in range(count):
            for t in range(0, 256, 32):
                at = slice((n * count + b) * 256 + t, (n * count + b) * 256 + t + 32)
                low, high = (BLK - count + b) * STEP + t, (2 * BLK + b) * STEP + t
                seq[low : low + 32, :] = pick(even, rb[at, :], ra[at, :])
                seq[high : high + 32, :] = pick(even, ra[at, :], rb[at, :])
        for part in range(PIECES):
            for t in range(part * PIECE, (part + 1) * PIECE):
                rows = seq[pl.ds(base + t, 8, stride=STEP), :]
                tiles[t, :, :] = jnp.where(valid, rows, 0.0)[0:CAP]
            at = pl.ds(part * PIECE, PIECE)
            copy = pltpu.make_async_copy(tiles.at[at], out.at[at], sems.at[n, part])
            copy.start()
            copies.append(copy)
    for copy in copies:
        copy.wait()


BOTH = ("region", "member")


def swap_near(value):
    return lax.ppermute(value, "member", [(i, i ^ 1) for i in range(lax.axis_size("member"))])


def swap_far(value):
    regions, members = lax.axis_size("region"), lax.axis_size("member")
    pairs = []
    for r in range(regions):
        for m in range(members):
            other = m + 1 if m % 2 else m - 1
            inside = 0 <= other < members
            target = r * members + other if inside else (r ^ 1) * members + m
            pairs.append((r * members + m, target))
    return lax.ppermute(value, BOTH, pairs)


def swap_regions(inner, outer):
    regions, members = lax.axis_size("region"), lax.axis_size("member")
    pairs = []
    for r in range(regions):
        other = r + 1 if r % 2 else r - 1
        inside = 0 <= other < regions
        for m in range(members):
            target = other * members + m if inside else r * members + (m ^ 1)
            pairs.append((r * members + m, target))
    inner = lax.ppermute(inner, "region", [(i, i ^ 1) for i in range(regions)])
    return inner, lax.ppermute(outer, BOTH, pairs)


def swap_blocks(first, second):
    count = lax.axis_size(BOTH)
    inner = [(i, i ^ 1) for i in range(count)]
    outer = [(i, (i + 1) % count if i % 2 else (i - 1) % count) for i in range(count)]
    return lax.ppermute(first, BOTH, inner), lax.ppermute(second, BOTH, outer)


def swap_faces(sa, sb, sc, sd):
    return (swap_near(sa), swap_far(sb), *swap_regions(sc, sd))


FULL, TWO, CFIELD = (ROWS, LANES), (2 * BS, LANES), (CROWS, LANES)
FACE, CFACE = (BS, LANES), (8, LANES)
ROW = ((2 * BLK + 8) * STEP, LANES)


def set_up(levels, new_owner, src, inv):
    outs = [jax.ShapeDtypeStruct((16, LANES), F32), jax.ShapeDtypeStruct((1,), jnp.int32)] + [
        jax.ShapeDtypeStruct(s, F32) for s in [FULL] * 6 + [TWO] * 2 + [CFIELD] * 2 + [FACE]
    ]
    vm, sm = pl.BlockSpec(memory_space=pltpu.VMEM), pl.BlockSpec(memory_space=pltpu.SMEM)
    return pl.pallas_call(
        weights_kernel,
        out_shape=outs,
        in_specs=[sm] * 2 + [vm] * 3,
        out_specs=[vm, sm] + [vm] * 11,
        compiler_params=pltpu.CompilerParams(vmem_limit_bytes=48 << 20),
        cost_estimate=pl.CostEstimate(flops=4000000, bytes_accessed=6 << 20, transcendentals=0),
    )(*levels, new_owner.reshape(-1, min(LANES, new_owner.size)), src, inv)


def faces_kernel(inv, sa, sb, sc, sd, sems):
    place = Place()
    low, high = (0, BS - 1)

    def copies(first, second, axis):
        if axis == 0:
            pair = ((inv.at[1, :, first, :], sa), (inv.at[1, :, second, :], sb))
        else:
            pair = ((inv.at[0, first], sc), (inv.at[0, second], sd))
        return [
            pltpu.make_async_copy(source, to, sems.at[2 * axis + n])
            for n, (source, to) in enumerate(pair)
        ]

    for axis in range(2):

        @pl.when(place.even[axis])
        def _():
            for copy in copies(high, low, axis):
                copy.start()

        @pl.when(jnp.logical_not(place.even[axis]))
        def _():
            for copy in copies(low, high, axis):
                copy.start()

    for axis in range(2):
        for copy in copies(low, high, axis):
            copy.wait()


def density_faces(inverse_density):
    return pl.pallas_call(
        faces_kernel,
        out_shape=[jax.ShapeDtypeStruct(FACE, F32)] * 4,
        in_specs=[pl.BlockSpec(memory_space=pltpu.HBM)],
        out_specs=[pl.BlockSpec(memory_space=pltpu.VMEM)] * 4,
        scratch_shapes=[pltpu.SemaphoreType.DMA((4,))],
        compiler_params=pltpu.CompilerParams(vmem_limit_bytes=48 << 20),
        cost_estimate=pl.CostEstimate(flops=2000000000, bytes_accessed=131072, transcendentals=0),
    )(inverse_density)


def place_blocks(count, owned, *arrays):
    slots, row = (256, CAP, LANES), ROW
    vm = pl.BlockSpec(memory_space=pltpu.VMEM)
    anywhere = pl.BlockSpec(memory_space=pl.ANY)
    outs = pl.pallas_call(
        functools.partial(place_kernel, count=count),
        out_shape=[jax.ShapeDtypeStruct(shape, F32) for shape in (slots, slots, row, row)],
        in_specs=[vm] * 5,
        out_specs=[anywhere] * 2 + [vm] * 2,
        scratch_shapes=[vmem(*slots), vmem(*slots), pltpu.SemaphoreType.DMA((2, PIECES))],
        input_output_aliases={1: 2, 2: 3},
        compiler_params=pltpu.CompilerParams(vmem_limit_bytes=48 << 20),
        cost_estimate=pl.CostEstimate(flops=2000000, bytes_accessed=6 << 20, transcendentals=0),
    )(owned, *arrays)
    return tuple(o.transpose(1, 0, 2).reshape(CAP, 256 * LANES) for o in outs[:2])


def on_device(source, inverse_density, block_level, level_sweeps, new_owner):
    levels = (block_level, level_sweeps)
    halos = swap_faces(*density_faces(inverse_density))
    owned, most, src, f0, fy, fz, fzs, c0, fx, fyf, czu, czd, limit = set_up(
        levels, new_owner, source.reshape(ROWS, LANES), inverse_density.reshape(3 * ROWS, LANES)
    )
    c, d, gx, gy, p, *sends = call(
        first_kernel,
        [FULL, FULL, TWO, TWO, FULL] + [FACE] * 4,
        [limit, src, f0, fy, fzs, c0, fx, fyf, *halos],
        (),
        [vmem(*FULL)],
        {5: 0},
    )
    fine = [src, c, f0, fy, fz]
    wide = None
    for cycle in range(CYCLES):
        if cycle > 0:
            halos = swap_faces(*sends)
            (ri,) = call(residual_kernel, [FULL], [*fine, p])
            _, p, *sends = call(
                smooth_kernel,
                [FULL, FULL] + [FACE] * 4,
                [ri, limit, f0, fy, fzs, d, p, gx, gy, *halos],
                (),
                [vmem(*FULL)],
                {0: 0},
            )
        sa, sb, sc, sd = sends
        ra = swap_near(sa)
        rc, rd = swap_regions(sc, sd)
        (qi,) = call(coarse_rhs_kernel, [CFIELD], [*fine, p], scratch=[vmem(*CFIELD)])
        packed, rows = [], CROWS
        if wide is None:
            packed = call(
                coarse_weights_kernel,
                [CFIELD],
                [f0, fy, gx, gy, czu, czd],
                scratch=[vmem(*CFIELD)] * 2,
            )
            rows = 2 * CROWS
        ma, mb = call(
            coarse_faces_kernel,
            [(rows, LANES), (rows + BS, LANES)],
            [qi, gx, gy, ra, rc, rd, sb, *packed],
            scratch=[vmem(*FACE)],
        )
        qa, qb = swap_near(ma), swap_far(mb)
        outs = [CFIELD] + [CFACE] * 4
        arrays = [ma, qa, qb, sb, gy]
        scratch = [vmem(3 * CROWS, LANES), vmem(*TWO)]
        if wide is None:
            cc, cyb, ta, tc, td, wide = call(
                first_coarse_kernel, outs + [(12 * CROWS, LANES)], arrays, scratch=scratch
            )
        else:
            cc, cyb, ta, tc, td = call(later_coarse_kernel, outs, [*arrays, wide], scratch=scratch)
        ka = swap_near(ta)
        kc, kd = swap_regions(tc, td)
        p, ri = call(
            correct_kernel, [FULL, FULL], [*fine, p, gy, qb, cc, cyb], scratch=[vmem(*FACE)]
        )
        _, p, *sends = call(
            smooth_corrected_kernel,
            [FULL, FULL] + [FACE] * 4,
            [ri, limit, f0, fy, fzs, d, p, gx, gy, ra, rc, rd, ka, kc, kd],
            (),
            [vmem(*FULL), vmem(*FACE)],
            {0: 0},
        )

    halos = swap_faces(*sends)
    ri, blocks_p = call(last_residual_kernel, [FULL, ROW], [*fine, p])
    _, blocks_r, sa, sb = call(
        final_kernel,
        [FULL, ROW] + [(512, LANES)] * 2,
        [ri, gx, gy, *halos, blocks_p],
        aliases={0: 0},
    )

    def one(owned, blocks_p, blocks_r, sa, sb):
        return place_blocks(1, owned, blocks_p, blocks_r, *swap_blocks(sa, sb))

    def several(owned, blocks_p, blocks_r, sa, sb):
        body = functools.partial(send_blocks_kernel, count=BLK)
        sends = call(body, [(2 * BLK * 256, LANES)] * 2, [blocks_p, blocks_r])
        return place_blocks(BLK, owned, blocks_p, blocks_r, *swap_blocks(*sends))

    return lax.cond(most.reshape(()) <= 1, one, several, owned, blocks_p, blocks_r, sa, sb)


def solution(mesh):
    placed = (
        P("region", "member", None),
        P(None, "region", "member", None),
        P(("region", "member")),
        P(),
        P(),
    )
    return jax.shard_map(
        on_device,
        mesh=mesh,
        in_specs=placed,
        out_specs=(P(("region", "member"), None), P(("region", "member"), None)),
        check_vma=False,
    )
```

```python
import functools

import jax
import jax.numpy as jnp
from jax import lax
from jax.experimental import pallas as pl
from jax.experimental.pallas import tpu as pltpu
from jax.sharding import PartitionSpec as P


BS = 32
BLK = 4
CSWEEPS = 8
CYCLES = 2
CAP = 6
SWEEP_MAX = 6
RELAX = 0.8
KEEP = 0.2
PART = 1.0 / 64.0
PIECES = 4
PIECE = 256 // PIECES
STEP = 264
LANES = 128
ROWS = BS * BS
XC = BS // 4
CROWS = XC * XC
ZERO = functools.partial(jnp.zeros, (BS, LANES), jnp.float32)
F32 = jnp.float32


def vmem(*shape):
    return pltpu.VMEM(shape, F32)


def call(body, out_rows, args, scalars=(), scratch=(), aliases=None, flops=2e6, mib=48):
    outs = [jax.ShapeDtypeStruct(s, F32) for s in out_rows]
    moved = sum(a.size * 4 for a in args) + sum(o.size * 4 for o in outs)
    return pl.pallas_call(
        body,
        out_shape=outs,
        in_specs=[pl.BlockSpec(memory_space=pltpu.SMEM)] * len(scalars)
        + [pl.BlockSpec(memory_space=pltpu.VMEM)] * len(args),
        out_specs=[pl.BlockSpec(memory_space=pltpu.VMEM)] * len(outs),
        scratch_shapes=list(scratch),
        input_output_aliases={len(scalars) + k: v for k, v in (aliases or {}).items()},
        compiler_params=pltpu.CompilerParams(vmem_limit_bytes=mib << 20),
        cost_estimate=pl.CostEstimate(flops=int(flops), bytes_accessed=int(moved), transcendentals=0),
    )(*scalars, *args)


class Place:
    def __init__(self):
        region, member = lax.axis_index("region"), lax.axis_index("member")
        self.device = region * lax.axis_size("member") + member
        self.even = (member % 2 == 0, region % 2 == 0)
        self.low = (member > 0, region > 0)
        self.high = (member < lax.axis_size("member") - 1, region < lax.axis_size("region") - 1)


def lane_ids(rows):
    return lax.broadcasted_iota(jnp.int32, (rows, LANES), 1)


def row_ids(rows):
    return lax.broadcasted_iota(jnp.int32, (rows, LANES), 0)


def next_y(v):
    return jnp.concatenate([v[8:32], pltpu.roll(v[0:8], 7, 0)], axis=0)


def prev_y(v):
    return jnp.concatenate([pltpu.roll(v[24:32], 1, 0), v[0:24]], axis=0)


def next_z(v):
    return pltpu.roll(v, LANES - 1, 1)


def prev_z(v):
    return pltpu.roll(v, 1, 1)


def fold(v):
    return v[0:8] + v[8:16] + v[16:24] + v[24:32]


def tiled(v):
    return jnp.concatenate([v, v, v, v], axis=0)


def plane(x):
    return slice(x * BS, (x + 1) * BS)


def after_plane(x):
    return plane(min(x + 1, BS - 1))


def pick(flag, yes, no):
    return jnp.where(jnp.full(yes.shape, flag.astype(jnp.int32), jnp.int32) == 1, yes, no)


def low_high(place, axis, first, second):
    low = pick(place.even[axis], second, first) * place.low[axis].astype(F32)
    high = pick(place.even[axis], first, second) * place.high[axis].astype(F32)
    return low, high


def group_matrix():
    return jnp.where(
        row_ids(LANES) // 4 == lane_ids(LANES) // 4, jnp.float32(1.0), jnp.float32(0.0)
    )


def group_sum(v, ones):
    return lax.dot_general(
        v, ones, (((1,), (0,)), ((), ())), precision=lax.Precision.HIGHEST, preferred_element_type=F32
    )


def by_fours(ref, base):
    total = ref[pl.ds(base, 8, stride=4), :]
    for j in range(1, 4):
        total = total + ref[pl.ds(base + j, 8, stride=4), :]
    return total


def weights_kernel(
    levels, level_sweeps, new_owner, src, inv,
    owned, most, src_t, f0, fy, fz, fzs, c0, fx, fyf, czu, czd, limit,
):
    row, lane = row_ids(BS), lane_ids(BS)

    def load(ref, x, offset):
        return jnp.concatenate(
            [ref[pl.ds(offset + x * BS + k, 8, stride=4), :] for k in range(4)], axis=0
        )

    before, here = ZERO(), load(inv, 0, 0)
    for xc in range(XC):
        total_up = jnp.zeros((8, LANES), F32)
        total_down = jnp.zeros((8, LANES), F32)
        for j in range(4):
            x = xc * 4 + j
            src_t[plane(x), :] = load(src, x, 0)
            after = load(inv, x + 1, 0) if x < BS - 1 else ZERO()
            one = load(inv, x, ROWS)
            two = load(inv, x, 2 * ROWS)
            one_n = jnp.where(row == BS - 1, 0.0, next_y(one))
            one_p = jnp.where(row == 0, 0.0, prev_y(one))
            two_n = jnp.where(lane == LANES - 1, 0.0, next_z(two))
            two_p = jnp.where(lane == 0, 0.0, prev_z(two))
            up0 = 0.5 * (here + after)
            upy = 0.5 * (one + one_n)
            upz = 0.5 * (two + two_n)
            downz = 0.5 * (two + two_p)
            f0[plane(x), :] = up0 if x < BS - 1 else ZERO()
            fy[plane(x), :] = jnp.where(row == BS - 1, 0.0, upy)
            fz[plane(x), :] = jnp.where(lane == LANES - 1, 0.0, upz)
            fzs[plane(x), :] = jnp.where(lane % BS == BS - 1, 0.0, upz)
            c0[plane(x), :] = up0 + upy + upz + 0.5 * (here + before) + 0.5 * (one + one_p) + downz
            total_up = total_up + fold(upz)
            total_down = total_down + fold(downz)
            before, here = here, after
        czu[8 * xc : 8 * xc + 8, :] = total_up
        czd[8 * xc : 8 * xc + 8, :] = total_down
    fx[0:BS, :] = load(inv, 0, 0)
    fx[BS : 2 * BS, :] = load(inv, BS - 1, 0)
    for g in range(4):
        fyf[8 * g : 8 * g + 8, :] = inv[pl.ds(ROWS + 256 * g, 8, stride=BS), :]
        fyf[BS + 8 * g : BS + 8 * g + 8, :] = inv[pl.ds(ROWS + 256 * g + 31, 8, stride=BS), :]
    limit[...] = sweep_limits(levels, level_sweeps)
    device = Place().device
    owner = new_owner[...]
    block = lax.broadcasted_iota(jnp.int32, owner.shape, 0) * owner.shape[1]
    block = block + lax.broadcasted_iota(jnp.int32, owner.shape, 1)
    home, place = block // BLK, block % BLK
    leaving = jnp.where(owner > home, BLK - place, jnp.where(owner < home, place + 1, 0))
    owned[0:8, :] = jnp.full((8, LANES), jnp.sum((owner < device).astype(F32)))
    owned[8:16, :] = jnp.full((8, LANES), jnp.sum((owner == device).astype(F32)))
    most[0] = jnp.max(leaving.astype(F32)).astype(jnp.int32)


def add_faces_y(ref, low, high):
    for g in range(4):
        at = pl.ds(256 * g, 8, stride=BS)
        ref[at, :] = ref[at, :] + low[8 * g : 8 * g + 8]
        at = pl.ds(256 * g + 31, 8, stride=BS)
        ref[at, :] = ref[at, :] + high[8 * g : 8 * g + 8]


def add_faces_x(ref, low, high):
    ref[0:BS, :] = ref[0:BS, :] + low
    ref[ROWS - BS : ROWS, :] = ref[ROWS - BS : ROWS, :] + high


def send_faces(place, p, sa, sb, sc, sd):
    even = place.even[0]
    for g in range(4):
        low = p[pl.ds(256 * g, 8, stride=BS), :]
        high = p[pl.ds(256 * g + 31, 8, stride=BS), :]
        sa[8 * g : 8 * g + 8, :] = pick(even, high, low)
        sb[8 * g : 8 * g + 8, :] = pick(even, low, high)
    low = p[0:BS, :]
    high = p[ROWS - BS : ROWS, :]
    sc[...] = pick(place.even[1], high, low)
    sd[...] = pick(place.even[1], low, high)


def sweep_limits(levels, level_sweeps):
    block = lane_ids(BS) // BS
    limit = jnp.zeros((BS, LANES), jnp.int32)
    for b in range(BLK):
        limit = jnp.where(block == b, level_sweeps[levels[b]], limit)
    return limit.astype(F32)


def relax(limit, r, e, f0, fy, fzs, d, finish):
    def sweep(i, load, store):
        active = limit > float(i)

        t0, here = ZERO(), load(plane(0))
        for x in range(BS):
            at = plane(x)
            after = load(after_plane(x))
            w0, wy, wz = f0[at, :], fy[at, :], fzs[at, :]
            t1 = w0 * here
            total = r[at, :] + t0 + w0 * after
            total = total + wy * next_y(here) + prev_y(wy * here)
            total = total + wz * next_z(here) + prev_z(wz * here)
            store(at, jnp.where(active, KEEP * here + d[at, :] * total, here))
            t0, here = t1, after

    def first(at):
        return d[at, :] * r[at, :]

    def held(at):
        return e[at, :]

    def keep(at, value):
        e[at, :] = value

    sweep(1, first, keep)
    for i in range(2, SWEEP_MAX - 1):
        sweep(i, held, keep)
    sweep(SWEEP_MAX - 1, held, finish)


def first_kernel(
    limit, src, f0, fy, fzs, c0, fx, fyf, ra, rb, rc, rd,
    c, d, gx, gy, p, sa, sb, sc, sd, e,
):
    def natural(ref):
        return jnp.concatenate([ref[pl.ds(k, 8, stride=4), :] for k in range(4)], axis=0)

    place = Place()
    xlo, xhi = low_high(place, 1, natural(rc), natural(rd))
    ylo, yhi = low_high(place, 0, ra[...], rb[...])
    gx[0:BS, :] = 0.5 * (fx[0:BS, :] + xlo)
    gx[BS : 2 * BS, :] = 0.5 * (fx[BS : 2 * BS, :] + xhi)
    gy[0:BS, :] = 0.5 * (fyf[0:BS, :] + ylo)
    gy[BS : 2 * BS, :] = 0.5 * (fyf[BS : 2 * BS, :] + yhi)
    add_faces_x(c, 0.5 * xlo, 0.5 * xhi)
    add_faces_y(c, 0.5 * ylo, 0.5 * yhi)

    for x in range(BS):
        at = plane(x)
        d[at, :] = RELAX / c[at, :]

    def finish(at, value):
        p[at, :] = value

    relax(limit[...], src, e, f0, fy, fzs, d, finish)
    send_faces(place, p, sa, sb, sc, sd)


def residual_plane(src, c, f0, fy, fz, at, t0, here, after):
    w0, wy, wz = f0[at, :], fy[at, :], fz[at, :]
    total = src[at, :] - c[at, :] * here + t0 + w0 * after
    total = total + wy * next_y(here) + prev_y(wy * here)
    total = total + wz * next_z(here) + prev_z(wz * here)
    return total, w0 * here


def coarse_rhs_kernel(src, c, f0, fy, fz, p, q, scr):
    t0, here = ZERO(), p[0:BS, :]
    for xc in range(XC):
        total = jnp.zeros((8, LANES), F32)
        for j in range(4):
            x = xc * 4 + j
            after = p[after_plane(x), :]
            r, t0 = residual_plane(src, c, f0, fy, fz, plane(x), t0, here, after)
            total = total + fold(r)
            here = after
        scr[8 * xc : 8 * xc + 8, :] = total
    q[...] = group_sum(scr[...], group_matrix()) * PART


def coarse_weights_kernel(f0, fy, gx, gy, czu, czd, packed, scr, cy):
    ones = group_matrix()
    lane = lane_ids(CROWS)
    row = row_ids(CROWS)
    for xc in range(XC):
        scr[8 * xc : 8 * xc + 8, :] = fold(f0[(4 * xc + 3) * BS : (4 * xc + 4) * BS, :])
        total = fy[4 * xc * BS + 24 : 4 * xc * BS + 32, :]
        for j in range(1, 4):
            at = (4 * xc + j) * BS
            total = total + fy[at + 24 : at + 32, :]
        cy[8 * xc : 8 * xc + 8, :] = total
    c0 = group_sum(scr[...], ones) * PART
    cy[pl.ds(7, 8, stride=8), :] = by_fours(gy, BS)
    up_y = group_sum(cy[...], ones) * PART
    gxlo = group_sum(fold(gx[0:BS, :]), ones) * PART
    gxhi = group_sum(fold(gx[BS : 2 * BS, :]), ones) * PART
    up_z = group_sum(jnp.where(lane % 4 == 3, czu[...], 0.0), ones) * PART
    down_z = group_sum(jnp.where(lane % 4 == 0, czd[...], 0.0), ones) * PART
    up_0 = jnp.concatenate([c0[0 : CROWS - 8], gxhi], axis=0)
    down_0 = jnp.concatenate([gxlo, c0[0 : CROWS - 8]], axis=0)
    cy[...] = jnp.concatenate(
        [pltpu.roll(up_y[8 * xc : 8 * xc + 8], 1, 0) for xc in range(XC)], axis=0
    )
    cy[pl.ds(0, 8, stride=8), :] = group_sum(by_fours(gy, 0), ones) * PART
    scale = RELAX / (up_0 + up_y + up_z + down_0 + cy[...] + down_z)
    couple_y = jnp.where(row % 8 == 7, up_y * Place().high[0].astype(F32), up_y)
    couple_z = jnp.where(lane >= LANES - 4, 0.0, up_z)
    slot = lane % 4
    packed[...] = jnp.where(
        slot == 0, c0, jnp.where(slot == 1, couple_y, jnp.where(slot == 2, couple_z, scale))
    )


def coarse_faces_kernel(qi, gx, gy, ra, rc, rd, sb, *rest):
    packed, (ma, mb, scr) = rest[:-3], rest[-3:]
    place = Place()
    xlo, xhi = low_high(place, 1, rc[...], rd[...])
    even = place.even[0]
    own = jnp.where(jnp.full(ra.shape, even.astype(jnp.int32)) == 1, gy[BS : 2 * BS, :], gy[0:BS, :])
    scr[...] = own * ra[...]
    faces = jnp.concatenate(
        [fold(gx[0:BS, :] * xlo), fold(gx[BS : 2 * BS, :] * xhi), by_fours(scr, 0)], axis=0
    )
    faces = group_sum(faces, group_matrix()) * PART
    ma[0:CROWS, :] = qi[...]
    ma[0:8, :] = ma[0:8, :] + faces[0:8]
    ma[CROWS - 8 : CROWS, :] = ma[CROWS - 8 : CROWS, :] + faces[8:16]
    nothing = jnp.zeros((8, LANES), F32)
    at = pl.ds(0, 8, stride=8)
    ma[at, :] = ma[at, :] + pick(even, nothing, faces[16:24])
    at = pl.ds(7, 8, stride=8)
    ma[at, :] = ma[at, :] + pick(even, faces[16:24], nothing)
    mb[0:CROWS, :] = ma[0:CROWS, :]
    mb[CROWS : CROWS + BS, :] = sb[...]
    for w in packed:
        ma[CROWS : 2 * CROWS, :] = w[...]
        mb[CROWS + BS : 2 * CROWS + BS, :] = w[...]


def joined(place, own, first, second):
    low, high = low_high(place, 0, first, second)
    parts = []
    for xc in range(XC):
        at = slice(8 * xc, 8 * xc + 8)
        parts += [low[at], own[at], high[at]]
    return jnp.concatenate(parts, axis=0)


def coarse_solve(place, ma, qa, qb, sb, gy, weights, c, cyb, sa, sc, sd, scr, two):
    even = place.even[0]
    w0, wy, wz, scale = weights
    scr[...] = joined(place, ma[0:CROWS, :], qa[0:CROWS, :], qb[0:CROWS, :])
    side = pick(even, gy[0:BS, :], gy[BS : 2 * BS, :])
    there = jnp.where(even, place.low[0].astype(F32), place.high[0].astype(F32))
    two[0:BS, :] = side * qb[CROWS : CROWS + BS, :] * there
    two[BS : 2 * BS, :] = side * sb[...]
    faces = jnp.concatenate([by_fours(two, 0), by_fours(two, BS)], axis=0)
    faces = group_sum(faces, group_matrix()) * PART
    mine, theirs = faces[0:8], faces[8:16]
    nothing = jnp.zeros((8, LANES), F32)
    for row, value in (
        (8, pick(even, mine, nothing)),
        (7, pick(even, theirs, nothing)),
        (15, pick(even, nothing, mine)),
        (16, pick(even, nothing, theirs)),
    ):
        at = pl.ds(row, 8, stride=24)
        scr[at, :] = scr[at, :] + value
    rhs = scr[...]

    def up_x(v):
        return jnp.concatenate([v[24:], v[:24]], axis=0)

    def down_x(v):
        return jnp.concatenate([v[-24:], v[:-24]], axis=0)

    def by_plane(v, shift):
        return jnp.concatenate(
            [pltpu.roll(v[24 * xc : 24 * xc + 24], shift, 0) for xc in range(XC)], axis=0
        )

    field = scale * rhs
    for _ in range(CSWEEPS - 1):
        total = rhs + w0 * up_x(field) + down_x(w0 * field)
        total = total + wy * by_plane(field, 23) + by_plane(wy * field, 1)
        total = total + wz * pltpu.roll(field, LANES - 4, 1) + pltpu.roll(wz * field, 4, 1)
        field = KEEP * field + scale * total
    scr[...] = field
    for xc in range(XC):
        c[8 * xc : 8 * xc + 8, :] = field[24 * xc + 8 : 24 * xc + 16]
    cyb[...] = pick(even, scr[pl.ds(7, 8, stride=24), :], scr[pl.ds(16, 8, stride=24), :])
    sa[...] = pick(even, scr[pl.ds(15, 8, stride=24), :], scr[pl.ds(8, 8, stride=24), :])
    low, high = field[8:16], field[24 * 7 + 8 : 24 * 7 + 16]
    sc[...] = pick(place.even[1], high, low)
    sd[...] = pick(place.even[1], low, high)


def first_coarse_kernel(ma, qa, qb, sb, gy, c, cyb, sa, sc, sd, wide, scr, two):
    place = Place()
    packed = joined(
        place, ma[CROWS : 2 * CROWS, :], qa[CROWS : 2 * CROWS, :], qb[CROWS + BS :, :]
    )
    ones = group_matrix()
    slot = lane_ids(3 * CROWS) % 4
    weights = [group_sum(jnp.where(slot == j, packed, 0.0), ones) for j in range(4)]
    for j in range(4):
        wide[3 * CROWS * j : 3 * CROWS * (j + 1), :] = weights[j]
    coarse_solve(place, ma, qa, qb, sb, gy, weights, c, cyb, sa, sc, sd, scr, two)


def later_coarse_kernel(ma, qa, qb, sb, gy, wide, c, cyb, sa, sc, sd, scr, two):
    weights = [wide[3 * CROWS * j : 3 * CROWS * (j + 1), :] for j in range(4)]
    coarse_solve(Place(), ma, qa, qb, sb, gy, weights, c, cyb, sa, sc, sd, scr, two)


def spread_rows(scr, value):
    for j in range(4):
        scr[pl.ds(j, 8, stride=4), :] = value
    return scr[...]


def correct_kernel(src, c, f0, fy, fz, p, gy, qb, cc, cyb, p2, r, scr):
    def corrected(x):
        return p[plane(x), :] + tiled(cc[8 * (x // 4) : 8 * (x // 4) + 8, :])

    t0, here = ZERO(), corrected(0)
    for x in range(BS):
        at = plane(x)
        after = corrected(min(x + 1, BS - 1))
        p2[at, :] = here
        r[at, :], t0 = residual_plane(src, c, f0, fy, fz, at, t0, here, after)
        here = after
    halo = qb[CROWS : CROWS + BS, :] + spread_rows(scr, cyb[...])
    ylo, yhi = low_high(Place(), 0, ZERO(), halo)
    add_faces_y(r, gy[0:BS, :] * ylo, gy[BS : 2 * BS, :] * yhi)


def residual_kernel(src, c, f0, fy, fz, p, r):
    t0, here = ZERO(), p[0:BS, :]
    for x in range(BS):
        at = plane(x)
        after = p[after_plane(x), :]
        r[at, :], t0 = residual_plane(src, c, f0, fy, fz, at, t0, here, after)
        here = after


def add_all(place, gx, gy, ra, rb, rc, rd, ref):
    xlo, xhi = low_high(place, 1, rc, rd)
    add_faces_x(ref, gx[0:BS, :] * xlo, gx[BS : 2 * BS, :] * xhi)
    ylo, yhi = low_high(place, 0, ra, rb)
    add_faces_y(ref, gy[0:BS, :] * ylo, gy[BS : 2 * BS, :] * yhi)


def finish_smooth(place, limit, r, f0, fy, fzs, d, p, p_out, sends, e):
    def finish(at, value):
        p_out[at, :] = p[at, :] + value

    relax(limit, r, e, f0, fy, fzs, d, finish)
    send_faces(place, p_out, *sends)


def smooth_corrected_kernel(
    ri, limit, f0, fy, fzs, d, p, gx, gy, ra, rc, rd, ka, kc, kd,
    r, p_out, sa, sb, sc, sd, e, scr,
):
    place = Place()
    near = ra[...] + spread_rows(scr, ka[...])
    add_all(place, gx, gy, near, ZERO(), rc[...] + tiled(kc[...]), rd[...] + tiled(kd[...]), r)
    finish_smooth(place, limit[...], r, f0, fy, fzs, d, p, p_out, (sa, sb, sc, sd), e)


def smooth_kernel(
    ri, limit, f0, fy, fzs, d, p, gx, gy, ra, rb, rc, rd,
    r, p_out, sa, sb, sc, sd, e,
):
    place = Place()
    add_all(place, gx, gy, ra[...], rb[...], rc[...], rd[...], r)
    finish_smooth(place, limit[...], r, f0, fy, fzs, d, p, p_out, (sa, sb, sc, sd), e)


def plane_to_blocks(v, x, out, base):
    lane = lane_ids(8)
    half = lane < 64
    even = (lane // BS) % 2 == 0
    v = [v[8 * k : 8 * k + 8] for k in range(4)]
    u = [None] * 4
    for k in range(2):
        low, high = v[k], v[k + 2]
        u[k] = jnp.where(half, low, pltpu.roll(high, 64, 1))
        u[k + 2] = jnp.where(half, pltpu.roll(low, 64, 1), high)
    for b in (0, 2):
        low, high = u[b], u[b + 1]
        first = jnp.where(even, low, pltpu.roll(high, BS, 1))
        second = jnp.where(even, pltpu.roll(low, LANES - BS, 1), high)
        at = base + b * STEP + x * 8
        out[at : at + 8, :] = first
        out[at + STEP : at + STEP + 8, :] = second


def pressure_blocks_kernel(p, blocks):
    for x in range(BS):
        plane_to_blocks(p[plane(x), :], x, blocks, BLK * STEP)


def final_kernel(ri, gx, gy, ra, rb, rc, rd, pblocks, r, blocks, sa, sb):
    place = Place()
    add_all(place, gx, gy, ra[...], rb[...], rc[...], rd[...], r)

    for x in range(BS):
        plane_to_blocks(r[plane(x), :], x, blocks, BLK * STEP)
    send_blocks_kernel(pblocks, blocks, sa, sb, count=1)


def send_blocks_kernel(pblocks, blocks, sa, sb, *, count):
    even = Place().even[0]
    for n, ref in enumerate((pblocks, blocks)):
        for b in range(count):
            for t in range(0, 256, 32):
                low = (BLK + b) * STEP + t
                high = (2 * BLK - count + b) * STEP + t
                low, high = ref[low : low + 32, :], ref[high : high + 32, :]
                at = slice((n * count + b) * 256 + t, (n * count + b) * 256 + t + 32)
                sa[at, :] = pick(even, high, low)
                sb[at, :] = pick(even, low, high)


def place_kernel(owned, in_p, in_r, ra, rb, out_p, out_r, seq_p, seq_r, held_p, held_r, sems, *, count):
    place = Place()
    even = place.even[0]
    start = jnp.max(owned[0:8, :]).astype(jnp.int32)
    base = jnp.clip(start - place.device * BLK + BLK, 0, 2 * BLK) * STEP
    valid = row_ids(8).astype(F32) < owned[8:16, :]
    copies = []
    fields = ((seq_p, held_p, out_p), (seq_r, held_r, out_r))
    for n, (seq, tiles, out) in enumerate(fields):
        for b in range(count):
            for t in range(0, 256, 32):
                at = slice((n * count + b) * 256 + t, (n * count + b) * 256 + t + 32)
                low, high = (BLK - count + b) * STEP + t, (2 * BLK + b) * STEP + t
                seq[low : low + 32, :] = pick(even, rb[at, :], ra[at, :])
                seq[high : high + 32, :] = pick(even, ra[at, :], rb[at, :])
        for part in range(PIECES):
            for t in range(part * PIECE, (part + 1) * PIECE):
                rows = seq[pl.ds(base + t, 8, stride=STEP), :]
                tiles[t, :, :] = jnp.where(valid, rows, 0.0)[0:CAP]
            at = pl.ds(part * PIECE, PIECE)
            copy = pltpu.make_async_copy(tiles.at[at], out.at[at], sems.at[n, part])
            copy.start()
            copies.append(copy)
    for copy in copies:
        copy.wait()


BOTH = ("region", "member")


def swap_near(value):
    return lax.ppermute(value, "member", [(i, i ^ 1) for i in range(lax.axis_size("member"))])


def swap_far(value):
    regions, members = lax.axis_size("region"), lax.axis_size("member")
    pairs = []
    for r in range(regions):
        for m in range(members):
            other = m + 1 if m % 2 else m - 1
            inside = 0 <= other < members
            target = r * members + other if inside else (r ^ 1) * members + m
            pairs.append((r * members + m, target))
    return lax.ppermute(value, BOTH, pairs)


def swap_regions(inner, outer):
    regions, members = lax.axis_size("region"), lax.axis_size("member")
    pairs = []
    for r in range(regions):
        other = r + 1 if r % 2 else r - 1
        inside = 0 <= other < regions
        for m in range(members):
            target = other * members + m if inside else r * members + (m ^ 1)
            pairs.append((r * members + m, target))
    inner = lax.ppermute(inner, "region", [(i, i ^ 1) for i in range(regions)])
    return inner, lax.ppermute(outer, BOTH, pairs)


def swap_blocks(first, second):
    count = lax.axis_size(BOTH)
    inner = [(i, i ^ 1) for i in range(count)]
    outer = [(i, (i + 1) % count if i % 2 else (i - 1) % count) for i in range(count)]
    return lax.ppermute(first, BOTH, inner), lax.ppermute(second, BOTH, outer)


def swap_faces(sa, sb, sc, sd):
    return (swap_near(sa), swap_far(sb), *swap_regions(sc, sd))


FULL, TWO, CFIELD = (ROWS, LANES), (2 * BS, LANES), (CROWS, LANES)
FACE, CFACE = (BS, LANES), (8, LANES)
ROW = ((2 * BLK + 8) * STEP, LANES)


def set_up(levels, new_owner, src, inv):
    outs = [jax.ShapeDtypeStruct((16, LANES), F32), jax.ShapeDtypeStruct((1,), jnp.int32)] + [
        jax.ShapeDtypeStruct(s, F32) for s in [FULL] * 6 + [TWO] * 2 + [CFIELD] * 2 + [FACE]
    ]
    vm, sm = pl.BlockSpec(memory_space=pltpu.VMEM), pl.BlockSpec(memory_space=pltpu.SMEM)
    return pl.pallas_call(
        weights_kernel,
        out_shape=outs,
        in_specs=[sm] * 2 + [vm] * 3,
        out_specs=[vm, sm] + [vm] * 11,
        compiler_params=pltpu.CompilerParams(vmem_limit_bytes=48 << 20),
        cost_estimate=pl.CostEstimate(flops=4000000, bytes_accessed=6 << 20, transcendentals=0),
    )(*levels, new_owner.reshape(-1, min(LANES, new_owner.size)), src, inv)


def faces_kernel(inv, sa, sb, sc, sd, sems):
    place = Place()
    low, high = (0, BS - 1)

    def copies(first, second, axis):
        if axis == 0:
            pair = ((inv.at[1, :, first, :], sa), (inv.at[1, :, second, :], sb))
        else:
            pair = ((inv.at[0, first], sc), (inv.at[0, second], sd))
        return [
            pltpu.make_async_copy(source, to, sems.at[2 * axis + n])
            for n, (source, to) in enumerate(pair)
        ]

    for axis in range(2):

        @pl.when(place.even[axis])
        def _():
            for copy in copies(high, low, axis):
                copy.start()

        @pl.when(jnp.logical_not(place.even[axis]))
        def _():
            for copy in copies(low, high, axis):
                copy.start()

    for axis in range(2):
        for copy in copies(low, high, axis):
            copy.wait()


def density_faces(inverse_density):
    return pl.pallas_call(
        faces_kernel,
        out_shape=[jax.ShapeDtypeStruct(FACE, F32)] * 4,
        in_specs=[pl.BlockSpec(memory_space=pl.ANY)],
        out_specs=[pl.BlockSpec(memory_space=pl.ANY)] * 4,
        scratch_shapes=[pltpu.SemaphoreType.DMA((4,))],
        cost_estimate=pl.CostEstimate(flops=2000000000, bytes_accessed=131072, transcendentals=0),
    )(inverse_density)


def place_blocks(count, owned, *arrays):
    slots, row = (256, CAP, LANES), ROW
    vm = pl.BlockSpec(memory_space=pltpu.VMEM)
    anywhere = pl.BlockSpec(memory_space=pl.ANY)
    outs = pl.pallas_call(
        functools.partial(place_kernel, count=count),
        out_shape=[jax.ShapeDtypeStruct(shape, F32) for shape in (slots, slots, row, row)],
        in_specs=[vm] * 5,
        out_specs=[anywhere] * 2 + [vm] * 2,
        scratch_shapes=[vmem(*slots), vmem(*slots), pltpu.SemaphoreType.DMA((2, PIECES))],
        input_output_aliases={1: 2, 2: 3},
        compiler_params=pltpu.CompilerParams(vmem_limit_bytes=48 << 20),
        cost_estimate=pl.CostEstimate(flops=2000000, bytes_accessed=6 << 20, transcendentals=0),
    )(owned, *arrays)
    return tuple(o.transpose(1, 0, 2).reshape(CAP, 256 * LANES) for o in outs[:2])


def on_device(source, inverse_density, block_level, level_sweeps, new_owner):
    levels = (block_level, level_sweeps)
    halos = swap_faces(*density_faces(inverse_density))
    owned, most, src, f0, fy, fz, fzs, c0, fx, fyf, czu, czd, limit = set_up(
        levels, new_owner, source.reshape(ROWS, LANES), inverse_density.reshape(3 * ROWS, LANES)
    )
    c, d, gx, gy, p, *sends = call(
        first_kernel,
        [FULL, FULL, TWO, TWO, FULL] + [FACE] * 4,
        [limit, src, f0, fy, fzs, c0, fx, fyf, *halos],
        (),
        [vmem(*FULL)],
        {5: 0},
    )
    fine = [src, c, f0, fy, fz]
    wide = None
    for cycle in range(CYCLES):
        if cycle > 0:
            halos = swap_faces(*sends)
            (ri,) = call(residual_kernel, [FULL], [*fine, p])
            _, p, *sends = call(
                smooth_kernel,
                [FULL, FULL] + [FACE] * 4,
                [ri, limit, f0, fy, fzs, d, p, gx, gy, *halos],
                (),
                [vmem(*FULL)],
                {0: 0},
            )
        sa, sb, sc, sd = sends
        ra = swap_near(sa)
        rc, rd = swap_regions(sc, sd)
        (qi,) = call(coarse_rhs_kernel, [CFIELD], [*fine, p], scratch=[vmem(*CFIELD)])
        packed, rows = [], CROWS
        if wide is None:
            packed = call(
                coarse_weights_kernel,
                [CFIELD],
                [f0, fy, gx, gy, czu, czd],
                scratch=[vmem(*CFIELD)] * 2,
            )
            rows = 2 * CROWS
        ma, mb = call(
            coarse_faces_kernel,
            [(rows, LANES), (rows + BS, LANES)],
            [qi, gx, gy, ra, rc, rd, sb, *packed],
            scratch=[vmem(*FACE)],
        )
        qa, qb = swap_near(ma), swap_far(mb)
        outs = [CFIELD] + [CFACE] * 4
        arrays = [ma, qa, qb, sb, gy]
        scratch = [vmem(3 * CROWS, LANES), vmem(*TWO)]
        if wide is None:
            cc, cyb, ta, tc, td, wide = call(
                first_coarse_kernel, outs + [(12 * CROWS, LANES)], arrays, scratch=scratch
            )
        else:
            cc, cyb, ta, tc, td = call(later_coarse_kernel, outs, [*arrays, wide], scratch=scratch)
        ka = swap_near(ta)
        kc, kd = swap_regions(tc, td)
        p, ri = call(
            correct_kernel, [FULL, FULL], [*fine, p, gy, qb, cc, cyb], scratch=[vmem(*FACE)]
        )
        _, p, *sends = call(
            smooth_corrected_kernel,
            [FULL, FULL] + [FACE] * 4,
            [ri, limit, f0, fy, fzs, d, p, gx, gy, ra, rc, rd, ka, kc, kd],
            (),
            [vmem(*FULL), vmem(*FACE)],
            {0: 0},
        )

    halos = swap_faces(*sends)
    (ri,) = call(residual_kernel, [FULL], [*fine, p])
    (blocks_p,) = call(pressure_blocks_kernel, [ROW], [p])
    _, blocks_r, sa, sb = call(
        final_kernel,
        [FULL, ROW] + [(512, LANES)] * 2,
        [ri, gx, gy, *halos, blocks_p],
        aliases={0: 0},
    )

    def one(owned, blocks_p, blocks_r, sa, sb):
        return place_blocks(1, owned, blocks_p, blocks_r, *swap_blocks(sa, sb))

    def several(owned, blocks_p, blocks_r, sa, sb):
        body = functools.partial(send_blocks_kernel, count=BLK)
        sends = call(body, [(2 * BLK * 256, LANES)] * 2, [blocks_p, blocks_r])
        return place_blocks(BLK, owned, blocks_p, blocks_r, *swap_blocks(*sends))

    return lax.cond(most.reshape(()) <= 1, one, several, owned, blocks_p, blocks_r, sa, sb)


def solution(mesh):
    placed = (
        P("region", "member", None),
        P(None, "region", "member", None),
        P(("region", "member")),
        P(),
        P(),
    )
    return jax.shard_map(
        on_device,
        mesh=mesh,
        in_specs=placed,
        out_specs=(P(("region", "member"), None), P(("region", "member"), None)),
        check_vma=False,
    )
```

```python
import functools

import jax
import jax.numpy as jnp
from jax import lax
from jax.experimental import pallas as pl
from jax.experimental.pallas import tpu as pltpu
from jax.sharding import PartitionSpec as P


BS = 32
BLK = 4
CSWEEPS = 8
CYCLES = 2
CAP = 6
SWEEP_MAX = 6
RELAX = 0.8
KEEP = 0.2
PART = 1.0 / 64.0
PIECES = 4
PIECE = 256 // PIECES
STEP = 264
LANES = 128
ROWS = BS * BS
XC = BS // 4
CROWS = XC * XC
ZERO = functools.partial(jnp.zeros, (BS, LANES), jnp.float32)
F32 = jnp.float32


def vmem(*shape):
    return pltpu.VMEM(shape, F32)


def call(body, out_rows, args, scalars=(), scratch=(), aliases=None, flops=2e6, mib=48):
    outs = [jax.ShapeDtypeStruct(s, F32) for s in out_rows]
    moved = sum(a.size * 4 for a in args) + sum(o.size * 4 for o in outs)
    return pl.pallas_call(
        body,
        out_shape=outs,
        in_specs=[pl.BlockSpec(memory_space=pltpu.SMEM)] * len(scalars)
        + [pl.BlockSpec(memory_space=pltpu.VMEM)] * len(args),
        out_specs=[pl.BlockSpec(memory_space=pltpu.VMEM)] * len(outs),
        scratch_shapes=list(scratch),
        input_output_aliases={len(scalars) + k: v for k, v in (aliases or {}).items()},
        compiler_params=pltpu.CompilerParams(vmem_limit_bytes=mib << 20),
        cost_estimate=pl.CostEstimate(flops=int(flops), bytes_accessed=int(moved), transcendentals=0),
    )(*scalars, *args)


class Place:
    def __init__(self):
        region, member = lax.axis_index("region"), lax.axis_index("member")
        self.device = region * lax.axis_size("member") + member
        self.even = (member % 2 == 0, region % 2 == 0)
        self.low = (member > 0, region > 0)
        self.high = (member < lax.axis_size("member") - 1, region < lax.axis_size("region") - 1)


def lane_ids(rows):
    return lax.broadcasted_iota(jnp.int32, (rows, LANES), 1)


def row_ids(rows):
    return lax.broadcasted_iota(jnp.int32, (rows, LANES), 0)


def next_y(v):
    return jnp.concatenate([v[8:32], pltpu.roll(v[0:8], 7, 0)], axis=0)


def prev_y(v):
    return jnp.concatenate([pltpu.roll(v[24:32], 1, 0), v[0:24]], axis=0)


def next_z(v):
    return pltpu.roll(v, LANES - 1, 1)


def prev_z(v):
    return pltpu.roll(v, 1, 1)


def fold(v):
    return v[0:8] + v[8:16] + v[16:24] + v[24:32]


def tiled(v):
    return jnp.concatenate([v, v, v, v], axis=0)


def plane(x):
    return slice(x * BS, (x + 1) * BS)


def after_plane(x):
    return plane(min(x + 1, BS - 1))


def pick(flag, yes, no):
    return jnp.where(jnp.full(yes.shape, flag.astype(jnp.int32), jnp.int32) == 1, yes, no)


def low_high(place, axis, first, second):
    low = pick(place.even[axis], second, first) * place.low[axis].astype(F32)
    high = pick(place.even[axis], first, second) * place.high[axis].astype(F32)
    return low, high


def group_matrix():
    return jnp.where(
        row_ids(LANES) // 4 == lane_ids(LANES) // 4, jnp.float32(1.0), jnp.float32(0.0)
    )


def group_sum(v, ones):
    return lax.dot_general(
        v, ones, (((1,), (0,)), ((), ())), precision=lax.Precision.HIGHEST, preferred_element_type=F32
    )


def by_fours(ref, base):
    total = ref[pl.ds(base, 8, stride=4), :]
    for j in range(1, 4):
        total = total + ref[pl.ds(base + j, 8, stride=4), :]
    return total


def weights_kernel(
    levels, level_sweeps, new_owner, src, inv,
    owned, most, src_t, f0, fy, fz, fzs, c0, fx, fyf, czu, czd, limit,
):
    row, lane = row_ids(BS), lane_ids(BS)

    def load(ref, x, offset):
        return jnp.concatenate(
            [ref[pl.ds(offset + x * BS + k, 8, stride=4), :] for k in range(4)], axis=0
        )

    before, here = ZERO(), load(inv, 0, 0)
    for xc in range(XC):
        total_up = jnp.zeros((8, LANES), F32)
        total_down = jnp.zeros((8, LANES), F32)
        for j in range(4):
            x = xc * 4 + j
            src_t[plane(x), :] = load(src, x, 0)
            after = load(inv, x + 1, 0) if x < BS - 1 else ZERO()
            one = load(inv, x, ROWS)
            two = load(inv, x, 2 * ROWS)
            one_n = jnp.where(row == BS - 1, 0.0, next_y(one))
            one_p = jnp.where(row == 0, 0.0, prev_y(one))
            two_n = jnp.where(lane == LANES - 1, 0.0, next_z(two))
            two_p = jnp.where(lane == 0, 0.0, prev_z(two))
            up0 = 0.5 * (here + after)
            upy = 0.5 * (one + one_n)
            upz = 0.5 * (two + two_n)
            downz = 0.5 * (two + two_p)
            f0[plane(x), :] = up0 if x < BS - 1 else ZERO()
            fy[plane(x), :] = jnp.where(row == BS - 1, 0.0, upy)
            fz[plane(x), :] = jnp.where(lane == LANES - 1, 0.0, upz)
            fzs[plane(x), :] = jnp.where(lane % BS == BS - 1, 0.0, upz)
            c0[plane(x), :] = up0 + upy + upz + 0.5 * (here + before) + 0.5 * (one + one_p) + downz
            total_up = total_up + fold(upz)
            total_down = total_down + fold(downz)
            before, here = here, after
        czu[8 * xc : 8 * xc + 8, :] = total_up
        czd[8 * xc : 8 * xc + 8, :] = total_down
    fx[0:BS, :] = load(inv, 0, 0)
    fx[BS : 2 * BS, :] = load(inv, BS - 1, 0)
    for g in range(4):
        fyf[8 * g : 8 * g + 8, :] = inv[pl.ds(ROWS + 256 * g, 8, stride=BS), :]
        fyf[BS + 8 * g : BS + 8 * g + 8, :] = inv[pl.ds(ROWS + 256 * g + 31, 8, stride=BS), :]
    limit[...] = sweep_limits(levels, level_sweeps)
    device = Place().device
    owner = new_owner[...]
    block = lax.broadcasted_iota(jnp.int32, owner.shape, 0) * owner.shape[1]
    block = block + lax.broadcasted_iota(jnp.int32, owner.shape, 1)
    home, place = block // BLK, block % BLK
    leaving = jnp.where(owner > home, BLK - place, jnp.where(owner < home, place + 1, 0))
    owned[0:8, :] = jnp.full((8, LANES), jnp.sum((owner < device).astype(F32)))
    owned[8:16, :] = jnp.full((8, LANES), jnp.sum((owner == device).astype(F32)))
    most[0] = jnp.max(leaving.astype(F32)).astype(jnp.int32)


def add_faces_y(ref, low, high):
    for g in range(4):
        at = pl.ds(256 * g, 8, stride=BS)
        ref[at, :] = ref[at, :] + low[8 * g : 8 * g + 8]
        at = pl.ds(256 * g + 31, 8, stride=BS)
        ref[at, :] = ref[at, :] + high[8 * g : 8 * g + 8]


def add_faces_x(ref, low, high):
    ref[0:BS, :] = ref[0:BS, :] + low
    ref[ROWS - BS : ROWS, :] = ref[ROWS - BS : ROWS, :] + high


def send_faces(place, p, sa, sb, sc, sd):
    even = place.even[0]
    for g in range(4):
        low = p[pl.ds(256 * g, 8, stride=BS), :]
        high = p[pl.ds(256 * g + 31, 8, stride=BS), :]
        sa[8 * g : 8 * g + 8, :] = pick(even, high, low)
        sb[8 * g : 8 * g + 8, :] = pick(even, low, high)
    low = p[0:BS, :]
    high = p[ROWS - BS : ROWS, :]
    sc[...] = pick(place.even[1], high, low)
    sd[...] = pick(place.even[1], low, high)


def sweep_limits(levels, level_sweeps):
    block = lane_ids(BS) // BS
    limit = jnp.zeros((BS, LANES), jnp.int32)
    for b in range(BLK):
        limit = jnp.where(block == b, level_sweeps[levels[b]], limit)
    return limit.astype(F32)


def relax(limit, r, e, f0, fy, fzs, d, finish):
    def sweep(i, load, store):
        active = limit > float(i)

        t0, here = ZERO(), load(plane(0))
        for x in range(BS):
            at = plane(x)
            after = load(after_plane(x))
            w0, wy, wz = f0[at, :], fy[at, :], fzs[at, :]
            t1 = w0 * here
            total = r[at, :] + t0 + w0 * after
            total = total + wy * next_y(here) + prev_y(wy * here)
            total = total + wz * next_z(here) + prev_z(wz * here)
            store(at, jnp.where(active, KEEP * here + d[at, :] * total, here))
            t0, here = t1, after

    def first(at):
        return d[at, :] * r[at, :]

    def held(at):
        return e[at, :]

    def keep(at, value):
        e[at, :] = value

    sweep(1, first, keep)
    for i in range(2, SWEEP_MAX - 1):
        sweep(i, held, keep)
    sweep(SWEEP_MAX - 1, held, finish)


def first_kernel(
    limit, src, f0, fy, fzs, c0, fx, fyf, ra, rb, rc, rd,
    c, d, gx, gy, p, sa, sb, sc, sd, e,
):
    def natural(ref):
        return jnp.concatenate([ref[pl.ds(k, 8, stride=4), :] for k in range(4)], axis=0)

    place = Place()
    xlo, xhi = low_high(place, 1, natural(rc), natural(rd))
    ylo, yhi = low_high(place, 0, ra[...], rb[...])
    gx[0:BS, :] = 0.5 * (fx[0:BS, :] + xlo)
    gx[BS : 2 * BS, :] = 0.5 * (fx[BS : 2 * BS, :] + xhi)
    gy[0:BS, :] = 0.5 * (fyf[0:BS, :] + ylo)
    gy[BS : 2 * BS, :] = 0.5 * (fyf[BS : 2 * BS, :] + yhi)
    add_faces_x(c, 0.5 * xlo, 0.5 * xhi)
    add_faces_y(c, 0.5 * ylo, 0.5 * yhi)

    for x in range(BS):
        at = plane(x)
        d[at, :] = RELAX / c[at, :]

    def finish(at, value):
        p[at, :] = value

    relax(limit[...], src, e, f0, fy, fzs, d, finish)
    send_faces(place, p, sa, sb, sc, sd)


def residual_plane(src, c, f0, fy, fz, at, t0, here, after):
    w0, wy, wz = f0[at, :], fy[at, :], fz[at, :]
    total = src[at, :] - c[at, :] * here + t0 + w0 * after
    total = total + wy * next_y(here) + prev_y(wy * here)
    total = total + wz * next_z(here) + prev_z(wz * here)
    return total, w0 * here


def coarse_rhs_kernel(src, c, f0, fy, fz, p, q, scr):
    t0, here = ZERO(), p[0:BS, :]
    for xc in range(XC):
        total = jnp.zeros((8, LANES), F32)
        for j in range(4):
            x = xc * 4 + j
            after = p[after_plane(x), :]
            r, t0 = residual_plane(src, c, f0, fy, fz, plane(x), t0, here, after)
            total = total + fold(r)
            here = after
        scr[8 * xc : 8 * xc + 8, :] = total
    q[...] = group_sum(scr[...], group_matrix()) * PART


def coarse_weights_kernel(f0, fy, gx, gy, czu, czd, packed, scr, cy):
    ones = group_matrix()
    lane = lane_ids(CROWS)
    row = row_ids(CROWS)
    for xc in range(XC):
        scr[8 * xc : 8 * xc + 8, :] = fold(f0[(4 * xc + 3) * BS : (4 * xc + 4) * BS, :])
        total = fy[4 * xc * BS + 24 : 4 * xc * BS + 32, :]
        for j in range(1, 4):
            at = (4 * xc + j) * BS
            total = total + fy[at + 24 : at + 32, :]
        cy[8 * xc : 8 * xc + 8, :] = total
    c0 = group_sum(scr[...], ones) * PART
    cy[pl.ds(7, 8, stride=8), :] = by_fours(gy, BS)
    up_y = group_sum(cy[...], ones) * PART
    gxlo = group_sum(fold(gx[0:BS, :]), ones) * PART
    gxhi = group_sum(fold(gx[BS : 2 * BS, :]), ones) * PART
    up_z = group_sum(jnp.where(lane % 4 == 3, czu[...], 0.0), ones) * PART
    down_z = group_sum(jnp.where(lane % 4 == 0, czd[...], 0.0), ones) * PART
    up_0 = jnp.concatenate([c0[0 : CROWS - 8], gxhi], axis=0)
    down_0 = jnp.concatenate([gxlo, c0[0 : CROWS - 8]], axis=0)
    cy[...] = jnp.concatenate(
        [pltpu.roll(up_y[8 * xc : 8 * xc + 8], 1, 0) for xc in range(XC)], axis=0
    )
    cy[pl.ds(0, 8, stride=8), :] = group_sum(by_fours(gy, 0), ones) * PART
    scale = RELAX / (up_0 + up_y + up_z + down_0 + cy[...] + down_z)
    couple_y = jnp.where(row % 8 == 7, up_y * Place().high[0].astype(F32), up_y)
    couple_z = jnp.where(lane >= LANES - 4, 0.0, up_z)
    slot = lane % 4
    packed[...] = jnp.where(
        slot == 0, c0, jnp.where(slot == 1, couple_y, jnp.where(slot == 2, couple_z, scale))
    )


def coarse_faces_kernel(qi, gx, gy, ra, rc, rd, sb, *rest):
    packed, (ma, mb, scr) = rest[:-3], rest[-3:]
    place = Place()
    xlo, xhi = low_high(place, 1, rc[...], rd[...])
    even = place.even[0]
    own = jnp.where(jnp.full(ra.shape, even.astype(jnp.int32)) == 1, gy[BS : 2 * BS, :], gy[0:BS, :])
    scr[...] = own * ra[...]
    faces = jnp.concatenate(
        [fold(gx[0:BS, :] * xlo), fold(gx[BS : 2 * BS, :] * xhi), by_fours(scr, 0)], axis=0
    )
    faces = group_sum(faces, group_matrix()) * PART
    ma[0:CROWS, :] = qi[...]
    ma[0:8, :] = ma[0:8, :] + faces[0:8]
    ma[CROWS - 8 : CROWS, :] = ma[CROWS - 8 : CROWS, :] + faces[8:16]
    nothing = jnp.zeros((8, LANES), F32)
    at = pl.ds(0, 8, stride=8)
    ma[at, :] = ma[at, :] + pick(even, nothing, faces[16:24])
    at = pl.ds(7, 8, stride=8)
    ma[at, :] = ma[at, :] + pick(even, faces[16:24], nothing)
    mb[0:CROWS, :] = ma[0:CROWS, :]
    mb[CROWS : CROWS + BS, :] = sb[...]
    for w in packed:
        ma[CROWS : 2 * CROWS, :] = w[...]
        mb[CROWS + BS : 2 * CROWS + BS, :] = w[...]


def joined(place, own, first, second):
    low, high = low_high(place, 0, first, second)
    parts = []
    for xc in range(XC):
        at = slice(8 * xc, 8 * xc + 8)
        parts += [low[at], own[at], high[at]]
    return jnp.concatenate(parts, axis=0)


def coarse_solve(place, ma, qa, qb, sb, gy, weights, c, cyb, sa, sc, sd, scr, two):
    even = place.even[0]
    w0, wy, wz, scale = weights
    scr[...] = joined(place, ma[0:CROWS, :], qa[0:CROWS, :], qb[0:CROWS, :])
    side = pick(even, gy[0:BS, :], gy[BS : 2 * BS, :])
    there = jnp.where(even, place.low[0].astype(F32), place.high[0].astype(F32))
    two[0:BS, :] = side * qb[CROWS : CROWS + BS, :] * there
    two[BS : 2 * BS, :] = side * sb[...]
    faces = jnp.concatenate([by_fours(two, 0), by_fours(two, BS)], axis=0)
    faces = group_sum(faces, group_matrix()) * PART
    mine, theirs = faces[0:8], faces[8:16]
    nothing = jnp.zeros((8, LANES), F32)
    for row, value in (
        (8, pick(even, mine, nothing)),
        (7, pick(even, theirs, nothing)),
        (15, pick(even, nothing, mine)),
        (16, pick(even, nothing, theirs)),
    ):
        at = pl.ds(row, 8, stride=24)
        scr[at, :] = scr[at, :] + value
    rhs = scr[...]

    def up_x(v):
        return jnp.concatenate([v[24:], v[:24]], axis=0)

    def down_x(v):
        return jnp.concatenate([v[-24:], v[:-24]], axis=0)

    def by_plane(v, shift):
        return jnp.concatenate(
            [pltpu.roll(v[24 * xc : 24 * xc + 24], shift, 0) for xc in range(XC)], axis=0
        )

    field = scale * rhs
    for _ in range(CSWEEPS - 1):
        total = rhs + w0 * up_x(field) + down_x(w0 * field)
        total = total + wy * by_plane(field, 23) + by_plane(wy * field, 1)
        total = total + wz * pltpu.roll(field, LANES - 4, 1) + pltpu.roll(wz * field, 4, 1)
        field = KEEP * field + scale * total
    scr[...] = field
    for xc in range(XC):
        c[8 * xc : 8 * xc + 8, :] = field[24 * xc + 8 : 24 * xc + 16]
    cyb[...] = pick(even, scr[pl.ds(7, 8, stride=24), :], scr[pl.ds(16, 8, stride=24), :])
    sa[...] = pick(even, scr[pl.ds(15, 8, stride=24), :], scr[pl.ds(8, 8, stride=24), :])
    low, high = field[8:16], field[24 * 7 + 8 : 24 * 7 + 16]
    sc[...] = pick(place.even[1], high, low)
    sd[...] = pick(place.even[1], low, high)


def first_coarse_kernel(ma, qa, qb, sb, gy, c, cyb, sa, sc, sd, wide, scr, two):
    place = Place()
    packed = joined(
        place, ma[CROWS : 2 * CROWS, :], qa[CROWS : 2 * CROWS, :], qb[CROWS + BS :, :]
    )
    ones = group_matrix()
    slot = lane_ids(3 * CROWS) % 4
    weights = [group_sum(jnp.where(slot == j, packed, 0.0), ones) for j in range(4)]
    for j in range(4):
        wide[3 * CROWS * j : 3 * CROWS * (j + 1), :] = weights[j]
    coarse_solve(place, ma, qa, qb, sb, gy, weights, c, cyb, sa, sc, sd, scr, two)


def later_coarse_kernel(ma, qa, qb, sb, gy, wide, c, cyb, sa, sc, sd, scr, two):
    weights = [wide[3 * CROWS * j : 3 * CROWS * (j + 1), :] for j in range(4)]
    coarse_solve(Place(), ma, qa, qb, sb, gy, weights, c, cyb, sa, sc, sd, scr, two)


def spread_rows(scr, value):
    for j in range(4):
        scr[pl.ds(j, 8, stride=4), :] = value
    return scr[...]


def correct_kernel(src, c, f0, fy, fz, p, gy, qb, cc, cyb, p2, r, scr):
    def corrected(x):
        return p[plane(x), :] + tiled(cc[8 * (x // 4) : 8 * (x // 4) + 8, :])

    t0, here = ZERO(), corrected(0)
    for x in range(BS):
        at = plane(x)
        after = corrected(min(x + 1, BS - 1))
        p2[at, :] = here
        r[at, :], t0 = residual_plane(src, c, f0, fy, fz, at, t0, here, after)
        here = after
    halo = qb[CROWS : CROWS + BS, :] + spread_rows(scr, cyb[...])
    ylo, yhi = low_high(Place(), 0, ZERO(), halo)
    add_faces_y(r, gy[0:BS, :] * ylo, gy[BS : 2 * BS, :] * yhi)


def residual_kernel(src, c, f0, fy, fz, p, r):
    t0, here = ZERO(), p[0:BS, :]
    for x in range(BS):
        at = plane(x)
        after = p[after_plane(x), :]
        r[at, :], t0 = residual_plane(src, c, f0, fy, fz, at, t0, here, after)
        here = after


def add_all(place, gx, gy, ra, rb, rc, rd, ref):
    xlo, xhi = low_high(place, 1, rc, rd)
    add_faces_x(ref, gx[0:BS, :] * xlo, gx[BS : 2 * BS, :] * xhi)
    ylo, yhi = low_high(place, 0, ra, rb)
    add_faces_y(ref, gy[0:BS, :] * ylo, gy[BS : 2 * BS, :] * yhi)


def finish_smooth(place, limit, r, f0, fy, fzs, d, p, p_out, sends, e):
    def finish(at, value):
        p_out[at, :] = p[at, :] + value

    relax(limit, r, e, f0, fy, fzs, d, finish)
    send_faces(place, p_out, *sends)


def smooth_corrected_kernel(
    ri, limit, f0, fy, fzs, d, p, gx, gy, ra, rc, rd, ka, kc, kd,
    r, p_out, sa, sb, sc, sd, e, scr,
):
    place = Place()
    near = ra[...] + spread_rows(scr, ka[...])
    add_all(place, gx, gy, near, ZERO(), rc[...] + tiled(kc[...]), rd[...] + tiled(kd[...]), r)
    finish_smooth(place, limit[...], r, f0, fy, fzs, d, p, p_out, (sa, sb, sc, sd), e)


def smooth_kernel(
    ri, limit, f0, fy, fzs, d, p, gx, gy, ra, rb, rc, rd,
    r, p_out, sa, sb, sc, sd, e,
):
    place = Place()
    add_all(place, gx, gy, ra[...], rb[...], rc[...], rd[...], r)
    finish_smooth(place, limit[...], r, f0, fy, fzs, d, p, p_out, (sa, sb, sc, sd), e)


def plane_to_blocks(v, x, out, base):
    lane = lane_ids(8)
    half = lane < 64
    even = (lane // BS) % 2 == 0
    v = [v[8 * k : 8 * k + 8] for k in range(4)]
    u = [None] * 4
    for k in range(2):
        low, high = v[k], v[k + 2]
        u[k] = jnp.where(half, low, pltpu.roll(high, 64, 1))
        u[k + 2] = jnp.where(half, pltpu.roll(low, 64, 1), high)
    for b in (0, 2):
        low, high = u[b], u[b + 1]
        first = jnp.where(even, low, pltpu.roll(high, BS, 1))
        second = jnp.where(even, pltpu.roll(low, LANES - BS, 1), high)
        at = base + b * STEP + x * 8
        out[at : at + 8, :] = first
        out[at + STEP : at + STEP + 8, :] = second


def pressure_blocks_kernel(p, blocks):
    for x in range(BS):
        plane_to_blocks(p[plane(x), :], x, blocks, BLK * STEP)


def final_kernel(ri, gx, gy, ra, rb, rc, rd, pblocks, r, blocks, sa, sb):
    place = Place()
    add_all(place, gx, gy, ra[...], rb[...], rc[...], rd[...], r)

    for x in range(BS):
        plane_to_blocks(r[plane(x), :], x, blocks, BLK * STEP)
    send_blocks_kernel(pblocks, blocks, sa, sb, count=1)


def send_blocks_kernel(pblocks, blocks, sa, sb, *, count):
    even = Place().even[0]
    for n, ref in enumerate((pblocks, blocks)):
        for b in range(count):
            for t in range(0, 256, 32):
                low = (BLK + b) * STEP + t
                high = (2 * BLK - count + b) * STEP + t
                low, high = ref[low : low + 32, :], ref[high : high + 32, :]
                at = slice((n * count + b) * 256 + t, (n * count + b) * 256 + t + 32)
                sa[at, :] = pick(even, high, low)
                sb[at, :] = pick(even, low, high)


def place_kernel(owned, in_p, in_r, ra, rb, out_p, out_r, seq_p, seq_r, held_p, held_r, sems, *, count):
    place = Place()
    even = place.even[0]
    start = jnp.max(owned[0:8, :]).astype(jnp.int32)
    base = jnp.clip(start - place.device * BLK + BLK, 0, 2 * BLK) * STEP
    valid = row_ids(8).astype(F32) < owned[8:16, :]
    copies = []
    fields = ((seq_p, held_p, out_p), (seq_r, held_r, out_r))
    for n, (seq, tiles, out) in enumerate(fields):
        for b in range(count):
            for t in range(0, 256, 32):
                at = slice((n * count + b) * 256 + t, (n * count + b) * 256 + t + 32)
                low, high = (BLK - count + b) * STEP + t, (2 * BLK + b) * STEP + t
                seq[low : low + 32, :] = pick(even, rb[at, :], ra[at, :])
                seq[high : high + 32, :] = pick(even, ra[at, :], rb[at, :])
        for part in range(PIECES):
            for t in range(part * PIECE, (part + 1) * PIECE):
                rows = seq[pl.ds(base + t, 8, stride=STEP), :]
                tiles[t, :, :] = jnp.where(valid, rows, 0.0)[0:CAP]
            at = pl.ds(part * PIECE, PIECE)
            copy = pltpu.make_async_copy(tiles.at[at], out.at[at], sems.at[n, part])
            copy.start()
            copies.append(copy)
    for copy in copies:
        copy.wait()


BOTH = ("region", "member")


def swap_near(value):
    return lax.ppermute(value, "member", [(i, i ^ 1) for i in range(lax.axis_size("member"))])


def swap_far(value):
    regions, members = lax.axis_size("region"), lax.axis_size("member")
    pairs = []
    for r in range(regions):
        for m in range(members):
            other = m + 1 if m % 2 else m - 1
            inside = 0 <= other < members
            target = r * members + other if inside else (r ^ 1) * members + m
            pairs.append((r * members + m, target))
    return lax.ppermute(value, BOTH, pairs)


def swap_regions(inner, outer):
    regions, members = lax.axis_size("region"), lax.axis_size("member")
    pairs = []
    for r in range(regions):
        other = r + 1 if r % 2 else r - 1
        inside = 0 <= other < regions
        for m in range(members):
            target = other * members + m if inside else r * members + (m ^ 1)
            pairs.append((r * members + m, target))
    inner = lax.ppermute(inner, "region", [(i, i ^ 1) for i in range(regions)])
    return inner, lax.ppermute(outer, BOTH, pairs)


def swap_blocks(first, second):
    count = lax.axis_size(BOTH)
    inner = [(i, i ^ 1) for i in range(count)]
    outer = [(i, (i + 1) % count if i % 2 else (i - 1) % count) for i in range(count)]
    return lax.ppermute(first, BOTH, inner), lax.ppermute(second, BOTH, outer)


def swap_faces(sa, sb, sc, sd):
    return (swap_near(sa), swap_far(sb), *swap_regions(sc, sd))


FULL, TWO, CFIELD = (ROWS, LANES), (2 * BS, LANES), (CROWS, LANES)
FACE, CFACE = (BS, LANES), (8, LANES)
ROW = ((2 * BLK + 8) * STEP, LANES)


def set_up(levels, new_owner, src, inv):
    outs = [jax.ShapeDtypeStruct((16, LANES), F32), jax.ShapeDtypeStruct((1,), jnp.int32)] + [
        jax.ShapeDtypeStruct(s, F32) for s in [FULL] * 6 + [TWO] * 2 + [CFIELD] * 2 + [FACE]
    ]
    vm, sm = pl.BlockSpec(memory_space=pltpu.VMEM), pl.BlockSpec(memory_space=pltpu.SMEM)
    return pl.pallas_call(
        weights_kernel,
        out_shape=outs,
        in_specs=[sm] * 2 + [vm] * 3,
        out_specs=[vm, sm] + [vm] * 11,
        compiler_params=pltpu.CompilerParams(vmem_limit_bytes=48 << 20),
        cost_estimate=pl.CostEstimate(flops=4000000, bytes_accessed=6 << 20, transcendentals=0),
    )(*levels, new_owner.reshape(-1, min(LANES, new_owner.size)), src, inv)


def faces_kernel(inv, sa, sb, sc, sd, sems):
    place = Place()
    low, high = (0, BS - 1)

    def copies(first, second, axis):
        if axis == 0:
            pair = ((inv.at[1, :, first, :], sa), (inv.at[1, :, second, :], sb))
        else:
            pair = ((inv.at[0, first], sc), (inv.at[0, second], sd))
        return [
            pltpu.make_async_copy(source, to, sems.at[2 * axis + n])
            for n, (source, to) in enumerate(pair)
        ]

    for axis in range(2):

        @pl.when(place.even[axis])
        def _():
            for copy in copies(high, low, axis):
                copy.start()

        @pl.when(jnp.logical_not(place.even[axis]))
        def _():
            for copy in copies(low, high, axis):
                copy.start()

    for axis in range(2):
        for copy in copies(low, high, axis):
            copy.wait()


def density_faces(inverse_density):
    return pl.pallas_call(
        faces_kernel,
        out_shape=[jax.ShapeDtypeStruct(FACE, F32)] * 4,
        in_specs=[pl.BlockSpec(memory_space=pl.ANY)],
        out_specs=[pl.BlockSpec(memory_space=pltpu.VMEM)] * 4,
        scratch_shapes=[pltpu.SemaphoreType.DMA((4,))],
        compiler_params=pltpu.CompilerParams(vmem_limit_bytes=48 << 20),
        cost_estimate=pl.CostEstimate(flops=2000000000, bytes_accessed=131072, transcendentals=0),
    )(inverse_density)


def place_blocks(count, owned, *arrays):
    slots, row = (256, CAP, LANES), ROW
    vm = pl.BlockSpec(memory_space=pltpu.VMEM)
    anywhere = pl.BlockSpec(memory_space=pl.ANY)
    outs = pl.pallas_call(
        functools.partial(place_kernel, count=count),
        out_shape=[jax.ShapeDtypeStruct(shape, F32) for shape in (slots, slots, row, row)],
        in_specs=[vm] * 5,
        out_specs=[anywhere] * 2 + [vm] * 2,
        scratch_shapes=[vmem(*slots), vmem(*slots), pltpu.SemaphoreType.DMA((2, PIECES))],
        input_output_aliases={1: 2, 2: 3},
        compiler_params=pltpu.CompilerParams(vmem_limit_bytes=48 << 20),
        cost_estimate=pl.CostEstimate(flops=2000000, bytes_accessed=6 << 20, transcendentals=0),
    )(owned, *arrays)
    return tuple(o.transpose(1, 0, 2).reshape(CAP, 256 * LANES) for o in outs[:2])


def on_device(source, inverse_density, block_level, level_sweeps, new_owner):
    levels = (block_level, level_sweeps)
    halos = swap_faces(*density_faces(inverse_density))
    owned, most, src, f0, fy, fz, fzs, c0, fx, fyf, czu, czd, limit = set_up(
        levels, new_owner, source.reshape(ROWS, LANES), inverse_density.reshape(3 * ROWS, LANES)
    )
    c, d, gx, gy, p, *sends = call(
        first_kernel,
        [FULL, FULL, TWO, TWO, FULL] + [FACE] * 4,
        [limit, src, f0, fy, fzs, c0, fx, fyf, *halos],
        (),
        [vmem(*FULL)],
        {5: 0},
    )
    fine = [src, c, f0, fy, fz]
    wide = None
    for cycle in range(CYCLES):
        if cycle > 0:
            halos = swap_faces(*sends)
            (ri,) = call(residual_kernel, [FULL], [*fine, p])
            _, p, *sends = call(
                smooth_kernel,
                [FULL, FULL] + [FACE] * 4,
                [ri, limit, f0, fy, fzs, d, p, gx, gy, *halos],
                (),
                [vmem(*FULL)],
                {0: 0},
            )
        sa, sb, sc, sd = sends
        ra = swap_near(sa)
        rc, rd = swap_regions(sc, sd)
        (qi,) = call(coarse_rhs_kernel, [CFIELD], [*fine, p], scratch=[vmem(*CFIELD)])
        packed, rows = [], CROWS
        if wide is None:
            packed = call(
                coarse_weights_kernel,
                [CFIELD],
                [f0, fy, gx, gy, czu, czd],
                scratch=[vmem(*CFIELD)] * 2,
            )
            rows = 2 * CROWS
        ma, mb = call(
            coarse_faces_kernel,
            [(rows, LANES), (rows + BS, LANES)],
            [qi, gx, gy, ra, rc, rd, sb, *packed],
            scratch=[vmem(*FACE)],
        )
        qa, qb = swap_near(ma), swap_far(mb)
        outs = [CFIELD] + [CFACE] * 4
        arrays = [ma, qa, qb, sb, gy]
        scratch = [vmem(3 * CROWS, LANES), vmem(*TWO)]
        if wide is None:
            cc, cyb, ta, tc, td, wide = call(
                first_coarse_kernel, outs + [(12 * CROWS, LANES)], arrays, scratch=scratch
            )
        else:
            cc, cyb, ta, tc, td = call(later_coarse_kernel, outs, [*arrays, wide], scratch=scratch)
        ka = swap_near(ta)
        kc, kd = swap_regions(tc, td)
        p, ri = call(
            correct_kernel, [FULL, FULL], [*fine, p, gy, qb, cc, cyb], scratch=[vmem(*FACE)]
        )
        _, p, *sends = call(
            smooth_corrected_kernel,
            [FULL, FULL] + [FACE] * 4,
            [ri, limit, f0, fy, fzs, d, p, gx, gy, ra, rc, rd, ka, kc, kd],
            (),
            [vmem(*FULL), vmem(*FACE)],
            {0: 0},
        )

    halos = swap_faces(*sends)
    (ri,) = call(residual_kernel, [FULL], [*fine, p])
    (blocks_p,) = call(pressure_blocks_kernel, [ROW], [p])
    _, blocks_r, sa, sb = call(
        final_kernel,
        [FULL, ROW] + [(512, LANES)] * 2,
        [ri, gx, gy, *halos, blocks_p],
        aliases={0: 0},
    )

    def one(owned, blocks_p, blocks_r, sa, sb):
        return place_blocks(1, owned, blocks_p, blocks_r, *swap_blocks(sa, sb))

    def several(owned, blocks_p, blocks_r, sa, sb):
        body = functools.partial(send_blocks_kernel, count=BLK)
        sends = call(body, [(2 * BLK * 256, LANES)] * 2, [blocks_p, blocks_r])
        return place_blocks(BLK, owned, blocks_p, blocks_r, *swap_blocks(*sends))

    return lax.cond(most.reshape(()) <= 1, one, several, owned, blocks_p, blocks_r, sa, sb)


def solution(mesh):
    placed = (
        P("region", "member", None),
        P(None, "region", "member", None),
        P(("region", "member")),
        P(),
        P(),
    )
    return jax.shard_map(
        on_device,
        mesh=mesh,
        in_specs=placed,
        out_specs=(P(("region", "member"), None), P(("region", "member"), None)),
        check_vma=False,
    )
```

```python
import functools

import jax
import jax.numpy as jnp
from jax import lax
from jax.experimental import pallas as pl
from jax.experimental.pallas import tpu as pltpu
from jax.sharding import PartitionSpec as P


BS = 32
BLK = 4
CSWEEPS = 8
CYCLES = 2
CAP = 6
SWEEP_MAX = 6
RELAX = 0.8
KEEP = 0.2
PART = 1.0 / 64.0
PIECES = 4
PIECE = 256 // PIECES
STEP = 264
LANES = 128
ROWS = BS * BS
XC = BS // 4
CROWS = XC * XC
ZERO = functools.partial(jnp.zeros, (BS, LANES), jnp.float32)
F32 = jnp.float32


def vmem(*shape):
    return pltpu.VMEM(shape, F32)


def call(body, out_rows, args, scalars=(), scratch=(), aliases=None, flops=2e6, mib=48):
    outs = [jax.ShapeDtypeStruct(s, F32) for s in out_rows]
    moved = sum(a.size * 4 for a in args) + sum(o.size * 4 for o in outs)
    return pl.pallas_call(
        body,
        out_shape=outs,
        in_specs=[pl.BlockSpec(memory_space=pltpu.SMEM)] * len(scalars)
        + [pl.BlockSpec(memory_space=pltpu.VMEM)] * len(args),
        out_specs=[pl.BlockSpec(memory_space=pltpu.VMEM)] * len(outs),
        scratch_shapes=list(scratch),
        input_output_aliases={len(scalars) + k: v for k, v in (aliases or {}).items()},
        compiler_params=pltpu.CompilerParams(vmem_limit_bytes=mib << 20),
        cost_estimate=pl.CostEstimate(flops=int(flops), bytes_accessed=int(moved), transcendentals=0),
    )(*scalars, *args)


class Place:
    def __init__(self):
        region, member = lax.axis_index("region"), lax.axis_index("member")
        self.device = region * lax.axis_size("member") + member
        self.even = (member % 2 == 0, region % 2 == 0)
        self.low = (member > 0, region > 0)
        self.high = (member < lax.axis_size("member") - 1, region < lax.axis_size("region") - 1)


def lane_ids(rows):
    return lax.broadcasted_iota(jnp.int32, (rows, LANES), 1)


def row_ids(rows):
    return lax.broadcasted_iota(jnp.int32, (rows, LANES), 0)


def next_y(v):
    return jnp.concatenate([v[8:32], pltpu.roll(v[0:8], 7, 0)], axis=0)


def prev_y(v):
    return jnp.concatenate([pltpu.roll(v[24:32], 1, 0), v[0:24]], axis=0)


def next_z(v):
    return pltpu.roll(v, LANES - 1, 1)


def prev_z(v):
    return pltpu.roll(v, 1, 1)


def fold(v):
    return v[0:8] + v[8:16] + v[16:24] + v[24:32]


def tiled(v):
    return jnp.concatenate([v, v, v, v], axis=0)


def plane(x):
    return slice(x * BS, (x + 1) * BS)


def after_plane(x):
    return plane(min(x + 1, BS - 1))


def pick(flag, yes, no):
    return jnp.where(jnp.full(yes.shape, flag.astype(jnp.int32), jnp.int32) == 1, yes, no)


def low_high(place, axis, first, second):
    low = pick(place.even[axis], second, first) * place.low[axis].astype(F32)
    high = pick(place.even[axis], first, second) * place.high[axis].astype(F32)
    return low, high


def group_matrix():
    return jnp.where(
        row_ids(LANES) // 4 == lane_ids(LANES) // 4, jnp.float32(1.0), jnp.float32(0.0)
    )


def group_sum(v, ones):
    return lax.dot_general(
        v, ones, (((1,), (0,)), ((), ())), precision=lax.Precision.HIGHEST, preferred_element_type=F32
    )


def by_fours(ref, base):
    total = ref[pl.ds(base, 8, stride=4), :]
    for j in range(1, 4):
        total = total + ref[pl.ds(base + j, 8, stride=4), :]
    return total


def weights_kernel(
    levels, level_sweeps, new_owner, src, inv,
    owned, most, src_t, f0, fy, fz, fzs, c0, fx, fyf, czu, czd, limit,
):
    row, lane = row_ids(BS), lane_ids(BS)

    def load(ref, x, offset):
        return jnp.concatenate(
            [ref[pl.ds(offset + x * BS + k, 8, stride=4), :] for k in range(4)], axis=0
        )

    before, here = ZERO(), load(inv, 0, 0)
    for xc in range(XC):
        total_up = jnp.zeros((8, LANES), F32)
        total_down = jnp.zeros((8, LANES), F32)
        for j in range(4):
            x = xc * 4 + j
            src_t[plane(x), :] = load(src, x, 0)
            after = load(inv, x + 1, 0) if x < BS - 1 else ZERO()
            one = load(inv, x, ROWS)
            two = load(inv, x, 2 * ROWS)
            one_n = jnp.where(row == BS - 1, 0.0, next_y(one))
            one_p = jnp.where(row == 0, 0.0, prev_y(one))
            two_n = jnp.where(lane == LANES - 1, 0.0, next_z(two))
            two_p = jnp.where(lane == 0, 0.0, prev_z(two))
            up0 = 0.5 * (here + after)
            upy = 0.5 * (one + one_n)
            upz = 0.5 * (two + two_n)
            downz = 0.5 * (two + two_p)
            f0[plane(x), :] = up0 if x < BS - 1 else ZERO()
            fy[plane(x), :] = jnp.where(row == BS - 1, 0.0, upy)
            fz[plane(x), :] = jnp.where(lane == LANES - 1, 0.0, upz)
            fzs[plane(x), :] = jnp.where(lane % BS == BS - 1, 0.0, upz)
            c0[plane(x), :] = up0 + upy + upz + 0.5 * (here + before) + 0.5 * (one + one_p) + downz
            total_up = total_up + fold(upz)
            total_down = total_down + fold(downz)
            before, here = here, after
        czu[8 * xc : 8 * xc + 8, :] = total_up
        czd[8 * xc : 8 * xc + 8, :] = total_down
    fx[0:BS, :] = load(inv, 0, 0)
    fx[BS : 2 * BS, :] = load(inv, BS - 1, 0)
    for g in range(4):
        fyf[8 * g : 8 * g + 8, :] = inv[pl.ds(ROWS + 256 * g, 8, stride=BS), :]
        fyf[BS + 8 * g : BS + 8 * g + 8, :] = inv[pl.ds(ROWS + 256 * g + 31, 8, stride=BS), :]
    limit[...] = sweep_limits(levels, level_sweeps)
    device = Place().device
    owner = new_owner[...]
    block = lax.broadcasted_iota(jnp.int32, owner.shape, 0) * owner.shape[1]
    block = block + lax.broadcasted_iota(jnp.int32, owner.shape, 1)
    home, place = block // BLK, block % BLK
    leaving = jnp.where(owner > home, BLK - place, jnp.where(owner < home, place + 1, 0))
    owned[0:8, :] = jnp.full((8, LANES), jnp.sum((owner < device).astype(F32)))
    owned[8:16, :] = jnp.full((8, LANES), jnp.sum((owner == device).astype(F32)))
    most[0] = jnp.max(leaving.astype(F32)).astype(jnp.int32)


def add_faces_y(ref, low, high):
    for g in range(4):
        at = pl.ds(256 * g, 8, stride=BS)
        ref[at, :] = ref[at, :] + low[8 * g : 8 * g + 8]
        at = pl.ds(256 * g + 31, 8, stride=BS)
        ref[at, :] = ref[at, :] + high[8 * g : 8 * g + 8]


def add_faces_x(ref, low, high):
    ref[0:BS, :] = ref[0:BS, :] + low
    ref[ROWS - BS : ROWS, :] = ref[ROWS - BS : ROWS, :] + high


def send_faces(place, p, sa, sb, sc, sd):
    even = place.even[0]
    for g in range(4):
        low = p[pl.ds(256 * g, 8, stride=BS), :]
        high = p[pl.ds(256 * g + 31, 8, stride=BS), :]
        sa[8 * g : 8 * g + 8, :] = pick(even, high, low)
        sb[8 * g : 8 * g + 8, :] = pick(even, low, high)
    low = p[0:BS, :]
    high = p[ROWS - BS : ROWS, :]
    sc[...] = pick(place.even[1], high, low)
    sd[...] = pick(place.even[1], low, high)


def sweep_limits(levels, level_sweeps):
    block = lane_ids(BS) // BS
    limit = jnp.zeros((BS, LANES), jnp.int32)
    for b in range(BLK):
        limit = jnp.where(block == b, level_sweeps[levels[b]], limit)
    return limit.astype(F32)


def relax(limit, r, e, f0, fy, fzs, d, finish):
    def sweep(i, load, store):
        active = limit > float(i)

        t0, here = ZERO(), load(plane(0))
        for x in range(BS):
            at = plane(x)
            after = load(after_plane(x))
            w0, wy, wz = f0[at, :], fy[at, :], fzs[at, :]
            t1 = w0 * here
            total = r[at, :] + t0 + w0 * after
            total = total + wy * next_y(here) + prev_y(wy * here)
            total = total + wz * next_z(here) + prev_z(wz * here)
            store(at, jnp.where(active, KEEP * here + d[at, :] * total, here))
            t0, here = t1, after

    def first(at):
        return d[at, :] * r[at, :]

    def held(at):
        return e[at, :]

    def keep(at, value):
        e[at, :] = value

    sweep(1, first, keep)
    for i in range(2, SWEEP_MAX - 1):
        sweep(i, held, keep)
    sweep(SWEEP_MAX - 1, held, finish)


def first_kernel(
    limit, src, f0, fy, fzs, c0, fx, fyf, ra, rb, rc, rd,
    c, d, gx, gy, p, sa, sb, sc, sd, e,
):
    def natural(ref):
        return jnp.concatenate([ref[pl.ds(k, 8, stride=4), :] for k in range(4)], axis=0)

    place = Place()
    xlo, xhi = low_high(place, 1, natural(rc), natural(rd))
    ylo, yhi = low_high(place, 0, ra[...], rb[...])
    gx[0:BS, :] = 0.5 * (fx[0:BS, :] + xlo)
    gx[BS : 2 * BS, :] = 0.5 * (fx[BS : 2 * BS, :] + xhi)
    gy[0:BS, :] = 0.5 * (fyf[0:BS, :] + ylo)
    gy[BS : 2 * BS, :] = 0.5 * (fyf[BS : 2 * BS, :] + yhi)
    add_faces_x(c, 0.5 * xlo, 0.5 * xhi)
    add_faces_y(c, 0.5 * ylo, 0.5 * yhi)

    for x in range(BS):
        at = plane(x)
        d[at, :] = RELAX / c[at, :]

    def finish(at, value):
        p[at, :] = value

    relax(limit[...], src, e, f0, fy, fzs, d, finish)
    send_faces(place, p, sa, sb, sc, sd)


def residual_plane(src, c, f0, fy, fz, at, t0, here, after):
    w0, wy, wz = f0[at, :], fy[at, :], fz[at, :]
    total = src[at, :] - c[at, :] * here + t0 + w0 * after
    total = total + wy * next_y(here) + prev_y(wy * here)
    total = total + wz * next_z(here) + prev_z(wz * here)
    return total, w0 * here


def coarse_rhs_kernel(src, c, f0, fy, fz, p, q, scr):
    t0, here = ZERO(), p[0:BS, :]
    for xc in range(XC):
        total = jnp.zeros((8, LANES), F32)
        for j in range(4):
            x = xc * 4 + j
            after = p[after_plane(x), :]
            r, t0 = residual_plane(src, c, f0, fy, fz, plane(x), t0, here, after)
            total = total + fold(r)
            here = after
        scr[8 * xc : 8 * xc + 8, :] = total
    q[...] = group_sum(scr[...], group_matrix()) * PART


def coarse_weights_kernel(f0, fy, gx, gy, czu, czd, packed, scr, cy):
    ones = group_matrix()
    lane = lane_ids(CROWS)
    row = row_ids(CROWS)
    for xc in range(XC):
        scr[8 * xc : 8 * xc + 8, :] = fold(f0[(4 * xc + 3) * BS : (4 * xc + 4) * BS, :])
        total = fy[4 * xc * BS + 24 : 4 * xc * BS + 32, :]
        for j in range(1, 4):
            at = (4 * xc + j) * BS
            total = total + fy[at + 24 : at + 32, :]
        cy[8 * xc : 8 * xc + 8, :] = total
    c0 = group_sum(scr[...], ones) * PART
    cy[pl.ds(7, 8, stride=8), :] = by_fours(gy, BS)
    up_y = group_sum(cy[...], ones) * PART
    gxlo = group_sum(fold(gx[0:BS, :]), ones) * PART
    gxhi = group_sum(fold(gx[BS : 2 * BS, :]), ones) * PART
    up_z = group_sum(jnp.where(lane % 4 == 3, czu[...], 0.0), ones) * PART
    down_z = group_sum(jnp.where(lane % 4 == 0, czd[...], 0.0), ones) * PART
    up_0 = jnp.concatenate([c0[0 : CROWS - 8], gxhi], axis=0)
    down_0 = jnp.concatenate([gxlo, c0[0 : CROWS - 8]], axis=0)
    cy[...] = jnp.concatenate(
        [pltpu.roll(up_y[8 * xc : 8 * xc + 8], 1, 0) for xc in range(XC)], axis=0
    )
    cy[pl.ds(0, 8, stride=8), :] = group_sum(by_fours(gy, 0), ones) * PART
    scale = RELAX / (up_0 + up_y + up_z + down_0 + cy[...] + down_z)
    couple_y = jnp.where(row % 8 == 7, up_y * Place().high[0].astype(F32), up_y)
    couple_z = jnp.where(lane >= LANES - 4, 0.0, up_z)
    slot = lane % 4
    packed[...] = jnp.where(
        slot == 0, c0, jnp.where(slot == 1, couple_y, jnp.where(slot == 2, couple_z, scale))
    )


def coarse_faces_kernel(qi, gx, gy, ra, rc, rd, sb, *rest):
    packed, (ma, mb, scr) = rest[:-3], rest[-3:]
    place = Place()
    xlo, xhi = low_high(place, 1, rc[...], rd[...])
    even = place.even[0]
    own = jnp.where(jnp.full(ra.shape, even.astype(jnp.int32)) == 1, gy[BS : 2 * BS, :], gy[0:BS, :])
    scr[...] = own * ra[...]
    faces = jnp.concatenate(
        [fold(gx[0:BS, :] * xlo), fold(gx[BS : 2 * BS, :] * xhi), by_fours(scr, 0)], axis=0
    )
    faces = group_sum(faces, group_matrix()) * PART
    ma[0:CROWS, :] = qi[...]
    ma[0:8, :] = ma[0:8, :] + faces[0:8]
    ma[CROWS - 8 : CROWS, :] = ma[CROWS - 8 : CROWS, :] + faces[8:16]
    nothing = jnp.zeros((8, LANES), F32)
    at = pl.ds(0, 8, stride=8)
    ma[at, :] = ma[at, :] + pick(even, nothing, faces[16:24])
    at = pl.ds(7, 8, stride=8)
    ma[at, :] = ma[at, :] + pick(even, faces[16:24], nothing)
    mb[0:CROWS, :] = ma[0:CROWS, :]
    mb[CROWS : CROWS + BS, :] = sb[...]
    for w in packed:
        ma[CROWS : 2 * CROWS, :] = w[...]
        mb[CROWS + BS : 2 * CROWS + BS, :] = w[...]


def joined(place, own, first, second):
    low, high = low_high(place, 0, first, second)
    parts = []
    for xc in range(XC):
        at = slice(8 * xc, 8 * xc + 8)
        parts += [low[at], own[at], high[at]]
    return jnp.concatenate(parts, axis=0)


def coarse_solve(place, ma, qa, qb, sb, gy, weights, c, cyb, sa, sc, sd, scr, two):
    even = place.even[0]
    w0, wy, wz, scale = weights
    scr[...] = joined(place, ma[0:CROWS, :], qa[0:CROWS, :], qb[0:CROWS, :])
    side = pick(even, gy[0:BS, :], gy[BS : 2 * BS, :])
    there = jnp.where(even, place.low[0].astype(F32), place.high[0].astype(F32))
    two[0:BS, :] = side * qb[CROWS : CROWS + BS, :] * there
    two[BS : 2 * BS, :] = side * sb[...]
    faces = jnp.concatenate([by_fours(two, 0), by_fours(two, BS)], axis=0)
    faces = group_sum(faces, group_matrix()) * PART
    mine, theirs = faces[0:8], faces[8:16]
    nothing = jnp.zeros((8, LANES), F32)
    for row, value in (
        (8, pick(even, mine, nothing)),
        (7, pick(even, theirs, nothing)),
        (15, pick(even, nothing, mine)),
        (16, pick(even, nothing, theirs)),
    ):
        at = pl.ds(row, 8, stride=24)
        scr[at, :] = scr[at, :] + value
    rhs = scr[...]

    def up_x(v):
        return jnp.concatenate([v[24:], v[:24]], axis=0)

    def down_x(v):
        return jnp.concatenate([v[-24:], v[:-24]], axis=0)

    def by_plane(v, shift):
        return jnp.concatenate(
            [pltpu.roll(v[24 * xc : 24 * xc + 24], shift, 0) for xc in range(XC)], axis=0
        )

    field = scale * rhs
    for _ in range(CSWEEPS - 1):
        total = rhs + w0 * up_x(field) + down_x(w0 * field)
        total = total + wy * by_plane(field, 23) + by_plane(wy * field, 1)
        total = total + wz * pltpu.roll(field, LANES - 4, 1) + pltpu.roll(wz * field, 4, 1)
        field = KEEP * field + scale * total
    scr[...] = field
    for xc in range(XC):
        c[8 * xc : 8 * xc + 8, :] = field[24 * xc + 8 : 24 * xc + 16]
    cyb[...] = pick(even, scr[pl.ds(7, 8, stride=24), :], scr[pl.ds(16, 8, stride=24), :])
    sa[...] = pick(even, scr[pl.ds(15, 8, stride=24), :], scr[pl.ds(8, 8, stride=24), :])
    low, high = field[8:16], field[24 * 7 + 8 : 24 * 7 + 16]
    sc[...] = pick(place.even[1], high, low)
    sd[...] = pick(place.even[1], low, high)


def first_coarse_kernel(ma, qa, qb, sb, gy, c, cyb, sa, sc, sd, wide, scr, two):
    place = Place()
    packed = joined(
        place, ma[CROWS : 2 * CROWS, :], qa[CROWS : 2 * CROWS, :], qb[CROWS + BS :, :]
    )
    ones = group_matrix()
    slot = lane_ids(3 * CROWS) % 4
    weights = [group_sum(jnp.where(slot == j, packed, 0.0), ones) for j in range(4)]
    for j in range(4):
        wide[3 * CROWS * j : 3 * CROWS * (j + 1), :] = weights[j]
    coarse_solve(place, ma, qa, qb, sb, gy, weights, c, cyb, sa, sc, sd, scr, two)


def later_coarse_kernel(ma, qa, qb, sb, gy, wide, c, cyb, sa, sc, sd, scr, two):
    weights = [wide[3 * CROWS * j : 3 * CROWS * (j + 1), :] for j in range(4)]
    coarse_solve(Place(), ma, qa, qb, sb, gy, weights, c, cyb, sa, sc, sd, scr, two)


def spread_rows(scr, value):
    for j in range(4):
        scr[pl.ds(j, 8, stride=4), :] = value
    return scr[...]


def correct_kernel(src, c, f0, fy, fz, p, gy, qb, cc, cyb, p2, r, scr):
    def corrected(x):
        return p[plane(x), :] + tiled(cc[8 * (x // 4) : 8 * (x // 4) + 8, :])

    t0, here = ZERO(), corrected(0)
    for x in range(BS):
        at = plane(x)
        after = corrected(min(x + 1, BS - 1))
        p2[at, :] = here
        r[at, :], t0 = residual_plane(src, c, f0, fy, fz, at, t0, here, after)
        here = after
    halo = qb[CROWS : CROWS + BS, :] + spread_rows(scr, cyb[...])
    ylo, yhi = low_high(Place(), 0, ZERO(), halo)
    add_faces_y(r, gy[0:BS, :] * ylo, gy[BS : 2 * BS, :] * yhi)


def residual_kernel(src, c, f0, fy, fz, p, r):
    t0, here = ZERO(), p[0:BS, :]
    for x in range(BS):
        at = plane(x)
        after = p[after_plane(x), :]
        r[at, :], t0 = residual_plane(src, c, f0, fy, fz, at, t0, here, after)
        here = after


def add_all(place, gx, gy, ra, rb, rc, rd, ref):
    xlo, xhi = low_high(place, 1, rc, rd)
    add_faces_x(ref, gx[0:BS, :] * xlo, gx[BS : 2 * BS, :] * xhi)
    ylo, yhi = low_high(place, 0, ra, rb)
    add_faces_y(ref, gy[0:BS, :] * ylo, gy[BS : 2 * BS, :] * yhi)


def finish_smooth(place, limit, r, f0, fy, fzs, d, p, p_out, sends, e):
    def finish(at, value):
        p_out[at, :] = p[at, :] + value

    relax(limit, r, e, f0, fy, fzs, d, finish)
    send_faces(place, p_out, *sends)


def smooth_corrected_kernel(
    ri, limit, f0, fy, fzs, d, p, gx, gy, ra, rc, rd, ka, kc, kd,
    r, p_out, sa, sb, sc, sd, e, scr,
):
    place = Place()
    near = ra[...] + spread_rows(scr, ka[...])
    add_all(place, gx, gy, near, ZERO(), rc[...] + tiled(kc[...]), rd[...] + tiled(kd[...]), r)
    finish_smooth(place, limit[...], r, f0, fy, fzs, d, p, p_out, (sa, sb, sc, sd), e)


def smooth_kernel(
    ri, limit, f0, fy, fzs, d, p, gx, gy, ra, rb, rc, rd,
    r, p_out, sa, sb, sc, sd, e,
):
    place = Place()
    add_all(place, gx, gy, ra[...], rb[...], rc[...], rd[...], r)
    finish_smooth(place, limit[...], r, f0, fy, fzs, d, p, p_out, (sa, sb, sc, sd), e)


def plane_to_blocks(v, x, out, base):
    lane = lane_ids(8)
    half = lane < 64
    even = (lane // BS) % 2 == 0
    v = [v[8 * k : 8 * k + 8] for k in range(4)]
    u = [None] * 4
    for k in range(2):
        low, high = v[k], v[k + 2]
        u[k] = jnp.where(half, low, pltpu.roll(high, 64, 1))
        u[k + 2] = jnp.where(half, pltpu.roll(low, 64, 1), high)
    for b in (0, 2):
        low, high = u[b], u[b + 1]
        first = jnp.where(even, low, pltpu.roll(high, BS, 1))
        second = jnp.where(even, pltpu.roll(low, LANES - BS, 1), high)
        at = base + b * STEP + x * 8
        out[at : at + 8, :] = first
        out[at + STEP : at + STEP + 8, :] = second


def pressure_blocks_kernel(p, blocks):
    for x in range(BS):
        plane_to_blocks(p[plane(x), :], x, blocks, BLK * STEP)


def final_kernel(ri, gx, gy, ra, rb, rc, rd, pblocks, r, blocks, sa, sb):
    place = Place()
    add_all(place, gx, gy, ra[...], rb[...], rc[...], rd[...], r)

    for x in range(BS):
        plane_to_blocks(r[plane(x), :], x, blocks, BLK * STEP)
    send_blocks_kernel(pblocks, blocks, sa, sb, count=1)


def send_blocks_kernel(pblocks, blocks, sa, sb, *, count):
    even = Place().even[0]
    for n, ref in enumerate((pblocks, blocks)):
        for b in range(count):
            for t in range(0, 256, 32):
                low = (BLK + b) * STEP + t
                high = (2 * BLK - count + b) * STEP + t
                low, high = ref[low : low + 32, :], ref[high : high + 32, :]
                at = slice((n * count + b) * 256 + t, (n * count + b) * 256 + t + 32)
                sa[at, :] = pick(even, high, low)
                sb[at, :] = pick(even, low, high)


def place_kernel(owned, in_p, in_r, ra, rb, out_p, out_r, seq_p, seq_r, held_p, held_r, sems, *, count):
    place = Place()
    even = place.even[0]
    start = jnp.max(owned[0:8, :]).astype(jnp.int32)
    base = jnp.clip(start - place.device * BLK + BLK, 0, 2 * BLK) * STEP
    valid = row_ids(8).astype(F32) < owned[8:16, :]
    copies = []
    fields = ((seq_p, held_p, out_p), (seq_r, held_r, out_r))
    for n, (seq, tiles, out) in enumerate(fields):
        for b in range(count):
            for t in range(0, 256, 32):
                at = slice((n * count + b) * 256 + t, (n * count + b) * 256 + t + 32)
                low, high = (BLK - count + b) * STEP + t, (2 * BLK + b) * STEP + t
                seq[low : low + 32, :] = pick(even, rb[at, :], ra[at, :])
                seq[high : high + 32, :] = pick(even, ra[at, :], rb[at, :])
        for part in range(PIECES):
            for t in range(part * PIECE, (part + 1) * PIECE):
                rows = seq[pl.ds(base + t, 8, stride=STEP), :]
                tiles[t, :, :] = jnp.where(valid, rows, 0.0)[0:CAP]
            at = pl.ds(part * PIECE, PIECE)
            copy = pltpu.make_async_copy(tiles.at[at], out.at[at], sems.at[n, part])
            copy.start()
            copies.append(copy)
    for copy in copies:
        copy.wait()


BOTH = ("region", "member")


def swap_near(value):
    return lax.ppermute(value, "member", [(i, i ^ 1) for i in range(lax.axis_size("member"))])


def swap_far(value):
    regions, members = lax.axis_size("region"), lax.axis_size("member")
    pairs = []
    for r in range(regions):
        for m in range(members):
            other = m + 1 if m % 2 else m - 1
            inside = 0 <= other < members
            target = r * members + other if inside else (r ^ 1) * members + m
            pairs.append((r * members + m, target))
    return lax.ppermute(value, BOTH, pairs)


def swap_regions(inner, outer):
    regions, members = lax.axis_size("region"), lax.axis_size("member")
    pairs = []
    for r in range(regions):
        other = r + 1 if r % 2 else r - 1
        inside = 0 <= other < regions
        for m in range(members):
            target = other * members + m if inside else r * members + (m ^ 1)
            pairs.append((r * members + m, target))
    inner = lax.ppermute(inner, "region", [(i, i ^ 1) for i in range(regions)])
    return inner, lax.ppermute(outer, BOTH, pairs)


def swap_blocks(first, second):
    count = lax.axis_size(BOTH)
    inner = [(i, i ^ 1) for i in range(count)]
    outer = [(i, (i + 1) % count if i % 2 else (i - 1) % count) for i in range(count)]
    return lax.ppermute(first, BOTH, inner), lax.ppermute(second, BOTH, outer)


def swap_faces(sa, sb, sc, sd):
    far = swap_far(sb)
    regions = swap_regions(sc, sd)
    return (swap_near(sa), far, *regions)


FULL, TWO, CFIELD = (ROWS, LANES), (2 * BS, LANES), (CROWS, LANES)
FACE, CFACE = (BS, LANES), (8, LANES)
ROW = ((2 * BLK + 8) * STEP, LANES)


def set_up(levels, new_owner, src, inv):
    outs = [jax.ShapeDtypeStruct((16, LANES), F32), jax.ShapeDtypeStruct((1,), jnp.int32)] + [
        jax.ShapeDtypeStruct(s, F32) for s in [FULL] * 6 + [TWO] * 2 + [CFIELD] * 2 + [FACE]
    ]
    vm, sm = pl.BlockSpec(memory_space=pltpu.VMEM), pl.BlockSpec(memory_space=pltpu.SMEM)
    return pl.pallas_call(
        weights_kernel,
        out_shape=outs,
        in_specs=[sm] * 2 + [vm] * 3,
        out_specs=[vm, sm] + [vm] * 11,
        compiler_params=pltpu.CompilerParams(vmem_limit_bytes=48 << 20),
        cost_estimate=pl.CostEstimate(flops=4000000, bytes_accessed=6 << 20, transcendentals=0),
    )(*levels, new_owner.reshape(-1, min(LANES, new_owner.size)), src, inv)


def faces_kernel(inv, sa, sb, sc, sd, sems):
    place = Place()
    low, high = (0, BS - 1)

    def copies(first, second, axis):
        if axis == 0:
            pair = ((inv.at[1, :, first, :], sa), (inv.at[1, :, second, :], sb))
        else:
            pair = ((inv.at[0, first], sc), (inv.at[0, second], sd))
        return [
            pltpu.make_async_copy(source, to, sems.at[2 * axis + n])
            for n, (source, to) in enumerate(pair)
        ]

    for axis in range(2):

        @pl.when(place.even[axis])
        def _():
            for copy in copies(high, low, axis):
                copy.start()

        @pl.when(jnp.logical_not(place.even[axis]))
        def _():
            for copy in copies(low, high, axis):
                copy.start()

    for axis in range(2):
        for copy in copies(low, high, axis):
            copy.wait()


def density_faces(inverse_density):
    return pl.pallas_call(
        faces_kernel,
        out_shape=[jax.ShapeDtypeStruct(FACE, F32)] * 4,
        in_specs=[pl.BlockSpec(memory_space=pl.ANY)],
        out_specs=[pl.BlockSpec(memory_space=pltpu.VMEM)] * 4,
        scratch_shapes=[pltpu.SemaphoreType.DMA((4,))],
        compiler_params=pltpu.CompilerParams(vmem_limit_bytes=48 << 20),
        cost_estimate=pl.CostEstimate(flops=2000000000, bytes_accessed=131072, transcendentals=0),
    )(inverse_density)


def place_blocks(count, owned, *arrays):
    slots, row = (256, CAP, LANES), ROW
    vm = pl.BlockSpec(memory_space=pltpu.VMEM)
    anywhere = pl.BlockSpec(memory_space=pl.ANY)
    outs = pl.pallas_call(
        functools.partial(place_kernel, count=count),
        out_shape=[jax.ShapeDtypeStruct(shape, F32) for shape in (slots, slots, row, row)],
        in_specs=[vm] * 5,
        out_specs=[anywhere] * 2 + [vm] * 2,
        scratch_shapes=[vmem(*slots), vmem(*slots), pltpu.SemaphoreType.DMA((2, PIECES))],
        input_output_aliases={1: 2, 2: 3},
        compiler_params=pltpu.CompilerParams(vmem_limit_bytes=48 << 20),
        cost_estimate=pl.CostEstimate(flops=2000000, bytes_accessed=6 << 20, transcendentals=0),
    )(owned, *arrays)
    return tuple(o.transpose(1, 0, 2).reshape(CAP, 256 * LANES) for o in outs[:2])


def on_device(source, inverse_density, block_level, level_sweeps, new_owner):
    levels = (block_level, level_sweeps)
    halos = swap_faces(*density_faces(inverse_density))
    owned, most, src, f0, fy, fz, fzs, c0, fx, fyf, czu, czd, limit = set_up(
        levels, new_owner, source.reshape(ROWS, LANES), inverse_density.reshape(3 * ROWS, LANES)
    )
    c, d, gx, gy, p, *sends = call(
        first_kernel,
        [FULL, FULL, TWO, TWO, FULL] + [FACE] * 4,
        [limit, src, f0, fy, fzs, c0, fx, fyf, *halos],
        (),
        [vmem(*FULL)],
        {5: 0},
    )
    fine = [src, c, f0, fy, fz]
    wide = None
    for cycle in range(CYCLES):
        if cycle > 0:
            halos = swap_faces(*sends)
            (ri,) = call(residual_kernel, [FULL], [*fine, p])
            _, p, *sends = call(
                smooth_kernel,
                [FULL, FULL] + [FACE] * 4,
                [ri, limit, f0, fy, fzs, d, p, gx, gy, *halos],
                (),
                [vmem(*FULL)],
                {0: 0},
            )
        sa, sb, sc, sd = sends
        ra = swap_near(sa)
        rc, rd = swap_regions(sc, sd)
        (qi,) = call(coarse_rhs_kernel, [CFIELD], [*fine, p], scratch=[vmem(*CFIELD)])
        packed, rows = [], CROWS
        if wide is None:
            packed = call(
                coarse_weights_kernel,
                [CFIELD],
                [f0, fy, gx, gy, czu, czd],
                scratch=[vmem(*CFIELD)] * 2,
            )
            rows = 2 * CROWS
        ma, mb = call(
            coarse_faces_kernel,
            [(rows, LANES), (rows + BS, LANES)],
            [qi, gx, gy, ra, rc, rd, sb, *packed],
            scratch=[vmem(*FACE)],
        )
        qa, qb = swap_near(ma), swap_far(mb)
        outs = [CFIELD] + [CFACE] * 4
        arrays = [ma, qa, qb, sb, gy]
        scratch = [vmem(3 * CROWS, LANES), vmem(*TWO)]
        if wide is None:
            cc, cyb, ta, tc, td, wide = call(
                first_coarse_kernel, outs + [(12 * CROWS, LANES)], arrays, scratch=scratch
            )
        else:
            cc, cyb, ta, tc, td = call(later_coarse_kernel, outs, [*arrays, wide], scratch=scratch)
        ka = swap_near(ta)
        kc, kd = swap_regions(tc, td)
        p, ri = call(
            correct_kernel, [FULL, FULL], [*fine, p, gy, qb, cc, cyb], scratch=[vmem(*FACE)]
        )
        _, p, *sends = call(
            smooth_corrected_kernel,
            [FULL, FULL] + [FACE] * 4,
            [ri, limit, f0, fy, fzs, d, p, gx, gy, ra, rc, rd, ka, kc, kd],
            (),
            [vmem(*FULL), vmem(*FACE)],
            {0: 0},
        )

    halos = swap_faces(*sends)
    (ri,) = call(residual_kernel, [FULL], [*fine, p])
    (blocks_p,) = call(pressure_blocks_kernel, [ROW], [p])
    _, blocks_r, sa, sb = call(
        final_kernel,
        [FULL, ROW] + [(512, LANES)] * 2,
        [ri, gx, gy, *halos, blocks_p],
        aliases={0: 0},
    )

    def one(owned, blocks_p, blocks_r, sa, sb):
        return place_blocks(1, owned, blocks_p, blocks_r, *swap_blocks(sa, sb))

    def several(owned, blocks_p, blocks_r, sa, sb):
        body = functools.partial(send_blocks_kernel, count=BLK)
        sends = call(body, [(2 * BLK * 256, LANES)] * 2, [blocks_p, blocks_r])
        return place_blocks(BLK, owned, blocks_p, blocks_r, *swap_blocks(*sends))

    return lax.cond(most.reshape(()) <= 1, one, several, owned, blocks_p, blocks_r, sa, sb)


def solution(mesh):
    placed = (
        P("region", "member", None),
        P(None, "region", "member", None),
        P(("region", "member")),
        P(),
        P(),
    )
    return jax.shard_map(
        on_device,
        mesh=mesh,
        in_specs=placed,
        out_specs=(P(("region", "member"), None), P(("region", "member"), None)),
        check_vma=False,
    )
```
